32 devices in a mesh: case: 4 (over y, x), space: 8 (over z, core).
Axes of the slice: x: 2, y: 2, z: 4, core: 2. Of those that a mesh axis runs over, the one named last changes fastest.
Arguments:
- density: float32 [48, 32, 128], P('space', 'case'), may hold values from 0.3 to 1
- void_depth: int32 [48, 32], P('space', 'case'), may hold values from 0 to 32
- supports: int32 [4, 2], P('case'), may hold values from 1 to 12
- load_x: int32 [4], P('case'), may hold values from 0 to 40
- load_y: int32 [4], P('case'), may hold values from 0 to 24
- load_vectors: float32 [4, 3, 48], P('case'), may hold values from -4 to 4
Outputs:
- displacement: float32 [4, 3, 48, 32, 128], P('case', None, 'space')
- sensitivity: float32 [48, 32, 128], P('space', 'case')
The draws below stay inside these ranges and needn't reach their ends.
All inputs are finite; a program needn't handle non-finite values.
Results may differ from the reference program's by a relative error of at most 0.0003.
Values sent between devices are 32-bit elements; how exact they have to be, the bound alone decides.
No kernel may reach another device: no remote copies, remote signals or barrier semaphores. Data moves between devices by JAX's collectives and lax.ppermute only.
A program may use at most 64 MiB of HBM per device.

```python
import math
import jax
import jax.numpy as jnp
from jax import lax

NY = 32
NZ = 128
SWEEPS = 3
LOADW = 8
NX = 48
NCASE = 4


def place_ends(entries, rng, least, top_value):
    extent = entries.shape
    index_at = [jax.random.randint(jax.random.fold_in(rng, axis), (), 0, extent[axis]) for axis in range(len(extent))]
    entries = entries.at[tuple(index_at)].set(least)
    longest = extent.index(max(extent))
    index_at[longest] = (index_at[longest] + 1) % extent[longest]
    return entries.at[tuple(index_at)].set(top_value)


def block_levels(stream_key, shape, cuts, least, high):
    def one(dim, blocks):
        steps = jax.random.uniform(jax.random.fold_in(jax.random.fold_in(stream_key, 6), dim), (blocks,), jnp.float32, least / len(cuts), high / len(cuts))
        return jnp.repeat(jnp.exp(steps), shape[dim] // blocks).reshape((-1,) + (1,) * (len(shape) - dim - 1))

    loudness = one(*cuts[0])
    for cut in cuts[1:]:
        loudness = loudness * one(*cut)
    return loudness


def bell_draw(key, dims, spread, most, split=(), dtype=jnp.bfloat16):
    drawn = jax.random.normal(key, dims, jnp.float32) * spread
    if len(split) > 0:
        drawn = block_levels(key, dims, split, -0.22, 0.18) * drawn
    return jnp.clip(drawn, min=-most, max=most).astype(dtype)


def setup_inputs(seed: int = 0) -> dict:
    key_of = jax.random.split(jax.random.key(seed), 7)
    density = jnp.clip(0.3 + 0.7 * jax.random.uniform(key_of[0], (NX, NY, NZ), jnp.float32) ** block_levels(key_of[0], (NX, NY, NZ), ((0, 8), (1, 4)), -0.2, 0.2), 0.3, 1.0)
    void_depth = place_ends(jax.random.randint(key_of[1], (NX, NY), 0, NZ // 4 + 1), jax.random.fold_in(key_of[1], 1), 0, (NZ // 4 + 1) - 1).astype(jnp.int32)
    supports = place_ends(jax.random.randint(key_of[2], (NCASE, 2), 1, NX // 4 + 1), jax.random.fold_in(key_of[2], 1), 1, (NX // 4 + 1) - 1).astype(jnp.int32)
    load_x = place_ends(jax.random.randint(key_of[3], (NCASE,), 0, NX - LOADW + 1), jax.random.fold_in(key_of[3], 1), 0, NX - LOADW).astype(jnp.int32)
    load_y = place_ends(jax.random.randint(key_of[4], (NCASE,), 0, NY - LOADW + 1), jax.random.fold_in(key_of[4], 1), 0, NY - LOADW).astype(jnp.int32)
    load_vectors = bell_draw(key_of[5], (NCASE, 3, NX), 1.0, 4.0, ((0, 4),), jnp.float32)
    return dict(density=density, void_depth=void_depth, supports=supports, load_x=load_x, load_y=load_y, load_vectors=load_vectors)


EMIN = 0.001
BETA = 0.5
LOWER = 0.06
UPPER = 3.0
patch_scale = 4.0

def stencil_table():
    table = []
    for shift_x in (-1, 0, 1):
        for shift_y in (-1, 0, 1):
            for shift_z in (-1, 0, 1):
                reach = abs(shift_x) + abs(shift_y) + abs(shift_z)
                if reach > 0:
                    length = math.sqrt(reach)
                    coupling = 1.0 / 2 ** (reach - 1)
                    table.append((shift_x, shift_y, shift_z, coupling, (shift_x / length, shift_y / length, shift_z / length)))
    return table

def relaxations(count):
    middle = 0.5 * (UPPER + LOWER)
    radius = 0.5 * (UPPER - LOWER)
    return [1.0 / (middle + radius * math.cos(math.pi * (2 * index + 1) / (2 * count))) for index in range(count)]

def pad_sides(array):
    widths = [(0, 0)] * (array.ndim - 2) + [(1, 1), (1, 1)]
    return jnp.pad(array, widths)

def neighbour(padded, shift_x, shift_y, shift_z, thick, rows, depth):
    return padded[..., 1 + shift_x:1 + shift_x + thick, 1 + shift_y:1 + shift_y + rows, 1 + shift_z:1 + shift_z + depth]

def diagonal(root):
    padded = pad_sides(root)
    thick = root.shape[0] - 2
    rows = root.shape[1]
    depth = root.shape[2]
    centre = neighbour(padded, 0, 0, 0, thick, rows, depth)
    totals = [jnp.zeros((thick, rows, depth), jnp.float32) for axis_k in range(3)]
    for shift_x, shift_y, shift_z, coupling, normal in stencil_table():
        bond = coupling * centre * neighbour(padded, shift_x, shift_y, shift_z, thick, rows, depth)
        totals = [totals[axis_k] + bond * (1.0 + BETA * normal[axis_k] * normal[axis_k]) for axis_k in range(3)]
    return jnp.stack(totals)

def bond_terms(field, root, energy):
    parts_pad = [pad_sides(field[axis_k]) for axis_k in range(3)]
    root_pad = pad_sides(root)
    thick = field.shape[1] - 2
    rows = field.shape[2]
    depth = field.shape[3]
    centre_parts = [neighbour(parts_pad[axis_k], 0, 0, 0, thick, rows, depth) for axis_k in range(3)]
    centre_root = neighbour(root_pad, 0, 0, 0, thick, rows, depth)
    total = jnp.zeros((thick, rows, depth), jnp.float32)
    totals = [jnp.zeros((thick, rows, depth), jnp.float32) for axis_k in range(3)]
    for shift_x, shift_y, shift_z, coupling, normal in stencil_table():
        bond = coupling * centre_root * neighbour(root_pad, shift_x, shift_y, shift_z, thick, rows, depth)
        differ = [centre_parts[axis_k] - neighbour(parts_pad[axis_k], shift_x, shift_y, shift_z, thick, rows, depth) for axis_k in range(3)]
        along = None
        for axis_k in range(3):
            if normal[axis_k] != 0.0:
                term = normal[axis_k] * differ[axis_k]
                along = term if along is None else along + term
        forces = []
        for axis_k in range(3):
            if normal[axis_k] != 0.0:
                forces.append(differ[axis_k] + BETA * normal[axis_k] * along)
            else:
                forces.append(differ[axis_k])
        if energy:
            total = total + bond * (differ[0] * forces[0] + differ[1] * forces[1] + differ[2] * forces[2])
        else:
            totals = [totals[axis_k] + bond * forces[axis_k] for axis_k in range(3)]
    if energy:
        return total
    return jnp.stack(totals)

def relax(field, root, diag, force, free, omega):
    product = bond_terms(field, root, False)
    return field[:, 1:-1] + omega * free * (force - product) / diag

def reference(density, void_depth, supports, load_x, load_y, load_vectors):
    shape = (NX, NY, NZ)
    heights = lax.broadcasted_iota(jnp.int32, shape, 2)
    places_x = lax.broadcasted_iota(jnp.int32, shape, 0)
    places_y = lax.broadcasted_iota(jnp.int32, shape, 1)
    offset = heights - NZ // 2
    hollow = (offset >= 0) & (offset < void_depth[:, :, None])
    solid = density * (1.0 - hollow.astype(jnp.float32))
    cubed = solid * solid * solid
    stiff = EMIN + (1.0 - EMIN) * cubed
    root = jnp.pad(jnp.sqrt(stiff), ((1, 1), (0, 0), (0, 0)))
    diag = diagonal(root)
    omegas = relaxations(SWEEPS)

    def one_case(inputs):
        support, corner_x, corner_y, vector = inputs
        pinned = (heights == 0) & ((places_x < support[0]) | (places_x >= NX - support[1]))
        free = 1.0 - pinned.astype(jnp.float32)
        patch = (heights == NZ - 1) & (places_x >= corner_x) & (places_x < corner_x + LOADW) & (places_y >= corner_y) & (places_y < corner_y + LOADW)
        force = (free * (solid + patch_scale * patch.astype(jnp.float32)))[None] * vector[:, :, None, None]
        field = omegas[0] * free * force / diag
        for index in range(1, SWEEPS):
            padded = jnp.pad(field, ((0, 0), (1, 1), (0, 0), (0, 0)))
            field = relax(padded, root, diag, force, free, omegas[index])
        padded = jnp.pad(field, ((0, 0), (1, 1), (0, 0), (0, 0)))
        return (field, bond_terms(padded, root, True))
    fields, energies = lax.map(one_case, (supports, load_x, load_y, load_vectors))
    total = lax.optimization_barrier(jnp.sum(energies, axis=0))
    factor = -1.5 * (1.0 - EMIN) * solid * solid / stiff
    return (fields, factor * total / NCASE)
```

```python
import math

import jax
import jax.numpy as jnp
from jax import lax
from jax.sharding import PartitionSpec as P

SWEEPS = 3
LOADW = 8


EMIN = 0.001
BETA = 0.5
LOWER = 0.06
UPPER = 3.0
patch_scale = 4.0


def extended(shard, sides, width):
    for axis, dim in sides:
        devices, length = (lax.axis_size(axis), shard.shape[dim])
        up = [(i, (i + 1) % devices) for i in range(devices - 1)]
        down = [(j, i) for i, j in up]
        last = lax.slice_in_dim(shard, length - width, length, axis=dim)
        first = lax.slice_in_dim(shard, 0, width, axis=dim)
        before = lax.ppermute(last, axis, up)
        after = lax.ppermute(first, axis, down)
        shard = jnp.concatenate([before, shard, after], axis=dim)
    return shard


def stencil_table():
    table = []
    for shift_x in (-1, 0, 1):
        for shift_y in (-1, 0, 1):
            for shift_z in (-1, 0, 1):
                reach = abs(shift_x) + abs(shift_y) + abs(shift_z)
                if reach > 0:
                    length = math.sqrt(reach)
                    coupling = 1.0 / 2 ** (reach - 1)
                    table.append(
                        (
                            shift_x,
                            shift_y,
                            shift_z,
                            coupling,
                            (shift_x / length, shift_y / length, shift_z / length),
                        )
                    )
    return table


def relaxations(count):
    middle = 0.5 * (UPPER + LOWER)
    radius = 0.5 * (UPPER - LOWER)
    return [
        1.0 / (middle + radius * math.cos(math.pi * (2 * index + 1) / (2 * count)))
        for index in range(count)
    ]


def pad_sides(array):
    widths = [(0, 0)] * (array.ndim - 2) + [(1, 1), (1, 1)]
    return jnp.pad(array, widths)


def neighbour(padded, shift_x, shift_y, shift_z, thick, rows, depth):
    return padded[
        ...,
        1 + shift_x : 1 + shift_x + thick,
        1 + shift_y : 1 + shift_y + rows,
        1 + shift_z : 1 + shift_z + depth,
    ]


def diagonal(root):
    padded = pad_sides(root)
    thick = root.shape[0] - 2
    rows = root.shape[1]
    depth = root.shape[2]
    centre = neighbour(padded, 0, 0, 0, thick, rows, depth)
    totals = [jnp.zeros((thick, rows, depth), jnp.float32) for axis_k in range(3)]
    for shift_x, shift_y, shift_z, coupling, normal in stencil_table():
        bond = coupling * centre * neighbour(padded, shift_x, shift_y, shift_z, thick, rows, depth)
        totals = [
            totals[axis_k] + bond * (1.0 + BETA * normal[axis_k] * normal[axis_k])
            for axis_k in range(3)
        ]
    return jnp.stack(totals)


def bond_terms(field, root, energy):
    parts_pad = [pad_sides(field[axis_k]) for axis_k in range(3)]
    root_pad = pad_sides(root)
    thick = field.shape[1] - 2
    rows = field.shape[2]
    depth = field.shape[3]
    centre_parts = [
        neighbour(parts_pad[axis_k], 0, 0, 0, thick, rows, depth) for axis_k in range(3)
    ]
    centre_root = neighbour(root_pad, 0, 0, 0, thick, rows, depth)
    total = jnp.zeros((thick, rows, depth), jnp.float32)
    totals = [jnp.zeros((thick, rows, depth), jnp.float32) for axis_k in range(3)]
    for shift_x, shift_y, shift_z, coupling, normal in stencil_table():
        bond = (
            coupling
            * centre_root
            * neighbour(root_pad, shift_x, shift_y, shift_z, thick, rows, depth)
        )
        differ = [
            centre_parts[axis_k]
            - neighbour(parts_pad[axis_k], shift_x, shift_y, shift_z, thick, rows, depth)
            for axis_k in range(3)
        ]
        along = None
        for axis_k in range(3):
            if normal[axis_k] != 0.0:
                term = normal[axis_k] * differ[axis_k]
                along = term if along is None else along + term
        forces = []
        for axis_k in range(3):
            if normal[axis_k] != 0.0:
                forces.append(differ[axis_k] + BETA * normal[axis_k] * along)
            else:
                forces.append(differ[axis_k])
        if energy:
            total = total + bond * (
                differ[0] * forces[0] + differ[1] * forces[1] + differ[2] * forces[2]
            )
        else:
            totals = [totals[axis_k] + bond * forces[axis_k] for axis_k in range(3)]
    if energy:
        return total
    return jnp.stack(totals)


def relax(field, root, diag, force, free, omega):
    product = bond_terms(field, root, False)
    return field[:, 1:-1] + omega * free * (force - product) / diag


def trim(array, have, want, axis_n):
    cut = have - want
    if cut == 0:
        return array
    return lax.slice_in_dim(array, cut, array.shape[axis_n] - cut, axis=axis_n)


def shards(density, void_depth, supports, load_x, load_y, load_vectors):
    cells_x, band, depth = density.shape
    groups = lax.axis_size("case")
    slabs = lax.axis_size("space")
    rows = band * groups
    total_x = cells_x * slabs
    heights = lax.broadcasted_iota(jnp.int32, density.shape, 2)
    offset = heights - depth // 2
    hollow = (offset >= 0) & (offset < void_depth[:, :, None])
    solid = density * (1.0 - hollow.astype(jnp.float32))
    margin = SWEEPS + 1
    brick = extended(solid, (("space", 0),), margin)
    widened = lax.all_gather(brick, "case", axis=1, tiled=True)
    places = (
        lax.axis_index("space") * cells_x
        - margin
        + lax.broadcasted_iota(jnp.int32, (cells_x + 2 * margin, 1, 1), 0)
    )
    inside = (places >= 0) & (places < total_x)
    cubed_wide = widened * widened * widened
    root = jnp.where(inside, jnp.sqrt(EMIN + (1.0 - EMIN) * cubed_wide), 0.0)
    base = margin - 1
    inner = places[1:-1]
    inner_inside = ((inner >= 0) & (inner < total_x)).astype(jnp.float32)
    diag = diagonal(root)
    diag_safe = diag + (1.0 - inner_inside)
    inner_shape = (cells_x + 2 * base, rows, depth)
    heights_ext = lax.broadcasted_iota(jnp.int32, inner_shape, 2)
    lateral = lax.broadcasted_iota(jnp.int32, inner_shape, 1)
    support = supports[0]
    pinned = (heights_ext == 0) & ((inner < support[0]) | (inner >= total_x - support[1]))
    free = inner_inside * (1.0 - pinned.astype(jnp.float32))
    corner_x = load_x[0]
    corner_y = load_y[0]
    patch = (
        (heights_ext == depth - 1)
        & (inner >= corner_x)
        & (inner < corner_x + LOADW)
        & (lateral >= corner_y)
        & (lateral < corner_y + LOADW)
    )
    solid_inner = widened[1:-1]
    profile = load_vectors[0]
    first_plane = lax.axis_index("space") * cells_x
    profile = jnp.pad(profile, ((0, 0), (base, base)))
    planes = lax.dynamic_slice_in_dim(profile, first_plane, cells_x + 2 * base, 1)
    force = (free * (solid_inner + patch_scale * patch.astype(jnp.float32)))[None] * planes[
        :, :, None, None
    ]
    omegas = relaxations(SWEEPS)
    field = omegas[0] * free * force / diag_safe
    extent = base
    for index in range(1, SWEEPS):
        target = extent - 1
        field = relax(
            field,
            trim(root, margin, extent, 0),
            trim(diag_safe, base, target, 1),
            trim(force, base, target, 1),
            trim(free, base, target, 0),
            omegas[index],
        )
        extent = target
    energy = bond_terms(trim(field, extent, 1, 1), trim(root, margin, 1, 0), True)
    pieces = energy.reshape(cells_x, groups, band, depth).transpose(1, 0, 2, 3)
    swapped = lax.all_to_all(pieces, "case", split_axis=0, concat_axis=0, tiled=True)
    share = jnp.sum(swapped, axis=0)
    cubed = solid * solid * solid
    stiff = EMIN + (1.0 - EMIN) * cubed
    factor = -1.5 * (1.0 - EMIN) * solid * solid / stiff
    return (trim(field, extent, 0, 1)[None], factor * share / groups)


def solution(mesh):
    return jax.shard_map(
        shards,
        mesh=mesh,
        in_specs=(
            P("space", "case", None),
            P("space", "case"),
            P("case", None),
            P("case"),
            P("case"),
            P("case", None, None),
        ),
        out_specs=(P("case", None, "space", None, None), P("space", "case", None)),
        check_vma=False,
    )
```

```python
import math

import jax
import jax.numpy as jnp
from jax import lax
from jax.experimental import pallas as pl
from jax.experimental.pallas import tpu as pltpu
from jax.sharding import PartitionSpec as P

SWEEPS = 3
LOADW = 8
EMIN = 0.001
LOWER = 0.06
UPPER = 3.0
PATCH = 4.0
SUB = 8
HALO = SWEEPS + 1

AXIAL = 1.5
SIDE = 1.0
PAIR = 0.625
FLAT = 0.5
FULL = 0.25 * (1.0 + 0.5 / 3.0)
CROSS2 = 0.125
CROSS3 = 0.125 / 3.0


def relaxations(count):
    middle = 0.5 * (UPPER + LOWER)
    radius = 0.5 * (UPPER - LOWER)
    return [
        1.0 / (middle + radius * math.cos(math.pi * (2 * index + 1) / (2 * count)))
        for index in range(count)
    ]


def relax_kernel(
    own_ref,
    low_ref,
    high_ref,
    supports_ref,
    load_x_ref,
    load_y_ref,
    vectors_ref,
    field_ref,
    energy_ref,
    natural,
    root_s,
    solid_s,
    inv_root_s,
    push_s,
    inverse_s,
    shear_s,
    main_s,
    first_s,
    second_s,
    bonds,
):
    groups, cells, band, depth = own_ref.shape
    rows = groups * band
    fold = rows // SUB
    total_x = vectors_ref.shape[2]
    first_plane = lax.axis_index("space") * cells
    wide = cells + 2 * HALO
    omegas = relaxations(SWEEPS)

    for g in range(groups):
        lines = slice(g * band, (g + 1) * band)
        natural[0:HALO, lines, :] = low_ref[g]
        natural[HALO : HALO + cells, lines, :] = own_ref[g]
        natural[HALO + cells : wide, lines, :] = high_ref[g]

    tile = (1, SUB, depth)
    lane = lax.broadcasted_iota(jnp.int32, tile, 2)
    line = lax.broadcasted_iota(jnp.int32, tile, 1)
    not_first_z = (lane > 0).astype(jnp.float32)
    not_last_z = (lane < depth - 1).astype(jnp.float32)
    not_first_s = (line > 0).astype(jnp.float32)
    not_last_s = (line < SUB - 1).astype(jnp.float32)
    at_bottom = (lane == 0).astype(jnp.float32)

    def along_z(a):
        after = pltpu.roll(a, depth - 1, 2) * not_last_z
        before = pltpu.roll(a, 1, 2) * not_first_z
        return after, before

    def along_y(a):
        after = pltpu.roll(a[0:1], SUB - 1, 1) * not_last_s
        before = pltpu.roll(a[fold - 1 : fold], 1, 1) * not_first_s
        return (
            jnp.concatenate([a[1:], after], axis=0),
            jnp.concatenate([before, a[:-1]], axis=0),
        )

    def both(pair):
        return pair[0] + pair[1], pair[0] - pair[1]

    def plus(pair):
        return pair[0] + pair[1]

    def minus(pair):
        return pair[0] - pair[1]

    def place_of(plane, margin):
        place = first_plane - margin + plane
        inside = jnp.logical_and(place >= 0, place < total_x)
        return place, inside

    for i in range(wide):
        place, inside = place_of(i, HALO)
        solid = jnp.stack([natural[i, pl.ds(t, SUB, stride=fold), :] for t in range(fold)])
        stiff = EMIN + (1.0 - EMIN) * (solid * solid * solid)
        inverse = lax.rsqrt(stiff)
        root_s[i] = stiff * inverse * inside.astype(jnp.float32)
        if 0 < i < wide - 1:
            solid_s[i - 1] = solid
            inv_root_s[i - 1] = inverse

    load_y = load_y_ref[0]
    load_x = load_x_ref[0]
    y_of = fold * lax.broadcasted_iota(jnp.int32, (fold, SUB, depth), 1) + lax.broadcasted_iota(
        jnp.int32, (fold, SUB, depth), 0
    )
    z_of = lax.broadcasted_iota(jnp.int32, (fold, SUB, depth), 2)
    patch = jnp.where(
        (z_of == depth - 1) & (y_of >= load_y) & (y_of < load_y + LOADW), PATCH, 0.0
    )

    def tensor_parts(r):
        zs, zd = both(along_z(r))
        ys, yd = both(along_y(r))
        yszs, ydzs = both(along_y(zs))
        yszd, ydzd = both(along_y(zd))
        cross = ys + zs
        corner = PAIR * yszs
        here = [
            cross + FLAT * yszs,
            cross + 0.5 * ys + corner,
            cross + 0.5 * zs + corner,
            CROSS2 * ydzd,
        ]
        base = FULL * yszs + 0.5 * cross + r
        even = [
            base + 0.5 * r + 0.125 * cross,
            base + 0.125 * ys,
            base + 0.125 * zs,
            CROSS3 * ydzd,
        ]
        odd = [CROSS2 * yd + CROSS3 * ydzs, CROSS2 * zd + CROSS3 * yszd]
        return here, even, odd

    older = None
    newer = None
    for i in range(wide):
        latest = tensor_parts(root_s[i])
        if i >= 2:
            j = i - 2
            place, inside = place_of(j, HALO - 1)
            keep = inside.astype(jnp.float32)
            tensor = [newer[0][k] + (latest[1][k] + older[1][k]) for k in range(4)]
            shear_s[0, j] = latest[2][0] - older[2][0]
            shear_s[1, j] = latest[2][1] - older[2][1]
            shear_s[2, j] = tensor[3]
            pinned = jnp.logical_or(
                place < supports_ref[0, 0], place >= total_x - supports_ref[0, 1]
            )
            free = keep - (keep * pinned.astype(jnp.float32)) * at_bottom
            loaded = jnp.logical_and(place >= load_x, place < load_x + LOADW).astype(jnp.float32)
            push = (solid_s[j] + loaded * patch) * inv_root_s[j]
            where = jnp.clip(place, 0, total_x - 1)
            for k in range(3):
                if HALO - 1 <= j < HALO - 1 + cells:
                    main_s[k, j - (HALO - 1)] = tensor[k]
                inverse = free / (tensor[k] + (1.0 - keep))
                inverse_s[k, j] = inverse
                push_s[k, j] = push * inverse * vectors_ref[0, k, where]
        older, newer = newer, latest

    def field_parts(w):
        pair = [both(along_z(w[k])) for k in range(3)]
        zs = [pair[k][0] for k in range(3)]
        zd = [pair[k][1] for k in range(3)]
        ysx, ydx = both(along_y(w[0]))
        ysy, ydy = both(along_y(w[1]))
        ysz = plus(along_y(w[2]))
        yszsx, ydzsx = both(along_y(zs[0]))
        yszsy, ydzsy = both(along_y(zs[1]))
        yszsz = plus(along_y(zs[2]))
        yszdx = plus(along_y(zd[0]))
        ydzdy = minus(along_y(zd[1]))
        yszdz, ydzdz = both(along_y(zd[2]))
        here = [
            ysx + FLAT * yszsx + zs[0],
            AXIAL * ysy + PAIR * yszsy + zs[1] + CROSS2 * ydzdz,
            ysz + PAIR * yszsz + AXIAL * zs[2] + CROSS2 * ydzdy,
        ]
        even = [
            AXIAL * w[0] + PAIR * (zs[0] + ysx) + FULL * yszsx,
            w[1] + FLAT * zs[1] + PAIR * ysy + FULL * yszsy + CROSS3 * ydzdz,
            w[2] + PAIR * zs[2] + FLAT * ysz + FULL * yszsz + CROSS3 * ydzdy,
        ]
        odd = [
            CROSS2 * (ydy + zd[2]) + CROSS3 * (ydzsy + yszdz),
            CROSS2 * ydx + CROSS3 * ydzsx,
            CROSS2 * zd[0] + CROSS3 * yszdx,
        ]
        ahead = [even[k] + odd[k] for k in range(3)]
        behind = [even[k] - odd[k] for k in range(3)]
        return here, ahead, behind

    def sweep(count, load, offset, omega, store):
        partial = None
        trail = None
        for i in range(count):
            r = root_s[i + offset]
            here, ahead, behind = field_parts([r * load(k, i) for k in range(3)])
            if i >= 2:
                j = i - 1
                d = j + offset - 1
                old = [load(k, j) for k in range(3)]
                shear = [shear_s[k, d] for k in range(3)]
                rest = [
                    shear[0] * old[1] + shear[1] * old[2],
                    shear[0] * old[0] + shear[2] * old[2],
                    shear[1] * old[0] + shear[2] * old[1],
                ]
                for k in range(3):
                    pull = (partial[k] + ahead[k] - rest[k]) * inverse_s[k, d]
                    store(k, j - 1, (1.0 - omega) * old[k] + omega * (push_s[k, d] + pull))
            if i >= 1:
                partial = [here[k] + trail[k] for k in range(3)]
            trail = behind

    def store_second(k, i, value):
        first_s[k, i] = value

    def store_third(k, i, value):
        second_s[k, i] = value
        if 1 <= i <= cells:
            for t in range(fold):
                field_ref[k, i - 1, pl.ds(t, SUB, stride=fold), :] = value[t]

    sweep(wide - 2, lambda k, i: omegas[0] * push_s[k, i], 1, omegas[1], store_second)
    sweep(wide - 4, lambda k, i: first_s[k, i], 2, omegas[2], store_third)

    def square_parts(w, v):
        qxx, qyy, qzz = w[0] * v[0], w[1] * v[1], w[2] * v[2]
        qxy, qxz, qyz = w[0] * v[1], w[0] * v[2], w[1] * v[2]
        s = qxx + qyy + qzz
        zs_s = plus(along_z(s))
        zs_x = plus(along_z(qxx))
        zs_z = plus(along_z(qzz))
        zs_xy = plus(along_z(qxy))
        zd_yz = minus(along_z(qyz))
        zd_xz = minus(along_z(qxz))
        twist = minus(along_y(zd_yz))
        half = 0.5 * zs_s + 0.125 * zs_z
        here = (
            zs_s
            + 0.5 * zs_z
            + plus(along_y(s + 0.5 * qyy + (PAIR * zs_s - 0.125 * zs_x)))
            + 0.25 * twist
        )
        even = (
            s
            + 0.5 * qxx
            + half
            + 0.125 * zs_x
            + plus(along_y(0.5 * s + 0.125 * (qxx + qyy) + FULL * zs_s))
            + (1.0 / 12.0) * twist
        )
        odd = (
            minus(along_y(0.25 * qxy + (1.0 / 12.0) * zs_xy))
            + 0.25 * zd_xz
            + plus(along_y((1.0 / 12.0) * zd_xz))
        )
        return here, even + odd, even - odd

    partial = None
    trail = None
    squares = None
    squares_trail = None
    for i in range(cells + 2):
        r = root_s[i + HALO - 1]
        v = [second_s[k, i] for k in range(3)]
        w = [r * v[k] for k in range(3)]
        here, ahead, behind = field_parts(w)
        sq_here, sq_ahead, sq_behind = square_parts(w, v)
        if i >= 2:
            j = i - 1
            old = [second_s[k, j] for k in range(3)]
            shear = [shear_s[k, j + HALO - 2] for k in range(3)]
            main = [main_s[k, j - 1] for k in range(3)]
            gather = squares + sq_ahead
            rest = [
                shear[0] * old[1] + shear[1] * old[2],
                shear[2] * old[2] + shear[0] * old[0],
                shear[1] * old[0] + shear[2] * old[1],
            ]
            for k in range(3):
                gather = gather + old[k] * (
                    main[k] * old[k] + rest[k] - 2.0 * (partial[k] + ahead[k])
                )
            gather = gather * root_s[j + HALO - 1]
            for t in range(fold):
                bonds[j - 1, pl.ds(t, SUB, stride=fold), :] = gather[t]
        if i >= 1:
            partial = [here[k] + trail[k] for k in range(3)]
            squares = sq_here + squares_trail
        trail = behind
        squares_trail = sq_behind
    for g in range(groups):
        energy_ref[g] = bonds[:, g * band : (g + 1) * band, :]


def relaxed(own, low, high, supports, load_x, load_y, load_vectors):
    groups, cells, band, depth = own.shape
    rows = groups * band
    fold = rows // SUB
    wide = cells + 2 * HALO
    vmem = pl.BlockSpec(memory_space=pltpu.VMEM)
    smem = pl.BlockSpec(memory_space=pltpu.SMEM)

    def planes(*lead):
        return pltpu.VMEM((*lead, fold, SUB, depth), jnp.float32)

    return pl.pallas_call(
        relax_kernel,
        out_shape=(
            jax.ShapeDtypeStruct((3, cells, rows, depth), jnp.float32),
            jax.ShapeDtypeStruct((groups, cells, band, depth), jnp.float32),
        ),
        in_specs=[vmem] * 3 + [smem] * 4,
        out_specs=(vmem, vmem),
        scratch_shapes=[
            pltpu.VMEM((wide, rows, depth), jnp.float32),
            planes(wide),
            planes(wide - 2),
            planes(wide - 2),
            planes(3, wide - 2),
            planes(3, wide - 2),
            planes(3, wide - 2),
            planes(3, cells),
            planes(3, wide - 4),
            planes(3, wide - 6),
            pltpu.VMEM((cells, rows, depth), jnp.float32),
        ],
        compiler_params=pltpu.CompilerParams(vmem_limit_bytes=32 * 1024 * 1024),
    )(own, low, high, supports, load_x, load_y, load_vectors)


def shards(density, void_depth, supports, load_x, load_y, load_vectors):
    cells, band, depth = density.shape
    groups = lax.axis_size("case")
    slabs = lax.axis_size("space")
    heights = lax.broadcasted_iota(jnp.int32, density.shape, 2)
    offset = heights - depth // 2
    hollow = (offset >= 0) & (offset < void_depth[:, :, None])
    solid = density * (1.0 - hollow.astype(jnp.float32))
    copies = jnp.broadcast_to(solid[None], (groups, cells, band, depth))
    own = lax.all_to_all(copies, "case", split_axis=0, concat_axis=0, tiled=True)
    up = [(i, i + 1) for i in range(slabs - 1)]
    down = [(j, i) for i, j in up]
    low = lax.ppermute(own[:, cells - HALO :], "space", up)
    high = lax.ppermute(own[:, :HALO], "space", down)
    field, energy = relaxed(own, low, high, supports, load_x, load_y, load_vectors)
    swapped = lax.all_to_all(energy, "case", split_axis=0, concat_axis=0, tiled=True)
    share = jnp.sum(swapped, axis=0)
    stiff = EMIN + (1.0 - EMIN) * (solid * solid * solid)
    factor = -1.5 * (1.0 - EMIN) * solid * solid / stiff
    return (field[None], factor * share / groups)


def solution(mesh):
    return jax.shard_map(
        shards,
        mesh=mesh,
        in_specs=(
            P("space", "case", None),
            P("space", "case"),
            P("case", None),
            P("case"),
            P("case"),
            P("case", None, None),
        ),
        out_specs=(P("case", None, "space", None, None), P("space", "case", None)),
        check_vma=False,
    )
```

```python
import math

import jax
import jax.numpy as jnp
from jax import lax
from jax.experimental import pallas as pl
from jax.experimental.pallas import tpu as pltpu
from jax.sharding import Mesh
from jax.sharding import PartitionSpec as P

SWEEPS = 3
LOADW = 8
EMIN = 0.001
LOWER = 0.06
UPPER = 3.0
PATCH = 4.0
SUB = 8
CORES = 2
HALO = SWEEPS + 1
EDGE = HALO - 1
PAD = 8

AXIAL = 1.5
PAIR = 0.625
FLAT = 0.5
FULL = 0.25 * (1.0 + 0.5 / 3.0)
CROSS2 = 0.125
CROSS3 = 0.125 / 3.0


def relaxations(count):
    middle = 0.5 * (UPPER + LOWER)
    radius = 0.5 * (UPPER - LOWER)
    return [
        1.0 / (middle + radius * math.cos(math.pi * (2 * index + 1) / (2 * count)))
        for index in range(count)
    ]


def both(pair):
    return pair[0] + pair[1], pair[0] - pair[1]


def plus(pair):
    return pair[0] + pair[1]


def minus(pair):
    return pair[0] - pair[1]


def span_of(cells):
    return CORES * cells + 2 * EDGE


def pack_kernel(
    density_ref, void_ref, supports_ref, load_x_ref, load_y_ref, vectors_ref, packed_ref
):
    copies, planes, band, depth = packed_ref.shape
    cells = planes - 1
    total_x = vectors_ref.shape[2]
    span = span_of(cells)
    first = lax.axis_index("column") * (CORES * cells) - EDGE
    z_of = lax.broadcasted_iota(jnp.int32, (band, depth), 1)
    level = z_of - depth // 2
    eye = lax.broadcasted_iota(jnp.int32, (band, band), 0) == lax.broadcasted_iota(
        jnp.int32, (band, band), 1
    )
    for i in range(cells):
        line = jnp.broadcast_to(void_ref[i : i + 1, :], (band, band)).astype(jnp.float32)
        column = jnp.sum(jnp.where(eye, line, 0.0), axis=1, keepdims=True)
        top = jnp.broadcast_to(column, (band, depth)).astype(jnp.int32)
        hollow = (level >= 0) & (level < top)
        solid = jnp.where(hollow, 0.0, density_ref[i])
        for copy in range(copies):
            packed_ref[copy, i] = solid
    lane = lax.broadcasted_iota(jnp.int32, (1, depth), 1)
    row = jnp.where(lane == 5 * span, load_y_ref[0].astype(jnp.float32), 0.0)
    for m in range(span):
        place = first + m
        inside = jnp.logical_and(place >= 0, place < total_x)
        where = jnp.clip(place, 0, total_x - 1)
        for k in range(3):
            value = jnp.where(inside, vectors_ref[0, k, where], 0.0)
            row = jnp.where(lane == k * span + m, value, row)
    place = first + lane - 3 * span
    pinned = (place < supports_ref[0, 0]) | (place >= total_x - supports_ref[0, 1])
    row = jnp.where((lane >= 3 * span) & (lane < 4 * span) & pinned, 1.0, row)
    place = first + lane - 4 * span
    loaded = (place >= load_x_ref[0]) & (place < load_x_ref[0] + LOADW)
    row = jnp.where((lane >= 4 * span) & (lane < 5 * span) & loaded, 1.0, row)
    for copy in range(copies):
        packed_ref[copy, cells] = jnp.broadcast_to(row, (band, depth))


def relax_kernel(
    chip_ref,
    halo_ref,
    field_ref,
    sensitivity_ref,
    natural,
    third_n,
    result_n,
    root_a,
    drive_a,
    push_a,
    inverse_a,
    shear_a,
    first_a,
    root_b,
    drive_b,
    push_b,
    inverse_b,
    shear_b,
    first_b,
    main_b,
    factor_b,
    second_b,
    squares_b,
    work_b,
):
    groups, cores, planes, band, depth = chip_ref.shape
    cells = planes - 1
    span = span_of(cells)
    rows = groups * band
    wide = cells + 2 * HALO
    core = lax.axis_index("core")
    case = lax.axis_index("case")
    chips = lax.axis_size("column")
    total_x = chips * CORES * cells
    first_plane = (lax.axis_index("column") * CORES + core) * cells
    shift = core * cells
    omegas = relaxations(SWEEPS)

    blank = jnp.zeros((PAD, depth), jnp.float32)
    tail = natural.shape[1] - PAD - rows
    for i in range(natural.shape[0]):
        natural[i, 0:PAD, :] = blank
        for at in range(PAD + rows, natural.shape[1], PAD):
            natural[i, at : at + PAD, :] = blank
    for k in range(3):
        for i in range(cells + 2):
            third_n[k, i, 0:PAD, :] = blank
            for at in range(PAD + rows, natural.shape[1], PAD):
                third_n[k, i, at : at + PAD, :] = blank
    for g in range(groups):
        lines = slice(PAD + g * band, PAD + (g + 1) * band)
        natural[0:HALO, lines, :] = halo_ref[g]
        for c in range(CORES):
            at = HALO + c * cells
            natural[at : at + cells, lines, :] = chip_ref[g, c, 0:cells]
        at = HALO + CORES * cells
        natural[at : at + HALO, lines, :] = halo_ref[g]

    tile = (1, SUB, depth)
    lane = lax.broadcasted_iota(jnp.int32, tile, 2)
    line = lax.broadcasted_iota(jnp.int32, tile, 1)
    not_first_z = (lane > 0).astype(jnp.float32)
    not_last_z = (lane < depth - 1).astype(jnp.float32)
    not_first_s = (line > 0).astype(jnp.float32)
    not_last_s = (line < SUB - 1).astype(jnp.float32)
    at_bottom = (lane == 0).astype(jnp.float32)

    def along_z(a):
        after = pltpu.roll(a, depth - 1, 2) * not_last_z
        before = pltpu.roll(a, 1, 2) * not_first_z
        return after, before

    def along_y(a, closed):
        fold = a.shape[0]
        after = pltpu.roll(a[0:1], SUB - 1, 1)
        before = pltpu.roll(a[fold - 1 : fold], 1, 1)
        if closed:
            after = after * not_last_s
            before = before * not_first_s
        return (
            jnp.concatenate([a[1:], after], axis=0),
            jnp.concatenate([before, a[:-1]], axis=0),
        )

    def inside_of(plane, margin):
        place = first_plane - margin + plane
        return jnp.logical_and(place >= 0, place < total_x).astype(jnp.float32)

    def lines_of(fold):
        shape = (fold, SUB, depth)
        return fold * lax.broadcasted_iota(jnp.int32, shape, 1) + lax.broadcasted_iota(
            jnp.int32, shape, 0
        )

    def case_values(which):
        plain = jnp.broadcast_to(chip_ref[which, 0, cells, 0:1, :], (SUB, depth))
        moved = pltpu.roll(plain, jnp.where(core == 0, 0, depth - cells), 1)

        def value(kind, j):
            at = kind * span + j
            return jnp.broadcast_to(moved[:, at : at + 1], (SUB, depth))[None]

        corner = jnp.broadcast_to(plain[:, 5 * span : 5 * span + 1], (SUB, depth))[None]
        return value, corner

    def patch_of(y_of, corner):
        y = y_of.astype(jnp.float32)
        high = lax.broadcasted_iota(jnp.int32, y_of.shape, 2) == depth - 1
        return jnp.where(high & (y >= corner) & (y < corner + LOADW), PATCH, 0.0)

    def stiffness(fold, start, keep_rows, root_s, drive_s, inv_s, factor_s):
        for i in range(wide):
            solid = jnp.stack(
                [natural[shift + i, pl.ds(start + t, SUB, stride=fold), :] for t in range(fold)]
            )
            stiff = EMIN + (1.0 - EMIN) * (solid * solid * solid)
            inv_root = lax.rsqrt(stiff)
            root = stiff * inv_root * inside_of(i, HALO)
            root_s[i] = root if keep_rows is None else root * keep_rows
            if 0 < i < wide - 1:
                drive_s[i - 1] = solid * inv_root
                inv_s[i - 1] = inv_root
            if factor_s is not None and HALO <= i < HALO + cells:
                ratio = solid * inv_root
                factor_s[i - HALO] = ((-1.5 * (1.0 - EMIN)) / groups) * (ratio * ratio)

    def tensor_parts(r, closed):
        zs, zd = both(along_z(r))
        ys, yd = both(along_y(r, closed))
        yszs, ydzs = both(along_y(zs, closed))
        yszd, ydzd = both(along_y(zd, closed))
        cross = ys + zs
        corner = PAIR * yszs
        here = [
            cross + FLAT * yszs,
            cross + 0.5 * ys + corner,
            cross + 0.5 * zs + corner,
            CROSS2 * ydzd,
        ]
        base = FULL * yszs + 0.5 * cross + r
        even = [
            base + 0.5 * r + 0.125 * cross,
            base + 0.125 * ys,
            base + 0.125 * zs,
            CROSS3 * ydzd,
        ]
        odd = [CROSS2 * yd + CROSS3 * ydzs, CROSS2 * zd + CROSS3 * yszd]
        return here, even, odd

    def tensor(closed, keep_rows, root_s, shear_s, inverse_s, main_s):
        older = None
        newer = None
        for i in range(wide):
            latest = tensor_parts(root_s[i], closed)
            if i >= 2:
                j = i - 2
                keep = inside_of(j, EDGE)
                if keep_rows is not None:
                    keep = keep * keep_rows
                total = [newer[0][k] + (latest[1][k] + older[1][k]) for k in range(4)]
                shear_s[0, j] = latest[2][0] - older[2][0]
                shear_s[1, j] = latest[2][1] - older[2][1]
                shear_s[2, j] = total[3]
                for k in range(3):
                    if main_s is not None and EDGE <= j < EDGE + cells:
                        main_s[k, j - EDGE] = total[k]
                    inverse_s[k, j] = keep / (total[k] + (1.0 - keep))
            older, newer = newer, latest

    def pushes(which, y_of, drive_s, inv_s, inverse_s, push_s):
        value, corner = case_values(which)
        patch = patch_of(y_of, corner)
        for j in range(wide - 2):
            free = 1.0 - value(3, j) * at_bottom
            push = (drive_s[j] + (value(4, j) * patch) * inv_s[j]) * free
            for k in range(3):
                push_s[k, j] = push * inverse_s[k, j] * value(k, j)
        return value

    def field_parts(w, closed):
        pair = [both(along_z(w[k])) for k in range(3)]
        zs = [pair[k][0] for k in range(3)]
        zd = [pair[k][1] for k in range(3)]
        ysx, ydx = both(along_y(w[0], closed))
        ysy, ydy = both(along_y(w[1], closed))
        ysz = plus(along_y(w[2], closed))
        yszsx, ydzsx = both(along_y(zs[0], closed))
        yszsy, ydzsy = both(along_y(zs[1], closed))
        yszsz = plus(along_y(zs[2], closed))
        yszdx = plus(along_y(zd[0], closed))
        ydzdy = minus(along_y(zd[1], closed))
        yszdz, ydzdz = both(along_y(zd[2], closed))
        here = [
            ysx + FLAT * yszsx + zs[0],
            AXIAL * ysy + PAIR * yszsy + zs[1] + CROSS2 * ydzdz,
            ysz + PAIR * yszsz + AXIAL * zs[2] + CROSS2 * ydzdy,
        ]
        even = [
            AXIAL * w[0] + PAIR * (zs[0] + ysx) + FULL * yszsx,
            w[1] + FLAT * zs[1] + PAIR * ysy + FULL * yszsy + CROSS3 * ydzdz,
            w[2] + PAIR * zs[2] + FLAT * ysz + FULL * yszsz + CROSS3 * ydzdy,
        ]
        odd = [
            CROSS2 * (ydy + zd[2]) + CROSS3 * (ydzsy + yszdz),
            CROSS2 * ydx + CROSS3 * ydzsx,
            CROSS2 * zd[0] + CROSS3 * yszdx,
        ]
        ahead = [even[k] + odd[k] for k in range(3)]
        behind = [even[k] - odd[k] for k in range(3)]
        return here, ahead, behind

    def sweep(closed, count, load, omega, value, store, root_s, push_s, inverse_s, shear_s):
        offset = (wide - count) // 2
        partial = None
        trail = None
        for i in range(count):
            r = root_s[i + offset]
            here, ahead, behind = field_parts([r * load(k, i) for k in range(3)], closed)
            if i >= 2:
                j = i - 1
                d = j + offset - 1
                free = 1.0 - value(3, d) * at_bottom
                old = [load(k, j) for k in range(3)]
                shear = [shear_s[k, d] for k in range(3)]
                rest = [
                    shear[0] * old[1] + shear[1] * old[2],
                    shear[0] * old[0] + shear[2] * old[2],
                    shear[1] * old[0] + shear[2] * old[1],
                ]
                for k in range(3):
                    pull = (partial[k] + ahead[k] - rest[k]) * (inverse_s[k, d] * free)
                    store(k, j - 1, (1.0 - omega) * old[k] + omega * (push_s[k, d] + pull))
            if i >= 1:
                partial = [here[k] + trail[k] for k in range(3)]
            trail = behind

    fold = rows // SUB
    inv_a = first_a.at[0]
    stiffness(fold, PAD, None, root_a, drive_a, inv_a, None)
    tensor(True, None, root_a, shear_a, inverse_a, None)
    value = pushes(case, lines_of(fold), drive_a, inv_a, inverse_a, push_a)

    def store_first_a(k, i, new):
        first_a[k, i] = new

    def store_third_a(k, i, new):
        for t in range(fold):
            third_n[k, i, pl.ds(PAD + t, SUB, stride=fold), :] = new[t]
            if 1 <= i <= cells:
                field_ref[k, i - 1, pl.ds(t, SUB, stride=fold), :] = new[t]

    arrays = (root_a, push_a, inverse_a, shear_a)
    sweep(
        True, wide - 2, lambda k, i: omegas[0] * push_a[k, i], omegas[1], value, store_first_a, *arrays
    )
    sweep(True, wide - 4, lambda k, i: first_a[k, i], omegas[2], value, store_third_a, *arrays)

    fold_b = result_n.shape[1] // SUB
    top = case * band - HALO
    y_of = top + lines_of(fold_b)
    keep_rows = ((y_of >= 0) & (y_of < rows)).astype(jnp.float32)
    inv_b = work_b.at[pl.ds(0, wide - 2)]
    stiffness(fold_b, PAD + top, keep_rows, root_b, drive_b, inv_b, factor_b)
    tensor(False, keep_rows, root_b, shear_b, inverse_b, main_b)
    gathered = work_b.at[pl.ds(wide - 2, cells)]
    empty = jnp.zeros((fold_b, SUB, depth), jnp.float32)
    for i in range(cells + 2):
        for n in range(6):
            squares_b[n, i] = empty
    for i in range(cells):
        gathered[i] = empty

    def store_first_b(k, i, new):
        first_b[k, i] = new

    def store_second_b(k, i, new):
        second_b[k, i] = new

    @pl.loop(0, groups)
    def add_case(other):
        @pl.when(other == 0)
        def take_own():
            for k in range(3):
                for i in range(cells + 2):
                    second_b[k, i] = jnp.stack(
                        [
                            third_n[k, i, pl.ds(PAD + top + t, SUB, stride=fold_b), :]
                            for t in range(fold_b)
                        ]
                    )

        @pl.when(other > 0)
        def relax_other():
            which = lax.rem(case + other, groups)
            value = pushes(which, y_of, drive_b, inv_b, inverse_b, push_b)
            arrays = (root_b, push_b, inverse_b, shear_b)
            sweep(
                False,
                wide - 2,
                lambda k, i: omegas[0] * push_b[k, i],
                omegas[1],
                value,
                store_first_b,
                *arrays,
            )
            sweep(
                False, wide - 4, lambda k, i: first_b[k, i], omegas[2], value, store_second_b, *arrays
            )

        partial = None
        trail = None
        for i in range(cells + 2):
            r = root_b[i + EDGE]
            v = [second_b[k, i] for k in range(3)]
            w = [r * v[k] for k in range(3)]
            for n, (a, b) in enumerate(((0, 0), (1, 1), (2, 2), (0, 1), (0, 2), (1, 2))):
                squares_b[n, i] += w[a] * v[b]
            here, ahead, behind = field_parts(w, False)
            if i >= 2:
                old = [second_b[k, i - 1] for k in range(3)]
                dot = [old[k] * (partial[k] + ahead[k]) for k in range(3)]
                gathered[i - 2] += dot[0] + dot[1] + dot[2]
            if i >= 1:
                partial = [here[k] + trail[k] for k in range(3)]
            trail = behind

    def square_parts(q):
        qxx, qyy, qzz, qxy, qxz, qyz = q
        s = qxx + qyy + qzz
        zs_s = plus(along_z(s))
        zs_x = plus(along_z(qxx))
        zs_z = plus(along_z(qzz))
        zs_xy = plus(along_z(qxy))
        zd_yz = minus(along_z(qyz))
        zd_xz = minus(along_z(qxz))
        twist = minus(along_y(zd_yz, False))
        half = 0.5 * zs_s + 0.125 * zs_z
        here = (
            zs_s
            + 0.5 * zs_z
            + plus(along_y(s + 0.5 * qyy + (PAIR * zs_s - 0.125 * zs_x), False))
            + 0.25 * twist
        )
        even = (
            s
            + 0.5 * qxx
            + half
            + 0.125 * zs_x
            + plus(along_y(0.5 * s + 0.125 * (qxx + qyy) + FULL * zs_s, False))
            + (1.0 / 12.0) * twist
        )
        odd = (
            minus(along_y(0.25 * qxy + (1.0 / 12.0) * zs_xy, False))
            + 0.25 * zd_xz
            + plus(along_y((1.0 / 12.0) * zd_xz, False))
        )
        return here, even + odd, even - odd

    partial = None
    trail = None
    for i in range(cells + 2):
        here, ahead, behind = square_parts([squares_b[n, i] for n in range(6)])
        if i >= 2:
            j = i - 2
            q = [squares_b[n, i - 1] for n in range(6)]
            d = j + EDGE
            held = main_b[0, j] * q[0] + main_b[1, j] * q[1] + main_b[2, j] * q[2]
            mixed = shear_b[0, d] * q[3] + shear_b[1, d] * q[4] + shear_b[2, d] * q[5]
            rest = partial + ahead - 2.0 * gathered[j]
            total = held + 2.0 * mixed + root_b[d + 1] * rest
            total = total * factor_b[j]
            for t in range(fold_b):
                result_n[j, pl.ds(t, SUB, stride=fold_b), :] = total[t]
        if i >= 1:
            partial = here + trail
        trail = behind
    sensitivity_ref[...] = result_n[:, HALO : HALO + band, :]


def on_vmem():
    return pl.BlockSpec(memory_space=pltpu.VMEM)


def on_smem():
    return pl.BlockSpec(memory_space=pltpu.SMEM)


def packed(density, void_depth, supports, load_x, load_y, load_vectors):
    cells, band, depth = density.shape
    copies = lax.axis_size("case") * CORES
    return pl.pallas_call(
        pack_kernel,
        out_shape=jax.ShapeDtypeStruct((copies, cells + 1, band, depth), jnp.float32),
        in_specs=[on_vmem()] * 2 + [on_smem()] * 4,
        out_specs=on_vmem(),
    )(density, void_depth, supports, load_x, load_y, load_vectors)


def relaxed(chip, halo):
    groups, cores, planes, band, depth = chip.shape
    cells = planes - 1
    rows = groups * band
    wide = cells + 2 * HALO
    fold = rows // SUB
    fold_b = -(-(band + 2 * HALO) // SUB)
    tall = PAD + rows + fold_b * SUB

    def area(*lead):
        return pltpu.VMEM((*lead, fold, SUB, depth), jnp.float32)

    def window(*lead):
        return pltpu.VMEM((*lead, fold_b, SUB, depth), jnp.float32)

    return pl.pallas_call(
        relax_kernel,
        out_shape=(
            jax.ShapeDtypeStruct((3, cells, rows, depth), jnp.float32),
            jax.ShapeDtypeStruct((cells, band, depth), jnp.float32),
        ),
        in_specs=[on_vmem()] * 2,
        out_specs=(on_vmem(), on_vmem()),
        scratch_shapes=[
            pltpu.VMEM((CORES * cells + 2 * HALO, tall, depth), jnp.float32),
            pltpu.VMEM((3, cells + 2, tall, depth), jnp.float32),
            pltpu.VMEM((cells, fold_b * SUB, depth), jnp.float32),
            area(wide),
            area(wide - 2),
            area(3, wide - 2),
            area(3, wide - 2),
            area(3, wide - 2),
            area(3, wide - 2),
            window(wide),
            window(wide - 2),
            window(3, wide - 2),
            window(3, wide - 2),
            window(3, wide - 2),
            window(3, wide - 4),
            window(3, cells),
            window(cells),
            window(3, cells + 2),
            window(6, cells + 2),
            window(wide - 2 + cells),
        ],
        compiler_params=pltpu.CompilerParams(vmem_limit_bytes=32 * 1024 * 1024),
    )(chip, halo)


def shards(density, void_depth, supports, load_x, load_y, load_vectors):
    cells, band, depth = density.shape
    groups = lax.axis_size("case")
    slabs = lax.axis_size("column") * CORES
    mine = packed(density, void_depth, supports, load_x, load_y, load_vectors)
    chip = lax.all_to_all(mine, ("case", "core"), split_axis=0, concat_axis=0, tiled=True)
    chip = chip.reshape(groups, CORES, cells + 1, band, depth)
    low = chip[:, 0, :HALO]
    high = chip[:, 1, cells - HALO : cells]
    near = jnp.where(lax.axis_index("core") == 0, low, high)
    pairs = [(i, i + 1) for i in range(1, slabs - 1, 2)]
    pairs += [(j, i) for i, j in pairs]
    halo = lax.ppermute(near, ("column", "core"), pairs)
    field, sensitivity = relaxed(chip, halo)
    return (field[None], sensitivity)


def solution(mesh):
    groups, slabs = mesh.devices.shape
    chips = Mesh(mesh.devices.reshape(groups, slabs // CORES, CORES), ("case", "column", "core"))
    space = ("column", "core")
    return jax.shard_map(
        shards,
        mesh=chips,
        in_specs=(
            P(space, "case", None),
            P(space, "case"),
            P("case", None),
            P("case"),
            P("case"),
            P("case", None, None),
        ),
        out_specs=(P("case", None, space, None, None), P(space, "case", None)),
        check_vma=False,
    )
```

```python
import math

import jax
import jax.numpy as jnp
from jax import lax
from jax.experimental import pallas as pl
from jax.experimental.pallas import tpu as pltpu
from jax.sharding import Mesh
from jax.sharding import PartitionSpec as P

SWEEPS = 3
LOADW = 8
EMIN = 0.001
LOWER = 0.06
UPPER = 3.0
PATCH = 4.0
SUB = 8
CORES = 2
HALO = SWEEPS + 1
EDGE = HALO - 1
PAD = 8

AXIAL = 1.5
PAIR = 0.625
FLAT = 0.5
FULL = 0.25 * (1.0 + 0.5 / 3.0)
CROSS2 = 0.125
CROSS3 = 0.125 / 3.0


def relaxations(count):
    middle = 0.5 * (UPPER + LOWER)
    radius = 0.5 * (UPPER - LOWER)
    return [
        1.0 / (middle + radius * math.cos(math.pi * (2 * index + 1) / (2 * count)))
        for index in range(count)
    ]


def both(pair):
    return pair[0] + pair[1], pair[0] - pair[1]


def plus(pair):
    return pair[0] + pair[1]


def minus(pair):
    return pair[0] - pair[1]


def span_of(cells):
    return CORES * cells + 2 * EDGE


def pack_kernel(
    density_in,
    void_in,
    supports_in,
    vectors_in,
    load_x_ref,
    load_y_ref,
    packed_ref,
    density_ref,
    void_ref,
    supports_ref,
    vectors_ref,
    arrived,
):
    fetches = [
        pltpu.make_async_copy(source, target, arrived.at[n])
        for n, (source, target) in enumerate(
            (
                (supports_in, supports_ref),
                (vectors_in, vectors_ref),
                (void_in, void_ref),
                (density_in, density_ref),
            )
        )
    ]
    for fetch in fetches:
        fetch.start()
    for fetch in fetches:
        fetch.wait()
    copies, planes, band, depth = packed_ref.shape
    cells = planes - 1
    total_x = vectors_ref.shape[2]
    span = span_of(cells)
    first = lax.axis_index("column") * (CORES * cells) - EDGE
    z_of = lax.broadcasted_iota(jnp.int32, (band, depth), 1)
    level = z_of - depth // 2
    eye = lax.broadcasted_iota(jnp.int32, (band, band), 0) == lax.broadcasted_iota(
        jnp.int32, (band, band), 1
    )
    for i in range(cells):
        line = jnp.broadcast_to(void_ref[i : i + 1, :], (band, band)).astype(jnp.float32)
        column = jnp.sum(jnp.where(eye, line, 0.0), axis=1, keepdims=True)
        top = jnp.broadcast_to(column, (band, depth)).astype(jnp.int32)
        hollow = (level >= 0) & (level < top)
        solid = jnp.where(hollow, 0.0, density_ref[i])
        for copy in range(copies):
            packed_ref[copy, i] = solid
    lane = lax.broadcasted_iota(jnp.int32, (1, depth), 1)
    row = jnp.where(lane == 5 * span, load_y_ref[0].astype(jnp.float32), 0.0)
    for m in range(span):
        place = first + m
        inside = jnp.logical_and(place >= 0, place < total_x)
        where = jnp.clip(place, 0, total_x - 1)
        for k in range(3):
            value = jnp.where(inside, vectors_ref[k, 0, where], 0.0)
            row = jnp.where(lane == k * span + m, value, row)
    place = first + lane - 3 * span
    pinned = (place < supports_ref[0, 0]) | (place >= total_x - supports_ref[0, 1])
    row = jnp.where((lane >= 3 * span) & (lane < 4 * span) & pinned, 1.0, row)
    place = first + lane - 4 * span
    loaded = (place >= load_x_ref[0]) & (place < load_x_ref[0] + LOADW)
    row = jnp.where((lane >= 4 * span) & (lane < 5 * span) & loaded, 1.0, row)
    for copy in range(copies):
        packed_ref[copy, cells] = jnp.broadcast_to(row, (band, depth))


def relax_kernel(
    chip_ref,
    halo_ref,
    field_ref,
    sensitivity_ref,
    natural,
    third_n,
    result_n,
    root_a,
    drive_a,
    push_a,
    inverse_a,
    shear_a,
    first_a,
    root_b,
    drive_b,
    push_b,
    inverse_b,
    shear_b,
    first_b,
    main_b,
    factor_b,
    second_b,
    squares_b,
    work_b,
):
    groups, cores, planes, band, depth = chip_ref.shape
    cells = planes - 1
    span = span_of(cells)
    rows = groups * band
    wide = cells + 2 * HALO
    core = lax.axis_index("core")
    case = lax.axis_index("case")
    chips = lax.axis_size("column")
    total_x = chips * CORES * cells
    first_plane = (lax.axis_index("column") * CORES + core) * cells
    shift = core * cells
    omegas = relaxations(SWEEPS)

    blank = jnp.zeros((PAD, depth), jnp.float32)
    tail = natural.shape[1] - PAD - rows
    for i in range(natural.shape[0]):
        natural[i, 0:PAD, :] = blank
        for at in range(PAD + rows, natural.shape[1], PAD):
            natural[i, at : at + PAD, :] = blank
    for k in range(3):
        for i in range(cells + 2):
            third_n[k, i, 0:PAD, :] = blank
            for at in range(PAD + rows, natural.shape[1], PAD):
                third_n[k, i, at : at + PAD, :] = blank
    for g in range(groups):
        lines = slice(PAD + g * band, PAD + (g + 1) * band)
        natural[0:HALO, lines, :] = halo_ref[g]
        for c in range(CORES):
            at = HALO + c * cells
            natural[at : at + cells, lines, :] = chip_ref[g, c, 0:cells]
        at = HALO + CORES * cells
        natural[at : at + HALO, lines, :] = halo_ref[g]

    tile = (1, SUB, depth)
    lane = lax.broadcasted_iota(jnp.int32, tile, 2)
    line = lax.broadcasted_iota(jnp.int32, tile, 1)
    not_first_z = (lane > 0).astype(jnp.float32)
    not_last_z = (lane < depth - 1).astype(jnp.float32)
    not_first_s = (line > 0).astype(jnp.float32)
    not_last_s = (line < SUB - 1).astype(jnp.float32)
    at_bottom = (lane == 0).astype(jnp.float32)

    def along_z(a):
        after = pltpu.roll(a, depth - 1, 2) * not_last_z
        before = pltpu.roll(a, 1, 2) * not_first_z
        return after, before

    def along_y(a, closed):
        fold = a.shape[0]
        after = pltpu.roll(a[0:1], SUB - 1, 1)
        before = pltpu.roll(a[fold - 1 : fold], 1, 1)
        if closed:
            after = after * not_last_s
            before = before * not_first_s
        return (
            jnp.concatenate([a[1:], after], axis=0),
            jnp.concatenate([before, a[:-1]], axis=0),
        )

    def inside_of(plane, margin):
        place = first_plane - margin + plane
        return jnp.logical_and(place >= 0, place < total_x).astype(jnp.float32)

    def lines_of(fold):
        shape = (fold, SUB, depth)
        return fold * lax.broadcasted_iota(jnp.int32, shape, 1) + lax.broadcasted_iota(
            jnp.int32, shape, 0
        )

    def case_values(which):
        plain = jnp.broadcast_to(chip_ref[which, 0, cells, 0:1, :], (SUB, depth))
        moved = pltpu.roll(plain, jnp.where(core == 0, 0, depth - cells), 1)

        def value(kind, j):
            at = kind * span + j
            return jnp.broadcast_to(moved[:, at : at + 1], (SUB, depth))[None]

        corner = jnp.broadcast_to(plain[:, 5 * span : 5 * span + 1], (SUB, depth))[None]
        return value, corner

    def patch_of(y_of, corner):
        y = y_of.astype(jnp.float32)
        high = lax.broadcasted_iota(jnp.int32, y_of.shape, 2) == depth - 1
        return jnp.where(high & (y >= corner) & (y < corner + LOADW), PATCH, 0.0)

    def stiffness(fold, start, keep_rows, root_s, drive_s, inv_s, factor_s):
        for i in range(wide):
            solid = jnp.stack(
                [natural[shift + i, pl.ds(start + t, SUB, stride=fold), :] for t in range(fold)]
            )
            stiff = EMIN + (1.0 - EMIN) * (solid * solid * solid)
            inv_root = lax.rsqrt(stiff)
            root = stiff * inv_root * inside_of(i, HALO)
            root_s[i] = root if keep_rows is None else root * keep_rows
            if 0 < i < wide - 1:
                drive_s[i - 1] = solid * inv_root
                inv_s[i - 1] = inv_root
            if factor_s is not None and HALO <= i < HALO + cells:
                ratio = solid * inv_root
                factor_s[i - HALO] = ((-1.5 * (1.0 - EMIN)) / groups) * (ratio * ratio)

    def tensor_parts(r, closed):
        zs, zd = both(along_z(r))
        ys, yd = both(along_y(r, closed))
        yszs, ydzs = both(along_y(zs, closed))
        yszd, ydzd = both(along_y(zd, closed))
        cross = ys + zs
        corner = PAIR * yszs
        here = [
            cross + FLAT * yszs,
            cross + 0.5 * ys + corner,
            cross + 0.5 * zs + corner,
            CROSS2 * ydzd,
        ]
        base = FULL * yszs + 0.5 * cross + r
        even = [
            base + 0.5 * r + 0.125 * cross,
            base + 0.125 * ys,
            base + 0.125 * zs,
            CROSS3 * ydzd,
        ]
        odd = [CROSS2 * yd + CROSS3 * ydzs, CROSS2 * zd + CROSS3 * yszd]
        return here, even, odd

    def tensor(closed, keep_rows, root_s, shear_s, inverse_s, main_s):
        older = None
        newer = None
        for i in range(wide):
            latest = tensor_parts(root_s[i], closed)
            if i >= 2:
                j = i - 2
                keep = inside_of(j, EDGE)
                if keep_rows is not None:
                    keep = keep * keep_rows
                total = [newer[0][k] + (latest[1][k] + older[1][k]) for k in range(4)]
                shear_s[0, j] = latest[2][0] - older[2][0]
                shear_s[1, j] = latest[2][1] - older[2][1]
                shear_s[2, j] = total[3]
                for k in range(3):
                    if main_s is not None and EDGE <= j < EDGE + cells:
                        main_s[k, j - EDGE] = total[k]
                    inverse_s[k, j] = keep / (total[k] + (1.0 - keep))
            older, newer = newer, latest

    def pushes(which, y_of, drive_s, inv_s, inverse_s, push_s):
        value, corner = case_values(which)
        patch = patch_of(y_of, corner)
        for j in range(wide - 2):
            free = 1.0 - value(3, j) * at_bottom
            push = (drive_s[j] + (value(4, j) * patch) * inv_s[j]) * free
            for k in range(3):
                push_s[k, j] = push * inverse_s[k, j] * value(k, j)
        return value

    def field_parts(w, closed):
        pair = [both(along_z(w[k])) for k in range(3)]
        zs = [pair[k][0] for k in range(3)]
        zd = [pair[k][1] for k in range(3)]
        ysx, ydx = both(along_y(w[0], closed))
        ysy, ydy = both(along_y(w[1], closed))
        ysz = plus(along_y(w[2], closed))
        yszsx, ydzsx = both(along_y(zs[0], closed))
        yszsy, ydzsy = both(along_y(zs[1], closed))
        yszsz = plus(along_y(zs[2], closed))
        yszdx = plus(along_y(zd[0], closed))
        ydzdy = minus(along_y(zd[1], closed))
        yszdz, ydzdz = both(along_y(zd[2], closed))
        here = [
            ysx + FLAT * yszsx + zs[0],
            AXIAL * ysy + PAIR * yszsy + zs[1] + CROSS2 * ydzdz,
            ysz + PAIR * yszsz + AXIAL * zs[2] + CROSS2 * ydzdy,
        ]
        even = [
            AXIAL * w[0] + PAIR * (zs[0] + ysx) + FULL * yszsx,
            w[1] + FLAT * zs[1] + PAIR * ysy + FULL * yszsy + CROSS3 * ydzdz,
            w[2] + PAIR * zs[2] + FLAT * ysz + FULL * yszsz + CROSS3 * ydzdy,
        ]
        odd = [
            CROSS2 * (ydy + zd[2]) + CROSS3 * (ydzsy + yszdz),
            CROSS2 * ydx + CROSS3 * ydzsx,
            CROSS2 * zd[0] + CROSS3 * yszdx,
        ]
        ahead = [even[k] + odd[k] for k in range(3)]
        behind = [even[k] - odd[k] for k in range(3)]
        return here, ahead, behind

    def sweep(closed, count, load, omega, value, store, root_s, push_s, inverse_s, shear_s):
        offset = (wide - count) // 2
        partial = None
        trail = None
        for i in range(count):
            r = root_s[i + offset]
            here, ahead, behind = field_parts([r * load(k, i) for k in range(3)], closed)
            if i >= 2:
                j = i - 1
                d = j + offset - 1
                free = 1.0 - value(3, d) * at_bottom
                old = [load(k, j) for k in range(3)]
                shear = [shear_s[k, d] for k in range(3)]
                rest = [
                    shear[0] * old[1] + shear[1] * old[2],
                    shear[0] * old[0] + shear[2] * old[2],
                    shear[1] * old[0] + shear[2] * old[1],
                ]
                for k in range(3):
                    pull = (partial[k] + ahead[k] - rest[k]) * (inverse_s[k, d] * free)
                    store(k, j - 1, (1.0 - omega) * old[k] + omega * (push_s[k, d] + pull))
            if i >= 1:
                partial = [here[k] + trail[k] for k in range(3)]
            trail = behind

    fold = rows // SUB
    inv_a = first_a.at[0]
    stiffness(fold, PAD, None, root_a, drive_a, inv_a, None)
    tensor(True, None, root_a, shear_a, inverse_a, None)
    value = pushes(case, lines_of(fold), drive_a, inv_a, inverse_a, push_a)

    def store_first_a(k, i, new):
        first_a[k, i] = new

    def store_third_a(k, i, new):
        for t in range(fold):
            third_n[k, i, pl.ds(PAD + t, SUB, stride=fold), :] = new[t]
            if 1 <= i <= cells:
                field_ref[k, i - 1, pl.ds(t, SUB, stride=fold), :] = new[t]

    arrays = (root_a, push_a, inverse_a, shear_a)
    sweep(
        True, wide - 2, lambda k, i: omegas[0] * push_a[k, i], omegas[1], value, store_first_a, *arrays
    )
    sweep(True, wide - 4, lambda k, i: first_a[k, i], omegas[2], value, store_third_a, *arrays)

    fold_b = result_n.shape[1] // SUB
    top = case * band - HALO
    y_of = top + lines_of(fold_b)
    keep_rows = ((y_of >= 0) & (y_of < rows)).astype(jnp.float32)
    inv_b = work_b.at[pl.ds(0, wide - 2)]
    stiffness(fold_b, PAD + top, keep_rows, root_b, drive_b, inv_b, factor_b)
    tensor(False, keep_rows, root_b, shear_b, inverse_b, main_b)
    gathered = work_b.at[pl.ds(wide - 2, cells)]
    empty = jnp.zeros((fold_b, SUB, depth), jnp.float32)
    for i in range(cells + 2):
        for n in range(6):
            squares_b[n, i] = empty
    for i in range(cells):
        gathered[i] = empty

    def store_first_b(k, i, new):
        first_b[k, i] = new

    def store_second_b(k, i, new):
        second_b[k, i] = new

    @pl.loop(0, groups)
    def add_case(other):
        @pl.when(other == 0)
        def take_own():
            for k in range(3):
                for i in range(cells + 2):
                    second_b[k, i] = jnp.stack(
                        [
                            third_n[k, i, pl.ds(PAD + top + t, SUB, stride=fold_b), :]
                            for t in range(fold_b)
                        ]
                    )

        @pl.when(other > 0)
        def relax_other():
            which = lax.rem(case + other, groups)
            value = pushes(which, y_of, drive_b, inv_b, inverse_b, push_b)
            arrays = (root_b, push_b, inverse_b, shear_b)
            sweep(
                False,
                wide - 2,
                lambda k, i: omegas[0] * push_b[k, i],
                omegas[1],
                value,
                store_first_b,
                *arrays,
            )
            sweep(
                False, wide - 4, lambda k, i: first_b[k, i], omegas[2], value, store_second_b, *arrays
            )

        partial = None
        trail = None
        for i in range(cells + 2):
            r = root_b[i + EDGE]
            v = [second_b[k, i] for k in range(3)]
            w = [r * v[k] for k in range(3)]
            for n, (a, b) in enumerate(((0, 0), (1, 1), (2, 2), (0, 1), (0, 2), (1, 2))):
                squares_b[n, i] += w[a] * v[b]
            here, ahead, behind = field_parts(w, False)
            if i >= 2:
                old = [second_b[k, i - 1] for k in range(3)]
                dot = [old[k] * (partial[k] + ahead[k]) for k in range(3)]
                gathered[i - 2] += dot[0] + dot[1] + dot[2]
            if i >= 1:
                partial = [here[k] + trail[k] for k in range(3)]
            trail = behind

    def square_parts(q):
        qxx, qyy, qzz, qxy, qxz, qyz = q
        s = qxx + qyy + qzz
        zs_s = plus(along_z(s))
        zs_x = plus(along_z(qxx))
        zs_z = plus(along_z(qzz))
        zs_xy = plus(along_z(qxy))
        zd_yz = minus(along_z(qyz))
        zd_xz = minus(along_z(qxz))
        twist = minus(along_y(zd_yz, False))
        half = 0.5 * zs_s + 0.125 * zs_z
        here = (
            zs_s
            + 0.5 * zs_z
            + plus(along_y(s + 0.5 * qyy + (PAIR * zs_s - 0.125 * zs_x), False))
            + 0.25 * twist
        )
        even = (
            s
            + 0.5 * qxx
            + half
            + 0.125 * zs_x
            + plus(along_y(0.5 * s + 0.125 * (qxx + qyy) + FULL * zs_s, False))
            + (1.0 / 12.0) * twist
        )
        odd = (
            minus(along_y(0.25 * qxy + (1.0 / 12.0) * zs_xy, False))
            + 0.25 * zd_xz
            + plus(along_y((1.0 / 12.0) * zd_xz, False))
        )
        return here, even + odd, even - odd

    partial = None
    trail = None
    for i in range(cells + 2):
        here, ahead, behind = square_parts([squares_b[n, i] for n in range(6)])
        if i >= 2:
            j = i - 2
            q = [squares_b[n, i - 1] for n in range(6)]
            d = j + EDGE
            held = main_b[0, j] * q[0] + main_b[1, j] * q[1] + main_b[2, j] * q[2]
            mixed = shear_b[0, d] * q[3] + shear_b[1, d] * q[4] + shear_b[2, d] * q[5]
            rest = partial + ahead - 2.0 * gathered[j]
            total = held + 2.0 * mixed + root_b[d + 1] * rest
            total = total * factor_b[j]
            for t in range(fold_b):
                result_n[j, pl.ds(t, SUB, stride=fold_b), :] = total[t]
        if i >= 1:
            partial = here + trail
        trail = behind
    sensitivity_ref[...] = result_n[:, HALO : HALO + band, :]


def on_vmem():
    return pl.BlockSpec(memory_space=pltpu.VMEM)


def on_smem():
    return pl.BlockSpec(memory_space=pltpu.SMEM)


def packed(density, void_depth, supports, load_x, load_y, load_vectors):
    cells, band, depth = density.shape
    copies = lax.axis_size("case") * CORES
    vectors = load_vectors.transpose(1, 0, 2)
    return pl.pallas_call(
        pack_kernel,
        out_shape=pltpu.VMEM((copies, cells + 1, band, depth), jnp.float32),
        in_specs=[pl.BlockSpec(memory_space=pltpu.HBM)] * 4 + [on_smem()] * 2,
        out_specs=on_vmem(),
        scratch_shapes=[
            pltpu.VMEM(density.shape, jnp.float32),
            pltpu.VMEM(void_depth.shape, jnp.int32),
            pltpu.SMEM(supports.shape, jnp.int32),
            pltpu.SMEM(vectors.shape, jnp.float32),
            pltpu.SemaphoreType.DMA((4,)),
        ],
    )(
        *(
            pltpu.with_memory_space_constraint(array, pltpu.HBM)
            for array in (density, void_depth, supports, vectors)
        ),
        load_x,
        load_y,
    )


def relaxed(chip, halo):
    groups, cores, planes, band, depth = chip.shape
    cells = planes - 1
    rows = groups * band
    wide = cells + 2 * HALO
    fold = rows // SUB
    fold_b = -(-(band + 2 * HALO) // SUB)
    tall = PAD + rows + fold_b * SUB

    def area(*lead):
        return pltpu.VMEM((*lead, fold, SUB, depth), jnp.float32)

    def window(*lead):
        return pltpu.VMEM((*lead, fold_b, SUB, depth), jnp.float32)

    return pl.pallas_call(
        relax_kernel,
        out_shape=(
            jax.ShapeDtypeStruct((3, cells, rows, depth), jnp.float32),
            jax.ShapeDtypeStruct((cells, band, depth), jnp.float32),
        ),
        in_specs=[on_vmem()] * 2,
        out_specs=(on_vmem(), on_vmem()),
        scratch_shapes=[
            pltpu.VMEM((CORES * cells + 2 * HALO, tall, depth), jnp.float32),
            pltpu.VMEM((3, cells + 2, tall, depth), jnp.float32),
            pltpu.VMEM((cells, fold_b * SUB, depth), jnp.float32),
            area(wide),
            area(wide - 2),
            area(3, wide - 2),
            area(3, wide - 2),
            area(3, wide - 2),
            area(3, wide - 2),
            window(wide),
            window(wide - 2),
            window(3, wide - 2),
            window(3, wide - 2),
            window(3, wide - 2),
            window(3, wide - 4),
            window(3, cells),
            window(cells),
            window(3, cells + 2),
            window(6, cells + 2),
            window(wide - 2 + cells),
        ],
        compiler_params=pltpu.CompilerParams(vmem_limit_bytes=32 * 1024 * 1024),
    )(chip, halo)


def shards(density, void_depth, supports, load_x, load_y, load_vectors):
    cells, band, depth = density.shape
    groups = lax.axis_size("case")
    slabs = lax.axis_size("column") * CORES
    mine = packed(density, void_depth, supports, load_x, load_y, load_vectors)
    chip = lax.all_to_all(mine, ("case", "core"), split_axis=0, concat_axis=0, tiled=True)
    chip = chip.reshape(groups, CORES, cells + 1, band, depth)
    low = chip[:, 0, :HALO]
    high = chip[:, 1, cells - HALO : cells]
    near = jnp.where(lax.axis_index("core") == 0, low, high)
    pairs = [(i, i + 1) for i in range(1, slabs - 1, 2)]
    pairs += [(j, i) for i, j in pairs]
    halo = lax.ppermute(near, ("column", "core"), pairs)
    field, sensitivity = relaxed(chip, halo)
    return (field[None], sensitivity)


def solution(mesh):
    groups, slabs = mesh.devices.shape
    chips = Mesh(mesh.devices.reshape(groups, slabs // CORES, CORES), ("case", "column", "core"))
    space = ("column", "core")
    return jax.shard_map(
        shards,
        mesh=chips,
        in_specs=(
            P(space, "case", None),
            P(space, "case"),
            P("case", None),
            P("case"),
            P("case"),
            P("case", None, None),
        ),
        out_specs=(P("case", None, space, None, None), P(space, "case", None)),
        check_vma=False,
    )
```

```python
import math

import jax
import jax.numpy as jnp
from jax import lax
from jax.experimental import pallas as pl
from jax.experimental.pallas import tpu as pltpu
from jax.sharding import PartitionSpec as P

SWEEPS = 3
LOADW = 8
EMIN = 0.001
LOWER = 0.06
UPPER = 3.0
PATCH = 4.0
SUB = 8
HALO = SWEEPS + 1
EDGE = HALO - 1
PAD = 8

AXIAL = 1.5
PAIR = 0.625
FLAT = 0.5
FULL = 0.25 * (1.0 + 0.5 / 3.0)
CROSS2 = 0.125
CROSS3 = 0.125 / 3.0


def relaxations(count):
    middle = 0.5 * (UPPER + LOWER)
    radius = 0.5 * (UPPER - LOWER)
    return [
        1.0 / (middle + radius * math.cos(math.pi * (2 * index + 1) / (2 * count)))
        for index in range(count)
    ]


def both(pair):
    return pair[0] + pair[1], pair[0] - pair[1]


def plus(pair):
    return pair[0] + pair[1]


def minus(pair):
    return pair[0] - pair[1]


def span_of(cells):
    return cells + 2 * EDGE


def settings_kernel(
    supports_in, vectors_in, load_x_ref, load_y_ref, row_ref, supports_ref, vectors_ref, arrived
):
    fetches = [
        pltpu.make_async_copy(supports_in, supports_ref, arrived.at[0]),
        pltpu.make_async_copy(vectors_in, vectors_ref, arrived.at[1]),
    ]
    for fetch in fetches:
        fetch.start()
    for fetch in fetches:
        fetch.wait()
    slabs = lax.axis_size("space")
    band, depth = row_ref.shape[1:]
    total_x = vectors_ref.shape[2]
    cells = total_x // slabs
    span = span_of(cells)
    first = lax.axis_index("space") * cells - EDGE
    lane = lax.broadcasted_iota(jnp.int32, (1, depth), 1)
    row = jnp.where(lane == 5 * span, load_y_ref[0].astype(jnp.float32), 0.0)
    for m in range(span):
        place = first + m
        inside = jnp.logical_and(place >= 0, place < total_x)
        where = jnp.clip(place, 0, total_x - 1)
        for k in range(3):
            value = jnp.where(inside, vectors_ref[k, 0, where], 0.0)
            row = jnp.where(lane == k * span + m, value, row)
    place = first + lane - 3 * span
    pinned = (place < supports_ref[0, 0]) | (place >= total_x - supports_ref[0, 1])
    row = jnp.where((lane >= 3 * span) & (lane < 4 * span) & pinned, 1.0, row)
    place = first + lane - 4 * span
    loaded = (place >= load_x_ref[0]) & (place < load_x_ref[0] + LOADW)
    row = jnp.where((lane >= 4 * span) & (lane < 5 * span) & loaded, 1.0, row)
    row_ref[0] = jnp.broadcast_to(row, (band, depth))


def relax_kernel(
    bands_ref,
    field_ref,
    sensitivity_ref,
    natural,
    third_n,
    result_n,
    root_a,
    drive_a,
    push_a,
    inverse_a,
    shear_a,
    first_a,
    root_b,
    drive_b,
    push_b,
    inverse_b,
    shear_b,
    first_b,
    main_b,
    factor_b,
    second_b,
    squares_b,
    work_b,
):
    groups, planes, band, depth = bands_ref.shape
    wide = planes - 1
    cells = wide - 2 * HALO
    span = span_of(cells)
    rows = groups * band
    case = lax.axis_index("case")
    total_x = lax.axis_size("space") * cells
    first_plane = lax.axis_index("space") * cells
    omegas = relaxations(SWEEPS)

    blank = jnp.zeros((PAD, depth), jnp.float32)
    for i in range(wide):
        natural[i, 0:PAD, :] = blank
        for at in range(PAD + rows, natural.shape[1], PAD):
            natural[i, at : at + PAD, :] = blank
    for k in range(3):
        for i in range(cells + 2):
            third_n[k, i, 0:PAD, :] = blank
            for at in range(PAD + rows, natural.shape[1], PAD):
                third_n[k, i, at : at + PAD, :] = blank
    for g in range(groups):
        natural[:, PAD + g * band : PAD + (g + 1) * band, :] = bands_ref[g, 0:wide]

    tile = (1, SUB, depth)
    lane = lax.broadcasted_iota(jnp.int32, tile, 2)
    line = lax.broadcasted_iota(jnp.int32, tile, 1)
    not_first_z = (lane > 0).astype(jnp.float32)
    not_last_z = (lane < depth - 1).astype(jnp.float32)
    not_first_s = (line > 0).astype(jnp.float32)
    not_last_s = (line < SUB - 1).astype(jnp.float32)
    at_bottom = (lane == 0).astype(jnp.float32)

    def along_z(a):
        after = pltpu.roll(a, depth - 1, 2) * not_last_z
        before = pltpu.roll(a, 1, 2) * not_first_z
        return after, before

    def along_y(a, closed):
        fold = a.shape[0]
        after = pltpu.roll(a[0:1], SUB - 1, 1)
        before = pltpu.roll(a[fold - 1 : fold], 1, 1)
        if closed:
            after = after * not_last_s
            before = before * not_first_s
        return (
            jnp.concatenate([a[1:], after], axis=0),
            jnp.concatenate([before, a[:-1]], axis=0),
        )

    def inside_of(plane, margin):
        place = first_plane - margin + plane
        return jnp.logical_and(place >= 0, place < total_x).astype(jnp.float32)

    def lines_of(fold):
        shape = (fold, SUB, depth)
        return fold * lax.broadcasted_iota(jnp.int32, shape, 1) + lax.broadcasted_iota(
            jnp.int32, shape, 0
        )

    def case_values(which):
        plain = jnp.broadcast_to(bands_ref[which, wide, 0:1, :], (SUB, depth))

        def value(kind, j):
            at = kind * span + j
            return jnp.broadcast_to(plain[:, at : at + 1], (SUB, depth))[None]

        corner = jnp.broadcast_to(plain[:, 5 * span : 5 * span + 1], (SUB, depth))[None]
        return value, corner

    def patch_of(y_of, corner):
        y = y_of.astype(jnp.float32)
        high = lax.broadcasted_iota(jnp.int32, y_of.shape, 2) == depth - 1
        return jnp.where(high & (y >= corner) & (y < corner + LOADW), PATCH, 0.0)

    def stiffness(fold, start, keep_rows, root_s, drive_s, inv_s, factor_s):
        for i in range(wide):
            solid = jnp.stack(
                [natural[i, pl.ds(start + t, SUB, stride=fold), :] for t in range(fold)]
            )
            stiff = EMIN + (1.0 - EMIN) * (solid * solid * solid)
            inv_root = lax.rsqrt(stiff)
            root = stiff * inv_root * inside_of(i, HALO)
            root_s[i] = root if keep_rows is None else root * keep_rows
            if 0 < i < wide - 1:
                drive_s[i - 1] = solid * inv_root
                inv_s[i - 1] = inv_root
            if factor_s is not None and HALO <= i < HALO + cells:
                ratio = solid * inv_root
                factor_s[i - HALO] = ((-1.5 * (1.0 - EMIN)) / groups) * (ratio * ratio)

    def tensor_parts(r, closed):
        zs, zd = both(along_z(r))
        ys, yd = both(along_y(r, closed))
        yszs, ydzs = both(along_y(zs, closed))
        yszd, ydzd = both(along_y(zd, closed))
        cross = ys + zs
        corner = PAIR * yszs
        here = [
            cross + FLAT * yszs,
            cross + 0.5 * ys + corner,
            cross + 0.5 * zs + corner,
            CROSS2 * ydzd,
        ]
        base = FULL * yszs + 0.5 * cross + r
        even = [
            base + 0.5 * r + 0.125 * cross,
            base + 0.125 * ys,
            base + 0.125 * zs,
            CROSS3 * ydzd,
        ]
        odd = [CROSS2 * yd + CROSS3 * ydzs, CROSS2 * zd + CROSS3 * yszd]
        return here, even, odd

    def tensor(closed, keep_rows, root_s, shear_s, inverse_s, main_s):
        older = None
        newer = None
        for i in range(wide):
            latest = tensor_parts(root_s[i], closed)
            if i >= 2:
                j = i - 2
                keep = inside_of(j, EDGE)
                if keep_rows is not None:
                    keep = keep * keep_rows
                total = [newer[0][k] + (latest[1][k] + older[1][k]) for k in range(4)]
                shear_s[0, j] = latest[2][0] - older[2][0]
                shear_s[1, j] = latest[2][1] - older[2][1]
                shear_s[2, j] = total[3]
                for k in range(3):
                    if main_s is not None and EDGE <= j < EDGE + cells:
                        main_s[k, j - EDGE] = total[k]
                    inverse_s[k, j] = keep / (total[k] + (1.0 - keep))
            older, newer = newer, latest

    def pushes(which, y_of, drive_s, inv_s, inverse_s, push_s):
        value, corner = case_values(which)
        patch = patch_of(y_of, corner)
        for j in range(wide - 2):
            free = 1.0 - value(3, j) * at_bottom
            push = (drive_s[j] + (value(4, j) * patch) * inv_s[j]) * free
            for k in range(3):
                push_s[k, j] = push * inverse_s[k, j] * value(k, j)
        return value

    def field_parts(w, closed):
        pair = [both(along_z(w[k])) for k in range(3)]
        zs = [pair[k][0] for k in range(3)]
        zd = [pair[k][1] for k in range(3)]
        ysx, ydx = both(along_y(w[0], closed))
        ysy, ydy = both(along_y(w[1], closed))
        ysz = plus(along_y(w[2], closed))
        yszsx, ydzsx = both(along_y(zs[0], closed))
        yszsy, ydzsy = both(along_y(zs[1], closed))
        yszsz = plus(along_y(zs[2], closed))
        yszdx = plus(along_y(zd[0], closed))
        ydzdy = minus(along_y(zd[1], closed))
        yszdz, ydzdz = both(along_y(zd[2], closed))
        here = [
            ysx + FLAT * yszsx + zs[0],
            AXIAL * ysy + PAIR * yszsy + zs[1] + CROSS2 * ydzdz,
            ysz + PAIR * yszsz + AXIAL * zs[2] + CROSS2 * ydzdy,
        ]
        even = [
            AXIAL * w[0] + PAIR * (zs[0] + ysx) + FULL * yszsx,
            w[1] + FLAT * zs[1] + PAIR * ysy + FULL * yszsy + CROSS3 * ydzdz,
            w[2] + PAIR * zs[2] + FLAT * ysz + FULL * yszsz + CROSS3 * ydzdy,
        ]
        odd = [
            CROSS2 * (ydy + zd[2]) + CROSS3 * (ydzsy + yszdz),
            CROSS2 * ydx + CROSS3 * ydzsx,
            CROSS2 * zd[0] + CROSS3 * yszdx,
        ]
        ahead = [even[k] + odd[k] for k in range(3)]
        behind = [even[k] - odd[k] for k in range(3)]
        return here, ahead, behind

    def sweep(closed, count, load, omega, value, store, root_s, push_s, inverse_s, shear_s):
        offset = (wide - count) // 2
        partial = None
        trail = None
        for i in range(count):
            r = root_s[i + offset]
            here, ahead, behind = field_parts([r * load(k, i) for k in range(3)], closed)
            if i >= 2:
                j = i - 1
                d = j + offset - 1
                free = 1.0 - value(3, d) * at_bottom
                old = [load(k, j) for k in range(3)]
                shear = [shear_s[k, d] for k in range(3)]
                rest = [
                    shear[0] * old[1] + shear[1] * old[2],
                    shear[0] * old[0] + shear[2] * old[2],
                    shear[1] * old[0] + shear[2] * old[1],
                ]
                for k in range(3):
                    pull = (partial[k] + ahead[k] - rest[k]) * (inverse_s[k, d] * free)
                    store(k, j - 1, (1.0 - omega) * old[k] + omega * (push_s[k, d] + pull))
            if i >= 1:
                partial = [here[k] + trail[k] for k in range(3)]
            trail = behind

    fold = rows // SUB
    inv_a = first_a.at[0]
    stiffness(fold, PAD, None, root_a, drive_a, inv_a, None)
    tensor(True, None, root_a, shear_a, inverse_a, None)
    value = pushes(case, lines_of(fold), drive_a, inv_a, inverse_a, push_a)

    def store_first_a(k, i, new):
        first_a[k, i] = new

    def store_third_a(k, i, new):
        for t in range(fold):
            third_n[k, i, pl.ds(PAD + t, SUB, stride=fold), :] = new[t]
            if 1 <= i <= cells:
                field_ref[k, i - 1, pl.ds(t, SUB, stride=fold), :] = new[t]

    arrays = (root_a, push_a, inverse_a, shear_a)
    sweep(
        True, wide - 2, lambda k, i: omegas[0] * push_a[k, i], omegas[1], value, store_first_a, *arrays
    )
    sweep(True, wide - 4, lambda k, i: first_a[k, i], omegas[2], value, store_third_a, *arrays)

    fold_b = result_n.shape[1] // SUB
    top = case * band - HALO
    y_of = top + lines_of(fold_b)
    keep_rows = ((y_of >= 0) & (y_of < rows)).astype(jnp.float32)
    inv_b = work_b.at[pl.ds(0, wide - 2)]
    stiffness(fold_b, PAD + top, keep_rows, root_b, drive_b, inv_b, factor_b)
    tensor(False, keep_rows, root_b, shear_b, inverse_b, main_b)
    gathered = work_b.at[pl.ds(wide - 2, cells)]
    empty = jnp.zeros((fold_b, SUB, depth), jnp.float32)
    for i in range(cells + 2):
        for n in range(6):
            squares_b[n, i] = empty
    for i in range(cells):
        gathered[i] = empty

    def store_first_b(k, i, new):
        first_b[k, i] = new

    def store_second_b(k, i, new):
        second_b[k, i] = new

    @pl.loop(0, groups)
    def add_case(other):
        @pl.when(other == 0)
        def take_own():
            for k in range(3):
                for i in range(cells + 2):
                    second_b[k, i] = jnp.stack(
                        [
                            third_n[k, i, pl.ds(PAD + top + t, SUB, stride=fold_b), :]
                            for t in range(fold_b)
                        ]
                    )

        @pl.when(other > 0)
        def relax_other():
            which = lax.rem(case + other, groups)
            value = pushes(which, y_of, drive_b, inv_b, inverse_b, push_b)
            arrays = (root_b, push_b, inverse_b, shear_b)
            sweep(
                False,
                wide - 2,
                lambda k, i: omegas[0] * push_b[k, i],
                omegas[1],
                value,
                store_first_b,
                *arrays,
            )
            sweep(
                False, wide - 4, lambda k, i: first_b[k, i], omegas[2], value, store_second_b, *arrays
            )

        partial = None
        trail = None
        for i in range(cells + 2):
            r = root_b[i + EDGE]
            v = [second_b[k, i] for k in range(3)]
            w = [r * v[k] for k in range(3)]
            for n, (a, b) in enumerate(((0, 0), (1, 1), (2, 2), (0, 1), (0, 2), (1, 2))):
                squares_b[n, i] += w[a] * v[b]
            here, ahead, behind = field_parts(w, False)
            if i >= 2:
                old = [second_b[k, i - 1] for k in range(3)]
                dot = [old[k] * (partial[k] + ahead[k]) for k in range(3)]
                gathered[i - 2] += dot[0] + dot[1] + dot[2]
            if i >= 1:
                partial = [here[k] + trail[k] for k in range(3)]
            trail = behind

    def square_parts(q):
        qxx, qyy, qzz, qxy, qxz, qyz = q
        s = qxx + qyy + qzz
        zs_s = plus(along_z(s))
        zs_x = plus(along_z(qxx))
        zs_z = plus(along_z(qzz))
        zs_xy = plus(along_z(qxy))
        zd_yz = minus(along_z(qyz))
        zd_xz = minus(along_z(qxz))
        twist = minus(along_y(zd_yz, False))
        half = 0.5 * zs_s + 0.125 * zs_z
        here = (
            zs_s
            + 0.5 * zs_z
            + plus(along_y(s + 0.5 * qyy + (PAIR * zs_s - 0.125 * zs_x), False))
            + 0.25 * twist
        )
        even = (
            s
            + 0.5 * qxx
            + half
            + 0.125 * zs_x
            + plus(along_y(0.5 * s + 0.125 * (qxx + qyy) + FULL * zs_s, False))
            + (1.0 / 12.0) * twist
        )
        odd = (
            minus(along_y(0.25 * qxy + (1.0 / 12.0) * zs_xy, False))
            + 0.25 * zd_xz
            + plus(along_y((1.0 / 12.0) * zd_xz, False))
        )
        return here, even + odd, even - odd

    partial = None
    trail = None
    for i in range(cells + 2):
        here, ahead, behind = square_parts([squares_b[n, i] for n in range(6)])
        if i >= 2:
            j = i - 2
            q = [squares_b[n, i - 1] for n in range(6)]
            d = j + EDGE
            held = main_b[0, j] * q[0] + main_b[1, j] * q[1] + main_b[2, j] * q[2]
            mixed = shear_b[0, d] * q[3] + shear_b[1, d] * q[4] + shear_b[2, d] * q[5]
            rest = partial + ahead - 2.0 * gathered[j]
            total = held + 2.0 * mixed + root_b[d + 1] * rest
            total = total * factor_b[j]
            for t in range(fold_b):
                result_n[j, pl.ds(t, SUB, stride=fold_b), :] = total[t]
        if i >= 1:
            partial = here + trail
        trail = behind
    sensitivity_ref[...] = result_n[:, HALO : HALO + band, :]


def on_vmem():
    return pl.BlockSpec(memory_space=pltpu.VMEM)


def on_smem():
    return pl.BlockSpec(memory_space=pltpu.SMEM)


def settings(band, depth, supports, load_x, load_y, load_vectors):
    vectors = load_vectors.transpose(1, 0, 2)
    return pl.pallas_call(
        settings_kernel,
        out_shape=jax.ShapeDtypeStruct((1, band, depth), jnp.float32),
        in_specs=[pl.BlockSpec(memory_space=pltpu.HBM)] * 2 + [on_smem()] * 2,
        out_specs=on_vmem(),
        scratch_shapes=[
            pltpu.SMEM(supports.shape, jnp.int32),
            pltpu.SMEM(vectors.shape, jnp.float32),
            pltpu.SemaphoreType.DMA((2,)),
        ],
    )(
        *(pltpu.with_memory_space_constraint(array, pltpu.HBM) for array in (supports, vectors)),
        load_x,
        load_y,
    )


def relaxed(bands):
    groups, planes, band, depth = bands.shape
    wide = planes - 1
    cells = wide - 2 * HALO
    rows = groups * band
    fold = rows // SUB
    fold_b = -(-(band + 2 * HALO) // SUB)
    tall = PAD + rows + fold_b * SUB

    def area(*lead):
        return pltpu.VMEM((*lead, fold, SUB, depth), jnp.float32)

    def window(*lead):
        return pltpu.VMEM((*lead, fold_b, SUB, depth), jnp.float32)

    return pl.pallas_call(
        relax_kernel,
        out_shape=(
            jax.ShapeDtypeStruct((3, cells, rows, depth), jnp.float32),
            jax.ShapeDtypeStruct((cells, band, depth), jnp.float32),
        ),
        in_specs=[on_vmem()],
        out_specs=(on_vmem(), on_vmem()),
        scratch_shapes=[
            pltpu.VMEM((wide, tall, depth), jnp.float32),
            pltpu.VMEM((3, cells + 2, tall, depth), jnp.float32),
            pltpu.VMEM((cells, fold_b * SUB, depth), jnp.float32),
            area(wide),
            area(wide - 2),
            area(3, wide - 2),
            area(3, wide - 2),
            area(3, wide - 2),
            area(3, wide - 2),
            window(wide),
            window(wide - 2),
            window(3, wide - 2),
            window(3, wide - 2),
            window(3, wide - 2),
            window(3, wide - 4),
            window(3, cells),
            window(cells),
            window(3, cells + 2),
            window(6, cells + 2),
            window(wide - 2 + cells),
        ],
        compiler_params=pltpu.CompilerParams(vmem_limit_bytes=32 * 1024 * 1024),
    )(bands)


def shards(density, void_depth, supports, load_x, load_y, load_vectors):
    cells, band, depth = density.shape
    groups = lax.axis_size("case")
    slabs = lax.axis_size("space")
    level = lax.broadcasted_iota(jnp.int32, density.shape, 2) - depth // 2
    hollow = (level >= 0) & (level < void_depth[:, :, None])
    solid = jnp.where(hollow, 0.0, density)
    ahead = [(i, i + 1) for i in range(slabs - 1)]
    behind = [(i + 1, i) for i in range(slabs - 1)]
    low = lax.ppermute(solid[cells - HALO :], "space", ahead)
    high = lax.ppermute(solid[:HALO], "space", behind)
    row = settings(band, depth, supports, load_x, load_y, load_vectors)
    mine = jnp.concatenate([low, solid, high, row])
    mine = jnp.broadcast_to(mine[None], (groups, *mine.shape))
    bands = lax.all_to_all(mine, "case", split_axis=0, concat_axis=0, tiled=True)
    field, sensitivity = relaxed(bands)
    return (field[None], sensitivity)


def solution(mesh):
    return jax.shard_map(
        shards,
        mesh=mesh,
        in_specs=(
            P("space", "case", None),
            P("space", "case"),
            P("case", None),
            P("case"),
            P("case"),
            P("case", None, None),
        ),
        out_specs=(P("case", None, "space", None, None), P("space", "case", None)),
        check_vma=False,
    )
```

```python
import math

import jax
import jax.numpy as jnp
from jax import lax
from jax.experimental import pallas as pl
from jax.experimental.pallas import tpu as pltpu
from jax.sharding import PartitionSpec as P

SWEEPS = 3
LOADW = 8
EMIN = 0.001
LOWER = 0.06
UPPER = 3.0
PATCH = 4.0
SUB = 8
CORES = 2
HALO = SWEEPS + 1
EDGE = HALO - 1
PAD = 8

AXIAL = 1.5
PAIR = 0.625
FLAT = 0.5
FULL = 0.25 * (1.0 + 0.5 / 3.0)
CROSS2 = 0.125
CROSS3 = 0.125 / 3.0


def relaxations(count):
    middle = 0.5 * (UPPER + LOWER)
    radius = 0.5 * (UPPER - LOWER)
    return [
        1.0 / (middle + radius * math.cos(math.pi * (2 * index + 1) / (2 * count)))
        for index in range(count)
    ]


def both(pair):
    return pair[0] + pair[1], pair[0] - pair[1]


def plus(pair):
    return pair[0] + pair[1]


def minus(pair):
    return pair[0] - pair[1]


def span_of(cells):
    return cells + 2 * EDGE


def settings_kernel(
    supports_in, vectors_in, load_x_ref, load_y_ref, row_ref, supports_ref, vectors_ref, arrived
):
    fetches = [
        pltpu.make_async_copy(supports_in, supports_ref, arrived.at[0]),
        pltpu.make_async_copy(vectors_in, vectors_ref, arrived.at[1]),
    ]
    for fetch in fetches:
        fetch.start()
    for fetch in fetches:
        fetch.wait()
    slabs = lax.axis_size("space")
    band, depth = row_ref.shape[1:]
    total_x = vectors_ref.shape[2]
    cells = total_x // slabs
    span = span_of(cells)
    first = lax.axis_index("space") * cells - EDGE
    lane = lax.broadcasted_iota(jnp.int32, (1, depth), 1)
    row = jnp.where(lane == 5 * span, load_y_ref[0].astype(jnp.float32), 0.0)
    for m in range(span):
        place = first + m
        inside = jnp.logical_and(place >= 0, place < total_x)
        where = jnp.clip(place, 0, total_x - 1)
        for k in range(3):
            value = jnp.where(inside, vectors_ref[k, 0, where], 0.0)
            row = jnp.where(lane == k * span + m, value, row)
    place = first + lane - 3 * span
    pinned = (place < supports_ref[0, 0]) | (place >= total_x - supports_ref[0, 1])
    row = jnp.where((lane >= 3 * span) & (lane < 4 * span) & pinned, 1.0, row)
    place = first + lane - 4 * span
    loaded = (place >= load_x_ref[0]) & (place < load_x_ref[0] + LOADW)
    row = jnp.where((lane >= 4 * span) & (lane < 5 * span) & loaded, 1.0, row)
    row_ref[0] = jnp.broadcast_to(row, (band, depth))


def relax_kernel(
    bands_ref,
    field_ref,
    sensitivity_ref,
    natural,
    third_n,
    result_n,
    root_a,
    drive_a,
    push_a,
    inverse_a,
    shear_a,
    first_a,
    root_b,
    drive_b,
    push_b,
    inverse_b,
    shear_b,
    first_b,
    main_b,
    factor_b,
    second_b,
    squares_b,
    work_b,
):
    groups, planes, band, depth = bands_ref.shape
    wide = planes - 1
    cells = wide - 2 * HALO
    span = span_of(cells)
    rows = groups * band
    case = lax.axis_index("case")
    total_x = lax.axis_size("space") * cells
    first_plane = lax.axis_index("space") * cells
    omegas = relaxations(SWEEPS)

    blank = jnp.zeros((PAD, depth), jnp.float32)
    for i in range(wide):
        natural[i, 0:PAD, :] = blank
        for at in range(PAD + rows, natural.shape[1], PAD):
            natural[i, at : at + PAD, :] = blank
    for k in range(3):
        for i in range(cells + 2):
            third_n[k, i, 0:PAD, :] = blank
            for at in range(PAD + rows, natural.shape[1], PAD):
                third_n[k, i, at : at + PAD, :] = blank
    for g in range(groups):
        natural[:, PAD + g * band : PAD + (g + 1) * band, :] = bands_ref[g, 0:wide]

    tile = (1, SUB, depth)
    lane = lax.broadcasted_iota(jnp.int32, tile, 2)
    line = lax.broadcasted_iota(jnp.int32, tile, 1)
    not_first_z = (lane > 0).astype(jnp.float32)
    not_last_z = (lane < depth - 1).astype(jnp.float32)
    not_first_s = (line > 0).astype(jnp.float32)
    not_last_s = (line < SUB - 1).astype(jnp.float32)
    at_bottom = (lane == 0).astype(jnp.float32)

    def along_z(a):
        after = pltpu.roll(a, depth - 1, 2) * not_last_z
        before = pltpu.roll(a, 1, 2) * not_first_z
        return after, before

    def along_y(a, closed):
        fold = a.shape[0]
        after = pltpu.roll(a[0:1], SUB - 1, 1)
        before = pltpu.roll(a[fold - 1 : fold], 1, 1)
        if closed:
            after = after * not_last_s
            before = before * not_first_s
        return (
            jnp.concatenate([a[1:], after], axis=0),
            jnp.concatenate([before, a[:-1]], axis=0),
        )

    def inside_of(plane, margin):
        place = first_plane - margin + plane
        return jnp.logical_and(place >= 0, place < total_x).astype(jnp.float32)

    def lines_of(fold):
        shape = (fold, SUB, depth)
        return fold * lax.broadcasted_iota(jnp.int32, shape, 1) + lax.broadcasted_iota(
            jnp.int32, shape, 0
        )

    def case_values(which):
        plain = jnp.broadcast_to(bands_ref[which, wide, 0:1, :], (SUB, depth))

        def value(kind, j):
            at = kind * span + j
            return jnp.broadcast_to(plain[:, at : at + 1], (SUB, depth))[None]

        corner = jnp.broadcast_to(plain[:, 5 * span : 5 * span + 1], (SUB, depth))[None]
        return value, corner

    def patch_of(y_of, corner):
        y = y_of.astype(jnp.float32)
        high = lax.broadcasted_iota(jnp.int32, y_of.shape, 2) == depth - 1
        return jnp.where(high & (y >= corner) & (y < corner + LOADW), PATCH, 0.0)

    def stiffness(fold, start, keep_rows, root_s, drive_s, inv_s, factor_s):
        for i in range(wide):
            solid = jnp.stack(
                [natural[i, pl.ds(start + t, SUB, stride=fold), :] for t in range(fold)]
            )
            stiff = EMIN + (1.0 - EMIN) * (solid * solid * solid)
            inv_root = lax.rsqrt(stiff)
            root = stiff * inv_root * inside_of(i, HALO)
            root_s[i] = root if keep_rows is None else root * keep_rows
            if 0 < i < wide - 1:
                drive_s[i - 1] = solid * inv_root
                inv_s[i - 1] = inv_root
            if factor_s is not None and HALO <= i < HALO + cells:
                ratio = solid * inv_root
                factor_s[i - HALO] = ((-1.5 * (1.0 - EMIN)) / groups) * (ratio * ratio)

    def tensor_parts(r, closed):
        zs, zd = both(along_z(r))
        ys, yd = both(along_y(r, closed))
        yszs, ydzs = both(along_y(zs, closed))
        yszd, ydzd = both(along_y(zd, closed))
        cross = ys + zs
        corner = PAIR * yszs
        here = [
            cross + FLAT * yszs,
            cross + 0.5 * ys + corner,
            cross + 0.5 * zs + corner,
            CROSS2 * ydzd,
        ]
        base = FULL * yszs + 0.5 * cross + r
        even = [
            base + 0.5 * r + 0.125 * cross,
            base + 0.125 * ys,
            base + 0.125 * zs,
            CROSS3 * ydzd,
        ]
        odd = [CROSS2 * yd + CROSS3 * ydzs, CROSS2 * zd + CROSS3 * yszd]
        return here, even, odd

    def tensor(closed, keep_rows, root_s, shear_s, inverse_s, main_s):
        older = None
        newer = None
        for i in range(wide):
            latest = tensor_parts(root_s[i], closed)
            if i >= 2:
                j = i - 2
                keep = inside_of(j, EDGE)
                if keep_rows is not None:
                    keep = keep * keep_rows
                total = [newer[0][k] + (latest[1][k] + older[1][k]) for k in range(4)]
                shear_s[0, j] = latest[2][0] - older[2][0]
                shear_s[1, j] = latest[2][1] - older[2][1]
                shear_s[2, j] = total[3]
                for k in range(3):
                    if main_s is not None and EDGE <= j < EDGE + cells:
                        main_s[k, j - EDGE] = total[k]
                    inverse_s[k, j] = keep / (total[k] + (1.0 - keep))
            older, newer = newer, latest

    def pushes(which, y_of, drive_s, inv_s, inverse_s, push_s):
        value, corner = case_values(which)
        patch = patch_of(y_of, corner)
        for j in range(wide - 2):
            free = 1.0 - value(3, j) * at_bottom
            push = (drive_s[j] + (value(4, j) * patch) * inv_s[j]) * free
            for k in range(3):
                push_s[k, j] = push * inverse_s[k, j] * value(k, j)
        return value

    def field_parts(w, closed):
        pair = [both(along_z(w[k])) for k in range(3)]
        zs = [pair[k][0] for k in range(3)]
        zd = [pair[k][1] for k in range(3)]
        ysx, ydx = both(along_y(w[0], closed))
        ysy, ydy = both(along_y(w[1], closed))
        ysz = plus(along_y(w[2], closed))
        yszsx, ydzsx = both(along_y(zs[0], closed))
        yszsy, ydzsy = both(along_y(zs[1], closed))
        yszsz = plus(along_y(zs[2], closed))
        yszdx = plus(along_y(zd[0], closed))
        ydzdy = minus(along_y(zd[1], closed))
        yszdz, ydzdz = both(along_y(zd[2], closed))
        here = [
            ysx + FLAT * yszsx + zs[0],
            AXIAL * ysy + PAIR * yszsy + zs[1] + CROSS2 * ydzdz,
            ysz + PAIR * yszsz + AXIAL * zs[2] + CROSS2 * ydzdy,
        ]
        even = [
            AXIAL * w[0] + PAIR * (zs[0] + ysx) + FULL * yszsx,
            w[1] + FLAT * zs[1] + PAIR * ysy + FULL * yszsy + CROSS3 * ydzdz,
            w[2] + PAIR * zs[2] + FLAT * ysz + FULL * yszsz + CROSS3 * ydzdy,
        ]
        odd = [
            CROSS2 * (ydy + zd[2]) + CROSS3 * (ydzsy + yszdz),
            CROSS2 * ydx + CROSS3 * ydzsx,
            CROSS2 * zd[0] + CROSS3 * yszdx,
        ]
        ahead = [even[k] + odd[k] for k in range(3)]
        behind = [even[k] - odd[k] for k in range(3)]
        return here, ahead, behind

    def sweep(closed, count, load, omega, value, store, root_s, push_s, inverse_s, shear_s):
        offset = (wide - count) // 2
        partial = None
        trail = None
        for i in range(count):
            r = root_s[i + offset]
            here, ahead, behind = field_parts([r * load(k, i) for k in range(3)], closed)
            if i >= 2:
                j = i - 1
                d = j + offset - 1
                free = 1.0 - value(3, d) * at_bottom
                old = [load(k, j) for k in range(3)]
                shear = [shear_s[k, d] for k in range(3)]
                rest = [
                    shear[0] * old[1] + shear[1] * old[2],
                    shear[0] * old[0] + shear[2] * old[2],
                    shear[1] * old[0] + shear[2] * old[1],
                ]
                for k in range(3):
                    pull = (partial[k] + ahead[k] - rest[k]) * (inverse_s[k, d] * free)
                    store(k, j - 1, (1.0 - omega) * old[k] + omega * (push_s[k, d] + pull))
            if i >= 1:
                partial = [here[k] + trail[k] for k in range(3)]
            trail = behind

    fold = rows // SUB
    inv_a = first_a.at[0]
    stiffness(fold, PAD, None, root_a, drive_a, inv_a, None)
    tensor(True, None, root_a, shear_a, inverse_a, None)
    value = pushes(case, lines_of(fold), drive_a, inv_a, inverse_a, push_a)

    def store_first_a(k, i, new):
        first_a[k, i] = new

    def store_third_a(k, i, new):
        for t in range(fold):
            third_n[k, i, pl.ds(PAD + t, SUB, stride=fold), :] = new[t]
            if 1 <= i <= cells:
                field_ref[k, i - 1, pl.ds(t, SUB, stride=fold), :] = new[t]

    arrays = (root_a, push_a, inverse_a, shear_a)
    sweep(
        True, wide - 2, lambda k, i: omegas[0] * push_a[k, i], omegas[1], value, store_first_a, *arrays
    )
    sweep(True, wide - 4, lambda k, i: first_a[k, i], omegas[2], value, store_third_a, *arrays)

    fold_b = result_n.shape[1] // SUB
    top = case * band - HALO
    y_of = top + lines_of(fold_b)
    keep_rows = ((y_of >= 0) & (y_of < rows)).astype(jnp.float32)
    inv_b = work_b.at[pl.ds(0, wide - 2)]
    stiffness(fold_b, PAD + top, keep_rows, root_b, drive_b, inv_b, factor_b)
    tensor(False, keep_rows, root_b, shear_b, inverse_b, main_b)
    gathered = work_b.at[pl.ds(wide - 2, cells)]
    empty = jnp.zeros((fold_b, SUB, depth), jnp.float32)
    for i in range(cells + 2):
        for n in range(6):
            squares_b[n, i] = empty
    for i in range(cells):
        gathered[i] = empty

    def store_first_b(k, i, new):
        first_b[k, i] = new

    def store_second_b(k, i, new):
        second_b[k, i] = new

    @pl.loop(0, groups)
    def add_case(other):
        @pl.when(other == 0)
        def take_own():
            for k in range(3):
                for i in range(cells + 2):
                    second_b[k, i] = jnp.stack(
                        [
                            third_n[k, i, pl.ds(PAD + top + t, SUB, stride=fold_b), :]
                            for t in range(fold_b)
                        ]
                    )

        @pl.when(other > 0)
        def relax_other():
            which = lax.rem(case + other, groups)
            value = pushes(which, y_of, drive_b, inv_b, inverse_b, push_b)
            arrays = (root_b, push_b, inverse_b, shear_b)
            sweep(
                False,
                wide - 2,
                lambda k, i: omegas[0] * push_b[k, i],
                omegas[1],
                value,
                store_first_b,
                *arrays,
            )
            sweep(
                False, wide - 4, lambda k, i: first_b[k, i], omegas[2], value, store_second_b, *arrays
            )

        partial = None
        trail = None
        for i in range(cells + 2):
            r = root_b[i + EDGE]
            v = [second_b[k, i] for k in range(3)]
            w = [r * v[k] for k in range(3)]
            for n, (a, b) in enumerate(((0, 0), (1, 1), (2, 2), (0, 1), (0, 2), (1, 2))):
                squares_b[n, i] += w[a] * v[b]
            here, ahead, behind = field_parts(w, False)
            if i >= 2:
                old = [second_b[k, i - 1] for k in range(3)]
                dot = [old[k] * (partial[k] + ahead[k]) for k in range(3)]
                gathered[i - 2] += dot[0] + dot[1] + dot[2]
            if i >= 1:
                partial = [here[k] + trail[k] for k in range(3)]
            trail = behind

    def square_parts(q):
        qxx, qyy, qzz, qxy, qxz, qyz = q
        s = qxx + qyy + qzz
        zs_s = plus(along_z(s))
        zs_x = plus(along_z(qxx))
        zs_z = plus(along_z(qzz))
        zs_xy = plus(along_z(qxy))
        zd_yz = minus(along_z(qyz))
        zd_xz = minus(along_z(qxz))
        twist = minus(along_y(zd_yz, False))
        half = 0.5 * zs_s + 0.125 * zs_z
        here = (
            zs_s
            + 0.5 * zs_z
            + plus(along_y(s + 0.5 * qyy + (PAIR * zs_s - 0.125 * zs_x), False))
            + 0.25 * twist
        )
        even = (
            s
            + 0.5 * qxx
            + half
            + 0.125 * zs_x
            + plus(along_y(0.5 * s + 0.125 * (qxx + qyy) + FULL * zs_s, False))
            + (1.0 / 12.0) * twist
        )
        odd = (
            minus(along_y(0.25 * qxy + (1.0 / 12.0) * zs_xy, False))
            + 0.25 * zd_xz
            + plus(along_y((1.0 / 12.0) * zd_xz, False))
        )
        return here, even + odd, even - odd

    partial = None
    trail = None
    for i in range(cells + 2):
        here, ahead, behind = square_parts([squares_b[n, i] for n in range(6)])
        if i >= 2:
            j = i - 2
            q = [squares_b[n, i - 1] for n in range(6)]
            d = j + EDGE
            held = main_b[0, j] * q[0] + main_b[1, j] * q[1] + main_b[2, j] * q[2]
            mixed = shear_b[0, d] * q[3] + shear_b[1, d] * q[4] + shear_b[2, d] * q[5]
            rest = partial + ahead - 2.0 * gathered[j]
            total = held + 2.0 * mixed + root_b[d + 1] * rest
            total = total * factor_b[j]
            for t in range(fold_b):
                result_n[j, pl.ds(t, SUB, stride=fold_b), :] = total[t]
        if i >= 1:
            partial = here + trail
        trail = behind
    sensitivity_ref[...] = result_n[:, HALO : HALO + band, :]


def on_vmem():
    return pl.BlockSpec(memory_space=pltpu.VMEM)


def on_smem():
    return pl.BlockSpec(memory_space=pltpu.SMEM)


def settings(band, depth, supports, load_x, load_y, load_vectors):
    vectors = load_vectors.transpose(1, 0, 2)
    return pl.pallas_call(
        settings_kernel,
        out_shape=pltpu.VMEM((1, band, depth), jnp.float32),
        in_specs=[pl.BlockSpec(memory_space=pltpu.HBM)] * 2 + [on_smem()] * 2,
        out_specs=on_vmem(),
        scratch_shapes=[
            pltpu.SMEM(supports.shape, jnp.int32),
            pltpu.SMEM(vectors.shape, jnp.float32),
            pltpu.SemaphoreType.DMA((2,)),
        ],
    )(
        *(pltpu.with_memory_space_constraint(array, pltpu.HBM) for array in (supports, vectors)),
        load_x,
        load_y,
    )


def relaxed(bands):
    groups, planes, band, depth = bands.shape
    wide = planes - 1
    cells = wide - 2 * HALO
    rows = groups * band
    fold = rows // SUB
    fold_b = -(-(band + 2 * HALO) // SUB)
    tall = PAD + rows + fold_b * SUB

    def area(*lead):
        return pltpu.VMEM((*lead, fold, SUB, depth), jnp.float32)

    def window(*lead):
        return pltpu.VMEM((*lead, fold_b, SUB, depth), jnp.float32)

    return pl.pallas_call(
        relax_kernel,
        out_shape=(
            jax.ShapeDtypeStruct((3, cells, rows, depth), jnp.float32),
            jax.ShapeDtypeStruct((cells, band, depth), jnp.float32),
        ),
        in_specs=[on_vmem()],
        out_specs=(on_vmem(), on_vmem()),
        scratch_shapes=[
            pltpu.VMEM((wide, tall, depth), jnp.float32),
            pltpu.VMEM((3, cells + 2, tall, depth), jnp.float32),
            pltpu.VMEM((cells, fold_b * SUB, depth), jnp.float32),
            area(wide),
            area(wide - 2),
            area(3, wide - 2),
            area(3, wide - 2),
            area(3, wide - 2),
            area(3, wide - 2),
            window(wide),
            window(wide - 2),
            window(3, wide - 2),
            window(3, wide - 2),
            window(3, wide - 2),
            window(3, wide - 4),
            window(3, cells),
            window(cells),
            window(3, cells + 2),
            window(6, cells + 2),
            window(wide - 2 + cells),
        ],
        compiler_params=pltpu.CompilerParams(vmem_limit_bytes=32 * 1024 * 1024),
    )(bands)


def shards(density, void_depth, supports, load_x, load_y, load_vectors):
    cells, band, depth = density.shape
    groups = lax.axis_size("case")
    slabs = lax.axis_size("space")
    level = lax.broadcasted_iota(jnp.int32, density.shape, 2) - depth // 2
    hollow = (level >= 0) & (level < void_depth[:, :, None])
    solid = jnp.where(hollow, 0.0, density)
    across = [(i, i + 1) for i in range(1, slabs - 1, 2)]
    across += [(j, i) for i, j in across]
    inside = [(i, i + 1) for i in range(0, slabs, 2)]
    inside += [(j, i) for i, j in inside]
    first = lax.rem(lax.axis_index("space"), CORES) == 0
    low = solid[:HALO]
    high = solid[cells - HALO :]
    outer = lax.ppermute(jnp.where(first, low, high), "space", across)
    inner = lax.ppermute(jnp.where(first, high, low), "space", inside)
    row = settings(band, depth, supports, load_x, load_y, load_vectors)
    before = jnp.where(first, outer, inner)
    after = jnp.where(first, inner, outer)
    mine = jnp.concatenate([before, solid, after, row])
    mine = jnp.broadcast_to(mine[None], (groups, *mine.shape))
    bands = lax.all_to_all(mine, "case", split_axis=0, concat_axis=0, tiled=True)
    field, sensitivity = relaxed(bands)
    return (field[None], sensitivity)


def solution(mesh):
    return jax.shard_map(
        shards,
        mesh=mesh,
        in_specs=(
            P("space", "case", None),
            P("space", "case"),
            P("case", None),
            P("case"),
            P("case"),
            P("case", None, None),
        ),
        out_specs=(P("case", None, "space", None, None), P("space", "case", None)),
        check_vma=False,
    )
```

```python
import math

import jax
import jax.numpy as jnp
from jax import lax
from jax.experimental import pallas as pl
from jax.experimental.pallas import tpu as pltpu
from jax.sharding import PartitionSpec as P

SWEEPS = 3
LOADW = 8
EMIN = 0.001
LOWER = 0.06
UPPER = 3.0
PATCH = 4.0
SUB = 8
CORES = 2
HALO = SWEEPS + 1
EDGE = HALO - 1
PAD = 8

AXIAL = 1.5
PAIR = 0.625
FLAT = 0.5
FULL = 0.25 * (1.0 + 0.5 / 3.0)
CROSS2 = 0.125
CROSS3 = 0.125 / 3.0


def relaxations(count):
    middle = 0.5 * (UPPER + LOWER)
    radius = 0.5 * (UPPER - LOWER)
    return [
        1.0 / (middle + radius * math.cos(math.pi * (2 * index + 1) / (2 * count)))
        for index in range(count)
    ]


def both(pair):
    return pair[0] + pair[1], pair[0] - pair[1]


def plus(pair):
    return pair[0] + pair[1]


def minus(pair):
    return pair[0] - pair[1]


def span_of(cells):
    return cells + 2 * EDGE


def solid_kernel(
    density_in, void_in, solid_ref, outer_ref, inner_ref, density_ref, void_ref, arrived
):
    fetches = [
        pltpu.make_async_copy(void_in, void_ref, arrived.at[0]),
        pltpu.make_async_copy(density_in, density_ref, arrived.at[1]),
    ]
    for fetch in fetches:
        fetch.start()
    cells, band, depth = solid_ref.shape
    first = lax.rem(lax.axis_index("space"), CORES) == 0
    level = lax.broadcasted_iota(jnp.int32, (band, depth), 1) - depth // 2
    eye = lax.broadcasted_iota(jnp.int32, (band, band), 0) == lax.broadcasted_iota(
        jnp.int32, (band, band), 1
    )
    for fetch in fetches:
        fetch.wait()
    for i in range(cells):
        line = jnp.broadcast_to(void_ref[i : i + 1, :], (band, band)).astype(jnp.float32)
        column = jnp.sum(jnp.where(eye, line, 0.0), axis=1, keepdims=True)
        top = jnp.broadcast_to(column, (band, depth)).astype(jnp.int32)
        hollow = (level >= 0) & (level < top)
        solid_ref[i] = jnp.where(hollow, 0.0, density_ref[i])
    for i in range(HALO):
        low = solid_ref[i]
        high = solid_ref[cells - HALO + i]
        outer_ref[i] = jnp.where(first, low, high)
        inner_ref[i] = jnp.where(first, high, low)


def settings_kernel(
    supports_in, vectors_in, load_x_ref, load_y_ref, row_ref, supports_ref, vectors_ref, arrived
):
    fetches = [
        pltpu.make_async_copy(supports_in, supports_ref, arrived.at[0]),
        pltpu.make_async_copy(vectors_in, vectors_ref, arrived.at[1]),
    ]
    for fetch in fetches:
        fetch.start()
    for fetch in fetches:
        fetch.wait()
    slabs = lax.axis_size("space")
    band, depth = row_ref.shape[1:]
    total_x = vectors_ref.shape[2]
    cells = total_x // slabs
    span = span_of(cells)
    first = lax.axis_index("space") * cells - EDGE
    lane = lax.broadcasted_iota(jnp.int32, (1, depth), 1)
    row = jnp.where(lane == 5 * span, load_y_ref[0].astype(jnp.float32), 0.0)
    for m in range(span):
        place = first + m
        inside = jnp.logical_and(place >= 0, place < total_x)
        where = jnp.clip(place, 0, total_x - 1)
        for k in range(3):
            value = jnp.where(inside, vectors_ref[k, 0, where], 0.0)
            row = jnp.where(lane == k * span + m, value, row)
    place = first + lane - 3 * span
    pinned = (place < supports_ref[0, 0]) | (place >= total_x - supports_ref[0, 1])
    row = jnp.where((lane >= 3 * span) & (lane < 4 * span) & pinned, 1.0, row)
    place = first + lane - 4 * span
    loaded = (place >= load_x_ref[0]) & (place < load_x_ref[0] + LOADW)
    row = jnp.where((lane >= 4 * span) & (lane < 5 * span) & loaded, 1.0, row)
    row_ref[0] = jnp.broadcast_to(row, (band, depth))


def relax_kernel(
    bands_ref,
    field_ref,
    sensitivity_ref,
    natural,
    third_n,
    result_n,
    root_a,
    drive_a,
    push_a,
    inverse_a,
    shear_a,
    first_a,
    root_b,
    drive_b,
    push_b,
    inverse_b,
    shear_b,
    first_b,
    main_b,
    factor_b,
    second_b,
    squares_b,
    work_b,
):
    groups, planes, band, depth = bands_ref.shape
    wide = planes - 1
    cells = wide - 2 * HALO
    span = span_of(cells)
    rows = groups * band
    case = lax.axis_index("case")
    total_x = lax.axis_size("space") * cells
    first_plane = lax.axis_index("space") * cells
    omegas = relaxations(SWEEPS)

    blank = jnp.zeros((PAD, depth), jnp.float32)
    for i in range(wide):
        natural[i, 0:PAD, :] = blank
        for at in range(PAD + rows, natural.shape[1], PAD):
            natural[i, at : at + PAD, :] = blank
    for k in range(3):
        for i in range(cells + 2):
            third_n[k, i, 0:PAD, :] = blank
            for at in range(PAD + rows, natural.shape[1], PAD):
                third_n[k, i, at : at + PAD, :] = blank
    for g in range(groups):
        natural[:, PAD + g * band : PAD + (g + 1) * band, :] = bands_ref[g, 0:wide]

    tile = (1, SUB, depth)
    lane = lax.broadcasted_iota(jnp.int32, tile, 2)
    line = lax.broadcasted_iota(jnp.int32, tile, 1)
    not_first_z = (lane > 0).astype(jnp.float32)
    not_last_z = (lane < depth - 1).astype(jnp.float32)
    not_first_s = (line > 0).astype(jnp.float32)
    not_last_s = (line < SUB - 1).astype(jnp.float32)
    at_bottom = (lane == 0).astype(jnp.float32)

    def along_z(a):
        after = pltpu.roll(a, depth - 1, 2) * not_last_z
        before = pltpu.roll(a, 1, 2) * not_first_z
        return after, before

    def along_y(a, closed):
        fold = a.shape[0]
        after = pltpu.roll(a[0:1], SUB - 1, 1)
        before = pltpu.roll(a[fold - 1 : fold], 1, 1)
        if closed:
            after = after * not_last_s
            before = before * not_first_s
        return (
            jnp.concatenate([a[1:], after], axis=0),
            jnp.concatenate([before, a[:-1]], axis=0),
        )

    def inside_of(plane, margin):
        place = first_plane - margin + plane
        return jnp.logical_and(place >= 0, place < total_x).astype(jnp.float32)

    def lines_of(fold):
        shape = (fold, SUB, depth)
        return fold * lax.broadcasted_iota(jnp.int32, shape, 1) + lax.broadcasted_iota(
            jnp.int32, shape, 0
        )

    def case_values(which):
        plain = jnp.broadcast_to(bands_ref[which, wide, 0:1, :], (SUB, depth))

        def value(kind, j):
            at = kind * span + j
            return jnp.broadcast_to(plain[:, at : at + 1], (SUB, depth))[None]

        corner = jnp.broadcast_to(plain[:, 5 * span : 5 * span + 1], (SUB, depth))[None]
        return value, corner

    def patch_of(y_of, corner):
        y = y_of.astype(jnp.float32)
        high = lax.broadcasted_iota(jnp.int32, y_of.shape, 2) == depth - 1
        return jnp.where(high & (y >= corner) & (y < corner + LOADW), PATCH, 0.0)

    def stiffness(fold, start, keep_rows, root_s, drive_s, inv_s, factor_s):
        for i in range(wide):
            solid = jnp.stack(
                [natural[i, pl.ds(start + t, SUB, stride=fold), :] for t in range(fold)]
            )
            stiff = EMIN + (1.0 - EMIN) * (solid * solid * solid)
            inv_root = lax.rsqrt(stiff)
            root = stiff * inv_root * inside_of(i, HALO)
            root_s[i] = root if keep_rows is None else root * keep_rows
            if 0 < i < wide - 1:
                drive_s[i - 1] = solid * inv_root
                inv_s[i - 1] = inv_root
            if factor_s is not None and HALO <= i < HALO + cells:
                ratio = solid * inv_root
                factor_s[i - HALO] = ((-1.5 * (1.0 - EMIN)) / groups) * (ratio * ratio)

    def tensor_parts(r, closed):
        zs, zd = both(along_z(r))
        ys, yd = both(along_y(r, closed))
        yszs, ydzs = both(along_y(zs, closed))
        yszd, ydzd = both(along_y(zd, closed))
        cross = ys + zs
        corner = PAIR * yszs
        here = [
            cross + FLAT * yszs,
            cross + 0.5 * ys + corner,
            cross + 0.5 * zs + corner,
            CROSS2 * ydzd,
        ]
        base = FULL * yszs + 0.5 * cross + r
        even = [
            base + 0.5 * r + 0.125 * cross,
            base + 0.125 * ys,
            base + 0.125 * zs,
            CROSS3 * ydzd,
        ]
        odd = [CROSS2 * yd + CROSS3 * ydzs, CROSS2 * zd + CROSS3 * yszd]
        return here, even, odd

    def tensor(closed, keep_rows, root_s, shear_s, inverse_s, main_s):
        older = None
        newer = None
        for i in range(wide):
            latest = tensor_parts(root_s[i], closed)
            if i >= 2:
                j = i - 2
                keep = inside_of(j, EDGE)
                if keep_rows is not None:
                    keep = keep * keep_rows
                total = [newer[0][k] + (latest[1][k] + older[1][k]) for k in range(4)]
                shear_s[0, j] = latest[2][0] - older[2][0]
                shear_s[1, j] = latest[2][1] - older[2][1]
                shear_s[2, j] = total[3]
                for k in range(3):
                    if main_s is not None and EDGE <= j < EDGE + cells:
                        main_s[k, j - EDGE] = total[k]
                    inverse_s[k, j] = keep / (total[k] + (1.0 - keep))
            older, newer = newer, latest

    def pushes(which, y_of, drive_s, inv_s, inverse_s, push_s):
        value, corner = case_values(which)
        patch = patch_of(y_of, corner)
        for j in range(wide - 2):
            free = 1.0 - value(3, j) * at_bottom
            push = (drive_s[j] + (value(4, j) * patch) * inv_s[j]) * free
            for k in range(3):
                push_s[k, j] = push * inverse_s[k, j] * value(k, j)
        return value

    def field_parts(w, closed):
        pair = [both(along_z(w[k])) for k in range(3)]
        zs = [pair[k][0] for k in range(3)]
        zd = [pair[k][1] for k in range(3)]
        ysx, ydx = both(along_y(w[0], closed))
        ysy, ydy = both(along_y(w[1], closed))
        ysz = plus(along_y(w[2], closed))
        yszsx, ydzsx = both(along_y(zs[0], closed))
        yszsy, ydzsy = both(along_y(zs[1], closed))
        yszsz = plus(along_y(zs[2], closed))
        yszdx = plus(along_y(zd[0], closed))
        ydzdy = minus(along_y(zd[1], closed))
        yszdz, ydzdz = both(along_y(zd[2], closed))
        here = [
            ysx + FLAT * yszsx + zs[0],
            AXIAL * ysy + PAIR * yszsy + zs[1] + CROSS2 * ydzdz,
            ysz + PAIR * yszsz + AXIAL * zs[2] + CROSS2 * ydzdy,
        ]
        even = [
            AXIAL * w[0] + PAIR * (zs[0] + ysx) + FULL * yszsx,
            w[1] + FLAT * zs[1] + PAIR * ysy + FULL * yszsy + CROSS3 * ydzdz,
            w[2] + PAIR * zs[2] + FLAT * ysz + FULL * yszsz + CROSS3 * ydzdy,
        ]
        odd = [
            CROSS2 * (ydy + zd[2]) + CROSS3 * (ydzsy + yszdz),
            CROSS2 * ydx + CROSS3 * ydzsx,
            CROSS2 * zd[0] + CROSS3 * yszdx,
        ]
        ahead = [even[k] + odd[k] for k in range(3)]
        behind = [even[k] - odd[k] for k in range(3)]
        return here, ahead, behind

    def sweep(closed, count, load, omega, value, store, root_s, push_s, inverse_s, shear_s):
        offset = (wide - count) // 2
        partial = None
        trail = None
        for i in range(count):
            r = root_s[i + offset]
            here, ahead, behind = field_parts([r * load(k, i) for k in range(3)], closed)
            if i >= 2:
                j = i - 1
                d = j + offset - 1
                free = 1.0 - value(3, d) * at_bottom
                old = [load(k, j) for k in range(3)]
                shear = [shear_s[k, d] for k in range(3)]
                rest = [
                    shear[0] * old[1] + shear[1] * old[2],
                    shear[0] * old[0] + shear[2] * old[2],
                    shear[1] * old[0] + shear[2] * old[1],
                ]
                for k in range(3):
                    pull = (partial[k] + ahead[k] - rest[k]) * (inverse_s[k, d] * free)
                    store(k, j - 1, (1.0 - omega) * old[k] + omega * (push_s[k, d] + pull))
            if i >= 1:
                partial = [here[k] + trail[k] for k in range(3)]
            trail = behind

    fold = rows // SUB
    inv_a = first_a.at[0]
    stiffness(fold, PAD, None, root_a, drive_a, inv_a, None)
    tensor(True, None, root_a, shear_a, inverse_a, None)
    value = pushes(case, lines_of(fold), drive_a, inv_a, inverse_a, push_a)

    def store_first_a(k, i, new):
        first_a[k, i] = new

    def store_third_a(k, i, new):
        for t in range(fold):
            third_n[k, i, pl.ds(PAD + t, SUB, stride=fold), :] = new[t]
            if 1 <= i <= cells:
                field_ref[k, i - 1, pl.ds(t, SUB, stride=fold), :] = new[t]

    arrays = (root_a, push_a, inverse_a, shear_a)
    sweep(
        True, wide - 2, lambda k, i: omegas[0] * push_a[k, i], omegas[1], value, store_first_a, *arrays
    )
    sweep(True, wide - 4, lambda k, i: first_a[k, i], omegas[2], value, store_third_a, *arrays)

    fold_b = result_n.shape[1] // SUB
    top = case * band - HALO
    y_of = top + lines_of(fold_b)
    keep_rows = ((y_of >= 0) & (y_of < rows)).astype(jnp.float32)
    inv_b = work_b.at[pl.ds(0, wide - 2)]
    stiffness(fold_b, PAD + top, keep_rows, root_b, drive_b, inv_b, factor_b)
    tensor(False, keep_rows, root_b, shear_b, inverse_b, main_b)
    gathered = work_b.at[pl.ds(wide - 2, cells)]
    empty = jnp.zeros((fold_b, SUB, depth), jnp.float32)
    for i in range(cells + 2):
        for n in range(6):
            squares_b[n, i] = empty
    for i in range(cells):
        gathered[i] = empty

    def store_first_b(k, i, new):
        first_b[k, i] = new

    def store_second_b(k, i, new):
        second_b[k, i] = new

    @pl.loop(0, groups)
    def add_case(other):
        @pl.when(other == 0)
        def take_own():
            for k in range(3):
                for i in range(cells + 2):
                    second_b[k, i] = jnp.stack(
                        [
                            third_n[k, i, pl.ds(PAD + top + t, SUB, stride=fold_b), :]
                            for t in range(fold_b)
                        ]
                    )

        @pl.when(other > 0)
        def relax_other():
            which = lax.rem(case + other, groups)
            value = pushes(which, y_of, drive_b, inv_b, inverse_b, push_b)
            arrays = (root_b, push_b, inverse_b, shear_b)
            sweep(
                False,
                wide - 2,
                lambda k, i: omegas[0] * push_b[k, i],
                omegas[1],
                value,
                store_first_b,
                *arrays,
            )
            sweep(
                False, wide - 4, lambda k, i: first_b[k, i], omegas[2], value, store_second_b, *arrays
            )

        partial = None
        trail = None
        for i in range(cells + 2):
            r = root_b[i + EDGE]
            v = [second_b[k, i] for k in range(3)]
            w = [r * v[k] for k in range(3)]
            for n, (a, b) in enumerate(((0, 0), (1, 1), (2, 2), (0, 1), (0, 2), (1, 2))):
                squares_b[n, i] += w[a] * v[b]
            here, ahead, behind = field_parts(w, False)
            if i >= 2:
                old = [second_b[k, i - 1] for k in range(3)]
                dot = [old[k] * (partial[k] + ahead[k]) for k in range(3)]
                gathered[i - 2] += dot[0] + dot[1] + dot[2]
            if i >= 1:
                partial = [here[k] + trail[k] for k in range(3)]
            trail = behind

    def square_parts(q):
        qxx, qyy, qzz, qxy, qxz, qyz = q
        s = qxx + qyy + qzz
        zs_s = plus(along_z(s))
        zs_x = plus(along_z(qxx))
        zs_z = plus(along_z(qzz))
        zs_xy = plus(along_z(qxy))
        zd_yz = minus(along_z(qyz))
        zd_xz = minus(along_z(qxz))
        twist = minus(along_y(zd_yz, False))
        half = 0.5 * zs_s + 0.125 * zs_z
        here = (
            zs_s
            + 0.5 * zs_z
            + plus(along_y(s + 0.5 * qyy + (PAIR * zs_s - 0.125 * zs_x), False))
            + 0.25 * twist
        )
        even = (
            s
            + 0.5 * qxx
            + half
            + 0.125 * zs_x
            + plus(along_y(0.5 * s + 0.125 * (qxx + qyy) + FULL * zs_s, False))
            + (1.0 / 12.0) * twist
        )
        odd = (
            minus(along_y(0.25 * qxy + (1.0 / 12.0) * zs_xy, False))
            + 0.25 * zd_xz
            + plus(along_y((1.0 / 12.0) * zd_xz, False))
        )
        return here, even + odd, even - odd

    partial = None
    trail = None
    for i in range(cells + 2):
        here, ahead, behind = square_parts([squares_b[n, i] for n in range(6)])
        if i >= 2:
            j = i - 2
            q = [squares_b[n, i - 1] for n in range(6)]
            d = j + EDGE
            held = main_b[0, j] * q[0] + main_b[1, j] * q[1] + main_b[2, j] * q[2]
            mixed = shear_b[0, d] * q[3] + shear_b[1, d] * q[4] + shear_b[2, d] * q[5]
            rest = partial + ahead - 2.0 * gathered[j]
            total = held + 2.0 * mixed + root_b[d + 1] * rest
            total = total * factor_b[j]
            for t in range(fold_b):
                result_n[j, pl.ds(t, SUB, stride=fold_b), :] = total[t]
        if i >= 1:
            partial = here + trail
        trail = behind
    sensitivity_ref[...] = result_n[:, HALO : HALO + band, :]


def on_vmem():
    return pl.BlockSpec(memory_space=pltpu.VMEM)


def on_smem():
    return pl.BlockSpec(memory_space=pltpu.SMEM)


def solids(density, void_depth):
    cells, band, depth = density.shape
    return pl.pallas_call(
        solid_kernel,
        out_shape=[
            pltpu.VMEM((planes, band, depth), jnp.float32) for planes in (cells, HALO, HALO)
        ],
        in_specs=[pl.BlockSpec(memory_space=pltpu.HBM)] * 2,
        out_specs=[on_vmem()] * 3,
        scratch_shapes=[
            pltpu.VMEM(density.shape, jnp.float32),
            pltpu.VMEM(void_depth.shape, jnp.int32),
            pltpu.SemaphoreType.DMA((2,)),
        ],
    )(*(pltpu.with_memory_space_constraint(array, pltpu.HBM) for array in (density, void_depth)))


def settings(band, depth, supports, load_x, load_y, load_vectors):
    vectors = load_vectors.transpose(1, 0, 2)
    return pl.pallas_call(
        settings_kernel,
        out_shape=pltpu.VMEM((1, band, depth), jnp.float32),
        in_specs=[pl.BlockSpec(memory_space=pltpu.HBM)] * 2 + [on_smem()] * 2,
        out_specs=on_vmem(),
        scratch_shapes=[
            pltpu.SMEM(supports.shape, jnp.int32),
            pltpu.SMEM(vectors.shape, jnp.float32),
            pltpu.SemaphoreType.DMA((2,)),
        ],
    )(
        *(pltpu.with_memory_space_constraint(array, pltpu.HBM) for array in (supports, vectors)),
        load_x,
        load_y,
    )


def relaxed(bands):
    groups, planes, band, depth = bands.shape
    wide = planes - 1
    cells = wide - 2 * HALO
    rows = groups * band
    fold = rows // SUB
    fold_b = -(-(band + 2 * HALO) // SUB)
    tall = PAD + rows + fold_b * SUB

    def area(*lead):
        return pltpu.VMEM((*lead, fold, SUB, depth), jnp.float32)

    def window(*lead):
        return pltpu.VMEM((*lead, fold_b, SUB, depth), jnp.float32)

    return pl.pallas_call(
        relax_kernel,
        out_shape=(
            jax.ShapeDtypeStruct((3, cells, rows, depth), jnp.float32),
            jax.ShapeDtypeStruct((cells, band, depth), jnp.float32),
        ),
        in_specs=[on_vmem()],
        out_specs=(on_vmem(), on_vmem()),
        scratch_shapes=[
            pltpu.VMEM((wide, tall, depth), jnp.float32),
            pltpu.VMEM((3, cells + 2, tall, depth), jnp.float32),
            pltpu.VMEM((cells, fold_b * SUB, depth), jnp.float32),
            area(wide),
            area(wide - 2),
            area(3, wide - 2),
            area(3, wide - 2),
            area(3, wide - 2),
            area(3, wide - 2),
            window(wide),
            window(wide - 2),
            window(3, wide - 2),
            window(3, wide - 2),
            window(3, wide - 2),
            window(3, wide - 4),
            window(3, cells),
            window(cells),
            window(3, cells + 2),
            window(6, cells + 2),
            window(wide - 2 + cells),
        ],
        compiler_params=pltpu.CompilerParams(vmem_limit_bytes=32 * 1024 * 1024),
    )(bands)


def shards(density, void_depth, supports, load_x, load_y, load_vectors):
    cells, band, depth = density.shape
    groups = lax.axis_size("case")
    slabs = lax.axis_size("space")
    solid, far, near = solids(density, void_depth)
    across = [(i, i + 1) for i in range(1, slabs - 1, 2)]
    across += [(j, i) for i, j in across]
    inside = [(i, i + 1) for i in range(0, slabs, 2)]
    inside += [(j, i) for i, j in inside]
    first = lax.rem(lax.axis_index("space"), CORES) == 0
    outer = lax.ppermute(far, "space", across)
    inner = lax.ppermute(near, "space", inside)
    row = settings(band, depth, supports, load_x, load_y, load_vectors)
    before = jnp.where(first, outer, inner)
    after = jnp.where(first, inner, outer)
    mine = jnp.concatenate([before, solid, after, row])
    mine = jnp.broadcast_to(mine[None], (groups, *mine.shape))
    bands = lax.all_to_all(mine, "case", split_axis=0, concat_axis=0, tiled=True)
    field, sensitivity = relaxed(bands)
    return (field[None], sensitivity)


def solution(mesh):
    return jax.shard_map(
        shards,
        mesh=mesh,
        in_specs=(
            P("space", "case", None),
            P("space", "case"),
            P("case", None),
            P("case"),
            P("case"),
            P("case", None, None),
        ),
        out_specs=(P("case", None, "space", None, None), P("space", "case", None)),
        check_vma=False,
    )
```

```python
import math

import jax
import jax.numpy as jnp
from jax import lax
from jax.experimental import pallas as pl
from jax.experimental.pallas import tpu as pltpu
from jax.sharding import PartitionSpec as P

SWEEPS = 3
LOADW = 8
EMIN = 0.001
LOWER = 0.06
UPPER = 3.0
PATCH = 4.0
SUB = 8
CORES = 2
HALO = SWEEPS + 1
EDGE = HALO - 1
PAD = 8

AXIAL = 1.5
PAIR = 0.625
FLAT = 0.5
FULL = 0.25 * (1.0 + 0.5 / 3.0)
CROSS2 = 0.125
CROSS3 = 0.125 / 3.0


def relaxations(count):
    middle = 0.5 * (UPPER + LOWER)
    radius = 0.5 * (UPPER - LOWER)
    return [
        1.0 / (middle + radius * math.cos(math.pi * (2 * index + 1) / (2 * count)))
        for index in range(count)
    ]


def both(pair):
    return pair[0] + pair[1], pair[0] - pair[1]


def plus(pair):
    return pair[0] + pair[1]


def minus(pair):
    return pair[0] - pair[1]


def span_of(cells):
    return cells + 2 * EDGE


def solid_kernel(
    density_in, void_in, solid_ref, outer_ref, inner_ref, density_ref, void_ref, arrived
):
    fetches = [
        pltpu.make_async_copy(void_in, void_ref, arrived.at[0]),
        pltpu.make_async_copy(density_in, density_ref, arrived.at[1]),
    ]
    for fetch in fetches:
        fetch.start()
    cells, band, depth = solid_ref.shape
    first = lax.rem(lax.axis_index("space"), CORES) == 0
    level = lax.broadcasted_iota(jnp.int32, (band, depth), 1) - depth // 2
    eye = lax.broadcasted_iota(jnp.int32, (band, band), 0) == lax.broadcasted_iota(
        jnp.int32, (band, band), 1
    )
    for fetch in fetches:
        fetch.wait()
    for i in range(cells):
        line = jnp.broadcast_to(void_ref[i : i + 1, :], (band, band)).astype(jnp.float32)
        column = jnp.sum(jnp.where(eye, line, 0.0), axis=1, keepdims=True)
        top = jnp.broadcast_to(column, (band, depth)).astype(jnp.int32)
        hollow = (level >= 0) & (level < top)
        solid_ref[i] = jnp.where(hollow, 0.0, density_ref[i])
    for i in range(HALO):
        low = solid_ref[i]
        high = solid_ref[cells - HALO + i]
        outer_ref[i] = jnp.where(first, low, high)
        inner_ref[i] = jnp.where(first, high, low)


def settings_kernel(
    supports_in, vectors_in, load_x_ref, load_y_ref, row_ref, supports_ref, vectors_ref, arrived
):
    fetches = [
        pltpu.make_async_copy(supports_in, supports_ref, arrived.at[0]),
        pltpu.make_async_copy(vectors_in, vectors_ref, arrived.at[1]),
    ]
    for fetch in fetches:
        fetch.start()
    for fetch in fetches:
        fetch.wait()
    slabs = lax.axis_size("space")
    band, depth = row_ref.shape[1:]
    total_x = vectors_ref.shape[2]
    cells = total_x // slabs
    span = span_of(cells)
    first = lax.axis_index("space") * cells - EDGE
    lane = lax.broadcasted_iota(jnp.int32, (1, depth), 1)
    row = jnp.where(lane == 5 * span, load_y_ref[0].astype(jnp.float32), 0.0)
    for m in range(span):
        place = first + m
        inside = jnp.logical_and(place >= 0, place < total_x)
        where = jnp.clip(place, 0, total_x - 1)
        for k in range(3):
            value = jnp.where(inside, vectors_ref[k, 0, where], 0.0)
            row = jnp.where(lane == k * span + m, value, row)
    place = first + lane - 3 * span
    pinned = (place < supports_ref[0, 0]) | (place >= total_x - supports_ref[0, 1])
    row = jnp.where((lane >= 3 * span) & (lane < 4 * span) & pinned, 1.0, row)
    place = first + lane - 4 * span
    loaded = (place >= load_x_ref[0]) & (place < load_x_ref[0] + LOADW)
    row = jnp.where((lane >= 4 * span) & (lane < 5 * span) & loaded, 1.0, row)
    row_ref[0] = jnp.broadcast_to(row, (band, depth))


def relax_kernel(
    bands_ref,
    field_ref,
    sensitivity_ref,
    natural,
    third_n,
    result_n,
    root_a,
    drive_a,
    push_a,
    inverse_a,
    shear_a,
    first_a,
    root_b,
    drive_b,
    push_b,
    inverse_b,
    shear_b,
    first_b,
    main_b,
    factor_b,
    second_b,
    squares_b,
    work_b,
    field_v,
    gone,
):
    groups, planes, band, depth = bands_ref.shape
    wide = planes - 1
    cells = wide - 2 * HALO
    span = span_of(cells)
    rows = groups * band
    case = lax.axis_index("case")
    total_x = lax.axis_size("space") * cells
    first_plane = lax.axis_index("space") * cells
    omegas = relaxations(SWEEPS)
    scale = omegas[0] * omegas[1] * omegas[2]

    blank = jnp.zeros((PAD, depth), jnp.float32)
    for i in range(wide):
        natural[i, 0:PAD, :] = blank
        for at in range(PAD + rows, natural.shape[1], PAD):
            natural[i, at : at + PAD, :] = blank
    for k in range(3):
        for i in range(cells + 2):
            third_n[k, i, 0:PAD, :] = blank
            for at in range(PAD + rows, natural.shape[1], PAD):
                third_n[k, i, at : at + PAD, :] = blank
    for g in range(groups):
        natural[:, PAD + g * band : PAD + (g + 1) * band, :] = bands_ref[g, 0:wide]

    tile = (1, SUB, depth)
    lane = lax.broadcasted_iota(jnp.int32, tile, 2)
    line = lax.broadcasted_iota(jnp.int32, tile, 1)
    not_first_z = (lane > 0).astype(jnp.float32)
    not_last_z = (lane < depth - 1).astype(jnp.float32)
    not_first_s = (line > 0).astype(jnp.float32)
    not_last_s = (line < SUB - 1).astype(jnp.float32)
    at_bottom = (lane == 0).astype(jnp.float32)
    half_first_z = 0.5 * not_first_z
    half_last_z = 0.5 * not_last_z

    def along_z(a):
        after = pltpu.roll(a, depth - 1, 2) * not_last_z
        before = pltpu.roll(a, 1, 2) * not_first_z
        return after, before

    def along_y(a, closed):
        fold = a.shape[0]
        after = pltpu.roll(a[0:1], SUB - 1, 1)
        before = pltpu.roll(a[fold - 1 : fold], 1, 1)
        if closed:
            after = after * not_last_s
            before = before * not_first_s
        return (
            jnp.concatenate([a[1:], after], axis=0),
            jnp.concatenate([before, a[:-1]], axis=0),
        )

    def inside_of(plane, margin):
        place = first_plane - margin + plane
        return jnp.logical_and(place >= 0, place < total_x).astype(jnp.float32)

    def lines_of(fold):
        shape = (fold, SUB, depth)
        return fold * lax.broadcasted_iota(jnp.int32, shape, 1) + lax.broadcasted_iota(
            jnp.int32, shape, 0
        )

    def case_values(which):
        plain = jnp.broadcast_to(bands_ref[which, wide, 0:1, :], (SUB, depth))

        def value(kind, j):
            at = kind * span + j
            return jnp.broadcast_to(plain[:, at : at + 1], (SUB, depth))[None]

        corner = jnp.broadcast_to(plain[:, 5 * span : 5 * span + 1], (SUB, depth))[None]
        return value, corner

    def patch_of(y_of, corner):
        y = y_of.astype(jnp.float32)
        high = lax.broadcasted_iota(jnp.int32, y_of.shape, 2) == depth - 1
        return jnp.where(high & (y >= corner) & (y < corner + LOADW), PATCH, 0.0)

    def stiffness(fold, start, keep_rows, root_s, drive_s, inv_s, factor_s):
        for i in range(wide):
            solid = jnp.stack(
                [natural[i, pl.ds(start + t, SUB, stride=fold), :] for t in range(fold)]
            )
            stiff = EMIN + (1.0 - EMIN) * (solid * solid * solid)
            inv_root = lax.rsqrt(stiff)
            root = stiff * inv_root * inside_of(i, HALO)
            root_s[i] = root if keep_rows is None else root * keep_rows
            if 0 < i < wide - 1:
                drive_s[i - 1] = solid * inv_root
                inv_s[i - 1] = inv_root
            if factor_s is not None and HALO <= i < HALO + cells:
                ratio = solid * inv_root
                factor_s[i - HALO] = ((-1.5 * (1.0 - EMIN)) * scale * scale / groups) * (ratio * ratio)

    def tensor_parts(r, closed):
        zs, zd = both(along_z(r))
        ys, yd = both(along_y(r, closed))
        yszs, ydzs = both(along_y(zs, closed))
        yszd, ydzd = both(along_y(zd, closed))
        cross = ys + zs
        corner = PAIR * yszs
        here = [
            cross + FLAT * yszs,
            cross + 0.5 * ys + corner,
            cross + 0.5 * zs + corner,
            CROSS2 * ydzd,
        ]
        base = FULL * yszs + 0.5 * cross + r
        even = [
            base + 0.5 * r + 0.125 * cross,
            base + 0.125 * ys,
            base + 0.125 * zs,
            CROSS3 * ydzd,
        ]
        odd = [CROSS2 * yd + CROSS3 * ydzs, CROSS2 * zd + CROSS3 * yszd]
        return here, even, odd

    def tensor(closed, keep_rows, root_s, shear_s, inverse_s, main_s):
        older = None
        newer = None
        for i in range(wide):
            latest = tensor_parts(root_s[i], closed)
            if i >= 2:
                j = i - 2
                keep = inside_of(j, EDGE)
                if keep_rows is not None:
                    keep = keep * keep_rows
                total = [newer[0][k] + (latest[1][k] + older[1][k]) for k in range(4)]
                shear_s[0, j] = latest[2][0] - older[2][0]
                shear_s[1, j] = latest[2][1] - older[2][1]
                shear_s[2, j] = total[3]
                for k in range(3):
                    if main_s is not None and EDGE <= j < EDGE + cells:
                        main_s[k, j - EDGE] = total[k]
                    inverse_s[k, j] = keep / (total[k] + (1.0 - keep))
            older, newer = newer, latest

    def pushes(which, y_of, drive_s, inv_s, inverse_s, push_s):
        value, corner = case_values(which)
        patch = patch_of(y_of, corner)
        for j in range(wide - 2):
            free = 1.0 - value(3, j) * at_bottom
            push = (drive_s[j] + (value(4, j) * patch) * inv_s[j]) * free
            for k in range(3):
                push_s[k, j] = push * inverse_s[k, j] * value(k, j)
        return value

    def field_parts(w, closed):
        zs, zd = [], []
        for k in range(3):
            after = pltpu.roll(w[k], depth - 1, 2) * half_last_z
            before = pltpu.roll(w[k], 1, 2) * half_first_z
            zs.append(after + before)
            zd.append(after - before)
        mean = [w[k] + zs[k] for k in range(2)]
        mixed = [CROSS2 * w[k] + (2.0 * CROSS3) * zs[k] for k in range(2)]
        even_y = [plus(along_y(0.5 * mean[k] + mixed[k], closed)) for k in range(2)]
        odd_y = [minus(along_y(mixed[k], closed)) for k in range(2)]
        strong = [(2.0 * PAIR) * mean[k] + (AXIAL - 2.0 * PAIR) * w[k] for k in range(2)]
        upright = w[2] + (2.0 * PAIR) * zs[2]
        flat = FLAT * w[2] + (2.0 * FULL) * zs[2]
        twist_y = minus(along_y(zd[1], closed))
        spread_z, twist_z = both(along_y(zd[2], closed))
        slope_x = (2.0 * CROSS2) * zd[0] + (2.0 * CROSS3) * plus(along_y(zd[0], closed))
        slope_z = (2.0 * CROSS2) * zd[2] + (2.0 * CROSS3) * spread_z
        here = [
            plus(along_y(mean[0], closed)) + (zs[0] + zs[0]),
            plus(along_y(strong[1], closed)) + (zs[1] + zs[1]) + (2.0 * CROSS2) * twist_z,
            plus(along_y(upright, closed)) + (2.0 * AXIAL) * zs[2] + (2.0 * CROSS2) * twist_y,
        ]
        even = [
            strong[0] + even_y[0],
            mean[1] + even_y[1] + (2.0 * CROSS3) * twist_z,
            upright + plus(along_y(flat, closed)) + (2.0 * CROSS3) * twist_y,
        ]
        odd = [odd_y[1] + slope_z, odd_y[0], slope_x]
        ahead = [even[k] + odd[k] for k in range(3)]
        behind = [even[k] - odd[k] for k in range(3)]
        return here, ahead, behind

    def sweep(closed, count, load, keep, drive, value, store, root_s, push_s, inverse_s, shear_s):
        offset = (wide - count) // 2
        partial = None
        trail = None
        free = None
        for i in range(count):
            held = free
            r = root_s[i + offset]
            if drive is not None:
                free = 1.0 - value(3, i + offset - 1) * at_bottom
                r = r * free
            here, ahead, behind = field_parts([r * load(k, i) for k in range(3)], closed)
            if i >= 2:
                j = i - 1
                d = j + offset - 1
                old = [load(k, j) for k in range(3)]
                shear = [shear_s[k, d] for k in range(3)]
                rest = [
                    shear[0] * old[1] + shear[1] * old[2],
                    shear[0] * old[0] + shear[2] * old[2],
                    shear[1] * old[0] + shear[2] * old[1],
                ]
                for k in range(3):
                    new = keep * old[k] + (partial[k] + ahead[k] - rest[k]) * inverse_s[k, d]
                    if drive is not None:
                        new = (new + drive * push_s[k, d]) * held
                    store(k, j - 1, new)
            if i >= 1:
                partial = [here[k] + trail[k] for k in range(3)]
            trail = behind

    keep_second = (1.0 - omegas[1]) / omegas[1] + 1.0 / omegas[0]
    keep_third = (1.0 - omegas[2]) / omegas[2]
    drive_third = 1.0 / (omegas[0] * omegas[1])

    fold = rows // SUB
    inv_a = first_a.at[0]
    stiffness(fold, PAD, None, root_a, drive_a, inv_a, None)
    tensor(True, None, root_a, shear_a, inverse_a, None)
    value = pushes(case, lines_of(fold), drive_a, inv_a, inverse_a, push_a)

    def store_first_a(k, i, new):
        first_a[k, i] = new

    def store_third_a(k, i, new):
        for t in range(fold):
            third_n[k, i, pl.ds(PAD + t, SUB, stride=fold), :] = new[t]
            if 1 <= i <= cells:
                field_v[k, i - 1, pl.ds(t, SUB, stride=fold), :] = scale * new[t]

    arrays = (root_a, push_a, inverse_a, shear_a)
    sweep(
        True, wide - 2, lambda k, i: push_a[k, i], keep_second, None, value, store_first_a, *arrays
    )
    sweep(
        True,
        wide - 4,
        lambda k, i: first_a[k, i],
        keep_third,
        drive_third,
        value,
        store_third_a,
        *arrays,
    )
    leaving = pltpu.make_async_copy(field_v, field_ref, gone.at[0])
    leaving.start()

    fold_b = result_n.shape[1] // SUB
    top = case * band - HALO
    y_of = top + lines_of(fold_b)
    keep_rows = ((y_of >= 0) & (y_of < rows)).astype(jnp.float32)
    inv_b = work_b.at[pl.ds(0, wide - 2)]
    stiffness(fold_b, PAD + top, keep_rows, root_b, drive_b, inv_b, factor_b)
    tensor(False, keep_rows, root_b, shear_b, inverse_b, main_b)
    gathered = work_b.at[pl.ds(wide - 2, cells)]
    empty = jnp.zeros((fold_b, SUB, depth), jnp.float32)
    for i in range(cells + 2):
        for n in range(6):
            squares_b[n, i] = empty
    for i in range(cells):
        gathered[i] = empty

    def store_first_b(k, i, new):
        first_b[k, i] = new

    def store_second_b(k, i, new):
        second_b[k, i] = new

    @pl.loop(0, groups)
    def add_case(other):
        @pl.when(other == 0)
        def take_own():
            for k in range(3):
                for i in range(cells + 2):
                    second_b[k, i] = jnp.stack(
                        [
                            third_n[k, i, pl.ds(PAD + top + t, SUB, stride=fold_b), :]
                            for t in range(fold_b)
                        ]
                    )

        @pl.when(other > 0)
        def relax_other():
            which = lax.rem(case + other, groups)
            value = pushes(which, y_of, drive_b, inv_b, inverse_b, push_b)
            arrays = (root_b, push_b, inverse_b, shear_b)
            sweep(
                False,
                wide - 2,
                lambda k, i: push_b[k, i],
                keep_second,
                None,
                value,
                store_first_b,
                *arrays,
            )
            sweep(
                False,
                wide - 4,
                lambda k, i: first_b[k, i],
                keep_third,
                drive_third,
                value,
                store_second_b,
                *arrays,
            )

        partial = None
        trail = None
        for i in range(cells + 2):
            r = root_b[i + EDGE]
            v = [second_b[k, i] for k in range(3)]
            w = [r * v[k] for k in range(3)]
            for n, (a, b) in enumerate(((0, 0), (1, 1), (2, 2), (0, 1), (0, 2), (1, 2))):
                squares_b[n, i] += w[a] * v[b]
            here, ahead, behind = field_parts(w, False)
            if i >= 2:
                old = [second_b[k, i - 1] for k in range(3)]
                dot = [old[k] * (partial[k] + ahead[k]) for k in range(3)]
                gathered[i - 2] += dot[0] + dot[1] + dot[2]
            if i >= 1:
                partial = [here[k] + trail[k] for k in range(3)]
            trail = behind

    def square_parts(q):
        qxx, qyy, qzz, qxy, qxz, qyz = q
        s = qxx + qyy + qzz
        zs_s = plus(along_z(s))
        zs_x = plus(along_z(qxx))
        zs_z = plus(along_z(qzz))
        zs_xy = plus(along_z(qxy))
        zd_yz = minus(along_z(qyz))
        zd_xz = minus(along_z(qxz))
        twist = minus(along_y(zd_yz, False))
        half = 0.5 * zs_s + 0.125 * zs_z
        here = (
            zs_s
            + 0.5 * zs_z
            + plus(along_y(s + 0.5 * qyy + (PAIR * zs_s - 0.125 * zs_x), False))
            + 0.25 * twist
        )
        even = (
            s
            + 0.5 * qxx
            + half
            + 0.125 * zs_x
            + plus(along_y(0.5 * s + 0.125 * (qxx + qyy) + FULL * zs_s, False))
            + (1.0 / 12.0) * twist
        )
        odd = (
            minus(along_y(0.25 * qxy + (1.0 / 12.0) * zs_xy, False))
            + 0.25 * zd_xz
            + plus(along_y((1.0 / 12.0) * zd_xz, False))
        )
        return here, even + odd, even - odd

    partial = None
    trail = None
    for i in range(cells + 2):
        here, ahead, behind = square_parts([squares_b[n, i] for n in range(6)])
        if i >= 2:
            j = i - 2
            q = [squares_b[n, i - 1] for n in range(6)]
            d = j + EDGE
            held = main_b[0, j] * q[0] + main_b[1, j] * q[1] + main_b[2, j] * q[2]
            mixed = shear_b[0, d] * q[3] + shear_b[1, d] * q[4] + shear_b[2, d] * q[5]
            rest = partial + ahead - 2.0 * gathered[j]
            total = held + 2.0 * mixed + root_b[d + 1] * rest
            total = total * factor_b[j]
            for t in range(fold_b):
                result_n[j, pl.ds(t, SUB, stride=fold_b), :] = total[t]
        if i >= 1:
            partial = here + trail
        trail = behind
    sensitivity_ref[...] = result_n[:, HALO : HALO + band, :]
    leaving.wait()


def on_vmem():
    return pl.BlockSpec(memory_space=pltpu.VMEM)


def on_smem():
    return pl.BlockSpec(memory_space=pltpu.SMEM)


def solids(density, void_depth):
    cells, band, depth = density.shape
    return pl.pallas_call(
        solid_kernel,
        out_shape=[
            pltpu.VMEM((planes, band, depth), jnp.float32) for planes in (cells, HALO, HALO)
        ],
        in_specs=[pl.BlockSpec(memory_space=pltpu.HBM)] * 2,
        out_specs=[on_vmem()] * 3,
        scratch_shapes=[
            pltpu.VMEM(density.shape, jnp.float32),
            pltpu.VMEM(void_depth.shape, jnp.int32),
            pltpu.SemaphoreType.DMA((2,)),
        ],
    )(*(pltpu.with_memory_space_constraint(array, pltpu.HBM) for array in (density, void_depth)))


def settings(band, depth, supports, load_x, load_y, load_vectors):
    vectors = load_vectors.transpose(1, 0, 2)
    return pl.pallas_call(
        settings_kernel,
        out_shape=pltpu.VMEM((1, band, depth), jnp.float32),
        in_specs=[pl.BlockSpec(memory_space=pltpu.HBM)] * 2 + [on_smem()] * 2,
        out_specs=on_vmem(),
        scratch_shapes=[
            pltpu.SMEM(supports.shape, jnp.int32),
            pltpu.SMEM(vectors.shape, jnp.float32),
            pltpu.SemaphoreType.DMA((2,)),
        ],
    )(
        *(pltpu.with_memory_space_constraint(array, pltpu.HBM) for array in (supports, vectors)),
        load_x,
        load_y,
    )


def relaxed(bands):
    groups, planes, band, depth = bands.shape
    wide = planes - 1
    cells = wide - 2 * HALO
    rows = groups * band
    fold = rows // SUB
    fold_b = -(-(band + 2 * HALO) // SUB)
    tall = PAD + rows + fold_b * SUB

    def area(*lead):
        return pltpu.VMEM((*lead, fold, SUB, depth), jnp.float32)

    def window(*lead):
        return pltpu.VMEM((*lead, fold_b, SUB, depth), jnp.float32)

    return pl.pallas_call(
        relax_kernel,
        out_shape=(
            jax.ShapeDtypeStruct((3, cells, rows, depth), jnp.float32),
            jax.ShapeDtypeStruct((cells, band, depth), jnp.float32),
        ),
        in_specs=[on_vmem()],
        out_specs=(pl.BlockSpec(memory_space=pltpu.HBM), on_vmem()),
        scratch_shapes=[
            pltpu.VMEM((wide, tall, depth), jnp.float32),
            pltpu.VMEM((3, cells + 2, tall, depth), jnp.float32),
            pltpu.VMEM((cells, fold_b * SUB, depth), jnp.float32),
            area(wide),
            area(wide - 2),
            area(3, wide - 2),
            area(3, wide - 2),
            area(3, wide - 2),
            area(3, wide - 2),
            window(wide),
            window(wide - 2),
            window(3, wide - 2),
            window(3, wide - 2),
            window(3, wide - 2),
            window(3, wide - 4),
            window(3, cells),
            window(cells),
            window(3, cells + 2),
            window(6, cells + 2),
            window(wide - 2 + cells),
            pltpu.VMEM((3, cells, rows, depth), jnp.float32),
            pltpu.SemaphoreType.DMA((1,)),
        ],
        compiler_params=pltpu.CompilerParams(vmem_limit_bytes=32 * 1024 * 1024),
    )(bands)


def shards(density, void_depth, supports, load_x, load_y, load_vectors):
    cells, band, depth = density.shape
    groups = lax.axis_size("case")
    slabs = lax.axis_size("space")
    solid, far, near = solids(density, void_depth)
    across = [(i, i + 1) for i in range(1, slabs - 1, 2)]
    across += [(j, i) for i, j in across]
    inside = [(i, i + 1) for i in range(0, slabs, 2)]
    inside += [(j, i) for i, j in inside]
    first = lax.rem(lax.axis_index("space"), CORES) == 0
    outer = lax.ppermute(far, "space", across)
    inner = lax.ppermute(near, "space", inside)
    row = settings(band, depth, supports, load_x, load_y, load_vectors)
    before = jnp.where(first, outer, inner)
    after = jnp.where(first, inner, outer)
    mine = jnp.concatenate([before, solid, after, row])
    mine = jnp.broadcast_to(mine[None], (groups, *mine.shape))
    bands = lax.all_to_all(mine, "case", split_axis=0, concat_axis=0, tiled=True)
    field, sensitivity = relaxed(bands)
    return (field[None], sensitivity)


def solution(mesh):
    return jax.shard_map(
        shards,
        mesh=mesh,
        in_specs=(
            P("space", "case", None),
            P("space", "case"),
            P("case", None),
            P("case"),
            P("case"),
            P("case", None, None),
        ),
        out_specs=(P("case", None, "space", None, None), P("space", "case", None)),
        check_vma=False,
    )
```

```python
import math

import jax
import jax.numpy as jnp
from jax import lax
from jax.experimental import pallas as pl
from jax.experimental.pallas import tpu as pltpu
from jax.sharding import PartitionSpec as P

SWEEPS = 3
LOADW = 8
EMIN = 0.001
LOWER = 0.06
UPPER = 3.0
PATCH = 4.0
SUB = 8
CORES = 2
HALO = SWEEPS + 1
EDGE = HALO - 1
PAD = 8

AXIAL = 1.5
PAIR = 0.625
FLAT = 0.5
FULL = 0.25 * (1.0 + 0.5 / 3.0)
CROSS2 = 0.125
CROSS3 = 0.125 / 3.0


def relaxations(count):
    middle = 0.5 * (UPPER + LOWER)
    radius = 0.5 * (UPPER - LOWER)
    return [
        1.0 / (middle + radius * math.cos(math.pi * (2 * index + 1) / (2 * count)))
        for index in range(count)
    ]


def both(pair):
    return pair[0] + pair[1], pair[0] - pair[1]


def plus(pair):
    return pair[0] + pair[1]


def minus(pair):
    return pair[0] - pair[1]


def span_of(cells):
    return cells + 2 * EDGE


def solid_kernel(
    density_in, void_in, solid_ref, outer_ref, inner_ref, density_ref, void_ref, arrived
):
    fetches = [
        pltpu.make_async_copy(void_in, void_ref, arrived.at[0]),
        pltpu.make_async_copy(density_in, density_ref, arrived.at[1]),
    ]
    for fetch in fetches:
        fetch.start()
    cells, band, depth = solid_ref.shape
    first = lax.rem(lax.axis_index("space"), CORES) == 0
    level = lax.broadcasted_iota(jnp.int32, (band, depth), 1) - depth // 2
    eye = lax.broadcasted_iota(jnp.int32, (band, band), 0) == lax.broadcasted_iota(
        jnp.int32, (band, band), 1
    )
    for fetch in fetches:
        fetch.wait()
    for i in range(cells):
        line = jnp.broadcast_to(void_ref[i : i + 1, :], (band, band)).astype(jnp.float32)
        column = jnp.sum(jnp.where(eye, line, 0.0), axis=1, keepdims=True)
        top = jnp.broadcast_to(column, (band, depth)).astype(jnp.int32)
        hollow = (level >= 0) & (level < top)
        solid_ref[i] = jnp.where(hollow, 0.0, density_ref[i])
    for i in range(HALO):
        low = solid_ref[i]
        high = solid_ref[cells - HALO + i]
        outer_ref[i] = jnp.where(first, low, high)
        inner_ref[i] = jnp.where(first, high, low)


def settings_kernel(
    supports_in, vectors_in, load_x_ref, load_y_ref, row_ref, supports_ref, vectors_ref, arrived
):
    fetches = [
        pltpu.make_async_copy(supports_in, supports_ref, arrived.at[0]),
        pltpu.make_async_copy(vectors_in, vectors_ref, arrived.at[1]),
    ]
    for fetch in fetches:
        fetch.start()
    for fetch in fetches:
        fetch.wait()
    slabs = lax.axis_size("space")
    band, depth = row_ref.shape[1:]
    total_x = vectors_ref.shape[2]
    cells = total_x // slabs
    span = span_of(cells)
    first = lax.axis_index("space") * cells - EDGE
    lane = lax.broadcasted_iota(jnp.int32, (1, depth), 1)
    row = jnp.where(lane == 5 * span, load_y_ref[0].astype(jnp.float32), 0.0)
    for m in range(span):
        place = first + m
        inside = jnp.logical_and(place >= 0, place < total_x)
        where = jnp.clip(place, 0, total_x - 1)
        for k in range(3):
            value = jnp.where(inside, vectors_ref[k, 0, where], 0.0)
            row = jnp.where(lane == k * span + m, value, row)
    place = first + lane - 3 * span
    pinned = (place < supports_ref[0, 0]) | (place >= total_x - supports_ref[0, 1])
    row = jnp.where((lane >= 3 * span) & (lane < 4 * span) & pinned, 1.0, row)
    place = first + lane - 4 * span
    loaded = (place >= load_x_ref[0]) & (place < load_x_ref[0] + LOADW)
    row = jnp.where((lane >= 4 * span) & (lane < 5 * span) & loaded, 1.0, row)
    row_ref[0] = jnp.broadcast_to(row, (band, depth))


def relax_kernel(
    bands_ref,
    field_ref,
    sensitivity_ref,
    natural,
    third_n,
    result_n,
    root_a,
    drive_a,
    push_a,
    inverse_a,
    shear_a,
    first_a,
    root_b,
    drive_b,
    push_b,
    inverse_b,
    shear_b,
    first_b,
    main_b,
    factor_b,
    second_b,
    squares_b,
    work_b,
    field_v,
    gone,
):
    groups, planes, band, depth = bands_ref.shape
    wide = planes - 1
    cells = wide - 2 * HALO
    span = span_of(cells)
    rows = groups * band
    case = lax.axis_index("case")
    total_x = lax.axis_size("space") * cells
    first_plane = lax.axis_index("space") * cells
    omegas = relaxations(SWEEPS)
    scale = omegas[0] * omegas[1] * omegas[2]

    blank = jnp.zeros((PAD, depth), jnp.float32)
    for i in range(wide):
        natural[i, 0:PAD, :] = blank
        for at in range(PAD + rows, natural.shape[1], PAD):
            natural[i, at : at + PAD, :] = blank
    for k in range(3):
        for i in range(cells + 2):
            third_n[k, i, 0:PAD, :] = blank
            for at in range(PAD + rows, natural.shape[1], PAD):
                third_n[k, i, at : at + PAD, :] = blank
    for g in range(groups):
        natural[:, PAD + g * band : PAD + (g + 1) * band, :] = bands_ref[g, 0:wide]

    tile = (1, SUB, depth)
    lane = lax.broadcasted_iota(jnp.int32, tile, 2)
    line = lax.broadcasted_iota(jnp.int32, tile, 1)
    not_first_z = (lane > 0).astype(jnp.float32)
    not_last_z = (lane < depth - 1).astype(jnp.float32)
    not_first_s = (line > 0).astype(jnp.float32)
    not_last_s = (line < SUB - 1).astype(jnp.float32)
    at_bottom = (lane == 0).astype(jnp.float32)
    half_first_z = 0.5 * not_first_z
    half_last_z = 0.5 * not_last_z

    def along_z(a):
        after = pltpu.roll(a, depth - 1, 2) * not_last_z
        before = pltpu.roll(a, 1, 2) * not_first_z
        return after, before

    def along_y(a, closed):
        fold = a.shape[0]
        after = pltpu.roll(a[0:1], SUB - 1, 1)
        before = pltpu.roll(a[fold - 1 : fold], 1, 1)
        if closed:
            after = after * not_last_s
            before = before * not_first_s
        return (
            jnp.concatenate([a[1:], after], axis=0),
            jnp.concatenate([before, a[:-1]], axis=0),
        )

    def inside_of(plane, margin):
        place = first_plane - margin + plane
        return jnp.logical_and(place >= 0, place < total_x).astype(jnp.float32)

    def lines_of(fold):
        shape = (fold, SUB, depth)
        return fold * lax.broadcasted_iota(jnp.int32, shape, 1) + lax.broadcasted_iota(
            jnp.int32, shape, 0
        )

    def case_values(which):
        plain = jnp.broadcast_to(bands_ref[which, wide, 0:1, :], (SUB, depth))

        def value(kind, j):
            at = kind * span + j
            return jnp.broadcast_to(plain[:, at : at + 1], (SUB, depth))[None]

        corner = jnp.broadcast_to(plain[:, 5 * span : 5 * span + 1], (SUB, depth))[None]
        return value, corner

    def patch_of(y_of, corner):
        y = y_of.astype(jnp.float32)
        high = lax.broadcasted_iota(jnp.int32, y_of.shape, 2) == depth - 1
        return jnp.where(high & (y >= corner) & (y < corner + LOADW), PATCH, 0.0)

    def stiffness(fold, start, keep_rows, root_s, drive_s, inv_s, factor_s):
        for i in range(wide):
            solid = jnp.stack(
                [natural[i, pl.ds(start + t, SUB, stride=fold), :] for t in range(fold)]
            )
            stiff = EMIN + (1.0 - EMIN) * (solid * solid * solid)
            inv_root = lax.rsqrt(stiff)
            root = stiff * inv_root * inside_of(i, HALO)
            root_s[i] = root if keep_rows is None else root * keep_rows
            if 0 < i < wide - 1:
                drive_s[i - 1] = solid * inv_root
                inv_s[i - 1] = inv_root
            if factor_s is not None and HALO <= i < HALO + cells:
                ratio = solid * inv_root
                factor_s[i - HALO] = ((-1.5 * (1.0 - EMIN)) * scale * scale / groups) * (ratio * ratio)

    def tensor_parts(r, closed):
        zs, zd = both(along_z(r))
        ys, yd = both(along_y(r, closed))
        yszs, ydzs = both(along_y(zs, closed))
        yszd, ydzd = both(along_y(zd, closed))
        cross = ys + zs
        corner = PAIR * yszs
        here = [
            cross + FLAT * yszs,
            cross + 0.5 * ys + corner,
            cross + 0.5 * zs + corner,
            CROSS2 * ydzd,
        ]
        base = FULL * yszs + 0.5 * cross + r
        even = [
            base + 0.5 * r + 0.125 * cross,
            base + 0.125 * ys,
            base + 0.125 * zs,
            CROSS3 * ydzd,
        ]
        odd = [CROSS2 * yd + CROSS3 * ydzs, CROSS2 * zd + CROSS3 * yszd]
        return here, even, odd

    def tensor(closed, keep_rows, root_s, shear_s, inverse_s, main_s):
        older = None
        newer = None
        for i in range(wide):
            latest = tensor_parts(root_s[i], closed)
            if i >= 2:
                j = i - 2
                keep = inside_of(j, EDGE)
                if keep_rows is not None:
                    keep = keep * keep_rows
                total = [newer[0][k] + (latest[1][k] + older[1][k]) for k in range(4)]
                shear_s[0, j] = latest[2][0] - older[2][0]
                shear_s[1, j] = latest[2][1] - older[2][1]
                shear_s[2, j] = total[3]
                for k in range(3):
                    if main_s is not None and EDGE <= j < EDGE + cells:
                        main_s[k, j - EDGE] = total[k]
                    inverse_s[k, j] = keep / (total[k] + (1.0 - keep))
            older, newer = newer, latest

    def pushes(which, y_of, drive_s, inv_s, inverse_s, push_s):
        value, corner = case_values(which)
        patch = patch_of(y_of, corner)
        for j in range(wide - 2):
            free = 1.0 - value(3, j) * at_bottom
            push = (drive_s[j] + (value(4, j) * patch) * inv_s[j]) * free
            for k in range(3):
                push_s[k, j] = push * inverse_s[k, j] * value(k, j)
        return value

    def field_parts(w, closed):
        zs, zd = [], []
        for k in range(3):
            after = pltpu.roll(w[k], depth - 1, 2) * half_last_z
            before = pltpu.roll(w[k], 1, 2) * half_first_z
            zs.append(after + before)
            zd.append(after - before)
        mean = [w[k] + zs[k] for k in range(2)]
        mixed = [CROSS2 * w[k] + (2.0 * CROSS3) * zs[k] for k in range(2)]
        even_y = [plus(along_y(0.5 * mean[k] + mixed[k], closed)) for k in range(2)]
        odd_y = [minus(along_y(mixed[k], closed)) for k in range(2)]
        strong = [(2.0 * PAIR) * mean[k] + (AXIAL - 2.0 * PAIR) * w[k] for k in range(2)]
        upright = w[2] + (2.0 * PAIR) * zs[2]
        flat = FLAT * w[2] + (2.0 * FULL) * zs[2]
        twist_y = minus(along_y(zd[1], closed))
        spread_z, twist_z = both(along_y(zd[2], closed))
        slope_x = (2.0 * CROSS2) * zd[0] + (2.0 * CROSS3) * plus(along_y(zd[0], closed))
        slope_z = (2.0 * CROSS2) * zd[2] + (2.0 * CROSS3) * spread_z
        here = [
            plus(along_y(mean[0], closed)) + (zs[0] + zs[0]),
            plus(along_y(strong[1], closed)) + (zs[1] + zs[1]) + (2.0 * CROSS2) * twist_z,
            plus(along_y(upright, closed)) + (2.0 * AXIAL) * zs[2] + (2.0 * CROSS2) * twist_y,
        ]
        even = [
            strong[0] + even_y[0],
            mean[1] + even_y[1] + (2.0 * CROSS3) * twist_z,
            upright + plus(along_y(flat, closed)) + (2.0 * CROSS3) * twist_y,
        ]
        odd = [odd_y[1] + slope_z, odd_y[0], slope_x]
        ahead = [even[k] + odd[k] for k in range(3)]
        behind = [even[k] - odd[k] for k in range(3)]
        return here, ahead, behind

    def window_parts(w):
        zs, zd = [], []
        for k in range(3):
            after = pltpu.roll(w[k], depth - 1, 2) * half_last_z
            before = pltpu.roll(w[k], 1, 2) * half_first_z
            zs.append(after + before)
            zd.append(after - before)
        mean = [w[k] + zs[k] for k in range(2)]
        mixed = [CROSS2 * w[k] + (2.0 * CROSS3) * zs[k] for k in range(2)]
        lift = [0.5 * mean[k] + mixed[k] for k in range(2)]
        strong = [(2.0 * PAIR) * mean[k] + (AXIAL - 2.0 * PAIR) * w[k] for k in range(2)]
        upright = w[2] + (2.0 * PAIR) * zs[2]
        flat = FLAT * w[2] + (2.0 * FULL) * zs[2]
        edge = [(2.0 * CROSS2) * zd[k] for k in range(3)]
        tip = [(2.0 * CROSS3) * zd[k] for k in range(3)]
        here = [
            (zs[0] + zs[0], mean[0], None),
            (zs[1] + zs[1], strong[1], edge[2]),
            ((2.0 * AXIAL) * zs[2], upright, edge[1]),
        ]
        ahead = [
            (strong[0] + edge[2], lift[0] + tip[2], mixed[1]),
            (mean[1], lift[1], tip[2] + mixed[0]),
            (upright + edge[0], flat + tip[0], tip[1]),
        ]
        behind = [
            (strong[0] - edge[2], lift[0] - tip[2], -mixed[1]),
            (mean[1], lift[1], tip[2] - mixed[0]),
            (upright - edge[0], flat - tip[0], tip[1]),
        ]
        return tuple([term for row in part for term in row] for part in (here, ahead, behind))

    def window_sums(terms):
        sums = []
        for k in range(3):
            stays, even, odd = terms[3 * k : 3 * k + 3]
            after = along_y(even + odd, False)[0]
            before = along_y(even - odd, False)[1]
            sums.append(stays + after + before)
        return sums

    def slab_parts(w):
        return field_parts(w, True)

    def slab_sums(terms):
        return terms

    def joined(left, right):
        return [b if a is None else a + b for a, b in zip(left, right)]

    def sweep(
        parts, sums, count, load, keep, drive, value, store, root_s, push_s, inverse_s, shear_s
    ):
        offset = (wide - count) // 2
        partial = None
        trail = None
        free = None
        for i in range(count):
            held = free
            r = root_s[i + offset]
            if drive is not None:
                free = 1.0 - value(3, i + offset - 1) * at_bottom
                r = r * free
            here, ahead, behind = parts([r * load(k, i) for k in range(3)])
            if i >= 2:
                j = i - 1
                d = j + offset - 1
                old = [load(k, j) for k in range(3)]
                shear = [shear_s[k, d] for k in range(3)]
                rest = [
                    shear[0] * old[1] + shear[1] * old[2],
                    shear[0] * old[0] + shear[2] * old[2],
                    shear[1] * old[0] + shear[2] * old[1],
                ]
                total = sums(joined(partial, ahead))
                for k in range(3):
                    new = keep * old[k] + (total[k] - rest[k]) * inverse_s[k, d]
                    if drive is not None:
                        new = (new + drive * push_s[k, d]) * held
                    store(k, j - 1, new)
            if i >= 1:
                partial = joined(here, trail)
            trail = behind

    keep_second = (1.0 - omegas[1]) / omegas[1] + 1.0 / omegas[0]
    keep_third = (1.0 - omegas[2]) / omegas[2]
    drive_third = 1.0 / (omegas[0] * omegas[1])

    fold = rows // SUB
    inv_a = first_a.at[0]
    stiffness(fold, PAD, None, root_a, drive_a, inv_a, None)
    tensor(True, None, root_a, shear_a, inverse_a, None)
    value = pushes(case, lines_of(fold), drive_a, inv_a, inverse_a, push_a)

    def store_first_a(k, i, new):
        first_a[k, i] = new

    def store_third_a(k, i, new):
        for t in range(fold):
            third_n[k, i, pl.ds(PAD + t, SUB, stride=fold), :] = new[t]
            if 1 <= i <= cells:
                field_v[k, i - 1, pl.ds(t, SUB, stride=fold), :] = scale * new[t]

    arrays = (root_a, push_a, inverse_a, shear_a)
    whole = (slab_parts, slab_sums)
    sweep(
        *whole,
        wide - 2,
        lambda k, i: push_a[k, i],
        keep_second,
        None,
        value,
        store_first_a,
        *arrays,
    )
    sweep(
        *whole,
        wide - 4,
        lambda k, i: first_a[k, i],
        keep_third,
        drive_third,
        value,
        store_third_a,
        *arrays,
    )
    leaving = pltpu.make_async_copy(field_v, field_ref, gone.at[0])
    leaving.start()

    fold_b = result_n.shape[1] // SUB
    top = case * band - HALO
    y_of = top + lines_of(fold_b)
    keep_rows = ((y_of >= 0) & (y_of < rows)).astype(jnp.float32)
    inv_b = work_b.at[pl.ds(0, wide - 2)]
    stiffness(fold_b, PAD + top, keep_rows, root_b, drive_b, inv_b, factor_b)
    tensor(False, keep_rows, root_b, shear_b, inverse_b, main_b)
    gathered = work_b.at[pl.ds(wide - 2, cells)]
    empty = jnp.zeros((fold_b, SUB, depth), jnp.float32)
    for i in range(cells + 2):
        for n in range(6):
            squares_b[n, i] = empty
    for i in range(cells):
        gathered[i] = empty

    def store_first_b(k, i, new):
        first_b[k, i] = new

    def store_second_b(k, i, new):
        second_b[k, i] = new

    window_only = (window_parts, window_sums)

    @pl.loop(0, groups)
    def add_case(other):
        @pl.when(other == 0)
        def take_own():
            for k in range(3):
                for i in range(cells + 2):
                    second_b[k, i] = jnp.stack(
                        [
                            third_n[k, i, pl.ds(PAD + top + t, SUB, stride=fold_b), :]
                            for t in range(fold_b)
                        ]
                    )

        @pl.when(other > 0)
        def relax_other():
            which = lax.rem(case + other, groups)
            value = pushes(which, y_of, drive_b, inv_b, inverse_b, push_b)
            arrays = (root_b, push_b, inverse_b, shear_b)
            sweep(
                *window_only,
                wide - 2,
                lambda k, i: push_b[k, i],
                keep_second,
                None,
                value,
                store_first_b,
                *arrays,
            )
            sweep(
                *window_only,
                wide - 4,
                lambda k, i: first_b[k, i],
                keep_third,
                drive_third,
                value,
                store_second_b,
                *arrays,
            )

        partial = None
        trail = None
        for i in range(cells + 2):
            r = root_b[i + EDGE]
            v = [second_b[k, i] for k in range(3)]
            w = [r * v[k] for k in range(3)]
            for n, (a, b) in enumerate(((0, 0), (1, 1), (2, 2), (0, 1), (0, 2), (1, 2))):
                squares_b[n, i] += w[a] * v[b]
            here, ahead, behind = window_parts(w)
            if i >= 2:
                old = [second_b[k, i - 1] for k in range(3)]
                total = window_sums(joined(partial, ahead))
                dot = [old[k] * total[k] for k in range(3)]
                gathered[i - 2] += dot[0] + dot[1] + dot[2]
            if i >= 1:
                partial = joined(here, trail)
            trail = behind

    def square_parts(q):
        qxx, qyy, qzz, qxy, qxz, qyz = q
        s = qxx + qyy + qzz
        zs_s = plus(along_z(s))
        zs_x = plus(along_z(qxx))
        zs_z = plus(along_z(qzz))
        zs_xy = plus(along_z(qxy))
        zd_yz = minus(along_z(qyz))
        zd_xz = minus(along_z(qxz))
        twist = minus(along_y(zd_yz, False))
        half = 0.5 * zs_s + 0.125 * zs_z
        here = (
            zs_s
            + 0.5 * zs_z
            + plus(along_y(s + 0.5 * qyy + (PAIR * zs_s - 0.125 * zs_x), False))
            + 0.25 * twist
        )
        even = (
            s
            + 0.5 * qxx
            + half
            + 0.125 * zs_x
            + plus(along_y(0.5 * s + 0.125 * (qxx + qyy) + FULL * zs_s, False))
            + (1.0 / 12.0) * twist
        )
        odd = (
            minus(along_y(0.25 * qxy + (1.0 / 12.0) * zs_xy, False))
            + 0.25 * zd_xz
            + plus(along_y((1.0 / 12.0) * zd_xz, False))
        )
        return here, even + odd, even - odd

    partial = None
    trail = None
    for i in range(cells + 2):
        here, ahead, behind = square_parts([squares_b[n, i] for n in range(6)])
        if i >= 2:
            j = i - 2
            q = [squares_b[n, i - 1] for n in range(6)]
            d = j + EDGE
            held = main_b[0, j] * q[0] + main_b[1, j] * q[1] + main_b[2, j] * q[2]
            mixed = shear_b[0, d] * q[3] + shear_b[1, d] * q[4] + shear_b[2, d] * q[5]
            rest = partial + ahead - 2.0 * gathered[j]
            total = held + 2.0 * mixed + root_b[d + 1] * rest
            total = total * factor_b[j]
            for t in range(fold_b):
                result_n[j, pl.ds(t, SUB, stride=fold_b), :] = total[t]
        if i >= 1:
            partial = here + trail
        trail = behind
    sensitivity_ref[...] = result_n[:, HALO : HALO + band, :]
    leaving.wait()


def on_vmem():
    return pl.BlockSpec(memory_space=pltpu.VMEM)


def on_smem():
    return pl.BlockSpec(memory_space=pltpu.SMEM)


def solids(density, void_depth):
    cells, band, depth = density.shape
    return pl.pallas_call(
        solid_kernel,
        out_shape=[
            pltpu.VMEM((planes, band, depth), jnp.float32) for planes in (cells, HALO, HALO)
        ],
        in_specs=[pl.BlockSpec(memory_space=pltpu.HBM)] * 2,
        out_specs=[on_vmem()] * 3,
        scratch_shapes=[
            pltpu.VMEM(density.shape, jnp.float32),
            pltpu.VMEM(void_depth.shape, jnp.int32),
            pltpu.SemaphoreType.DMA((2,)),
        ],
    )(*(pltpu.with_memory_space_constraint(array, pltpu.HBM) for array in (density, void_depth)))


def settings(band, depth, supports, load_x, load_y, load_vectors):
    vectors = load_vectors.transpose(1, 0, 2)
    return pl.pallas_call(
        settings_kernel,
        out_shape=pltpu.VMEM((1, band, depth), jnp.float32),
        in_specs=[pl.BlockSpec(memory_space=pltpu.HBM)] * 2 + [on_smem()] * 2,
        out_specs=on_vmem(),
        scratch_shapes=[
            pltpu.SMEM(supports.shape, jnp.int32),
            pltpu.SMEM(vectors.shape, jnp.float32),
            pltpu.SemaphoreType.DMA((2,)),
        ],
    )(
        *(pltpu.with_memory_space_constraint(array, pltpu.HBM) for array in (supports, vectors)),
        load_x,
        load_y,
    )


def relaxed(bands):
    groups, planes, band, depth = bands.shape
    wide = planes - 1
    cells = wide - 2 * HALO
    rows = groups * band
    fold = rows // SUB
    fold_b = -(-(band + 2 * HALO) // SUB)
    tall = PAD + rows + fold_b * SUB

    def area(*lead):
        return pltpu.VMEM((*lead, fold, SUB, depth), jnp.float32)

    def window(*lead):
        return pltpu.VMEM((*lead, fold_b, SUB, depth), jnp.float32)

    return pl.pallas_call(
        relax_kernel,
        out_shape=(
            jax.ShapeDtypeStruct((3, cells, rows, depth), jnp.float32),
            jax.ShapeDtypeStruct((cells, band, depth), jnp.float32),
        ),
        in_specs=[on_vmem()],
        out_specs=(pl.BlockSpec(memory_space=pltpu.HBM), on_vmem()),
        scratch_shapes=[
            pltpu.VMEM((wide, tall, depth), jnp.float32),
            pltpu.VMEM((3, cells + 2, tall, depth), jnp.float32),
            pltpu.VMEM((cells, fold_b * SUB, depth), jnp.float32),
            area(wide),
            area(wide - 2),
            area(3, wide - 2),
            area(3, wide - 2),
            area(3, wide - 2),
            area(3, wide - 2),
            window(wide),
            window(wide - 2),
            window(3, wide - 2),
            window(3, wide - 2),
            window(3, wide - 2),
            window(3, wide - 4),
            window(3, cells),
            window(cells),
            window(3, cells + 2),
            window(6, cells + 2),
            window(wide - 2 + cells),
            pltpu.VMEM((3, cells, rows, depth), jnp.float32),
            pltpu.SemaphoreType.DMA((1,)),
        ],
        compiler_params=pltpu.CompilerParams(vmem_limit_bytes=32 * 1024 * 1024),
    )(bands)


def shards(density, void_depth, supports, load_x, load_y, load_vectors):
    cells, band, depth = density.shape
    groups = lax.axis_size("case")
    slabs = lax.axis_size("space")
    solid, far, near = solids(density, void_depth)
    across = [(i, i + 1) for i in range(1, slabs - 1, 2)]
    across += [(j, i) for i, j in across]
    inside = [(i, i + 1) for i in range(0, slabs, 2)]
    inside += [(j, i) for i, j in inside]
    first = lax.rem(lax.axis_index("space"), CORES) == 0
    outer = lax.ppermute(far, "space", across)
    inner = lax.ppermute(near, "space", inside)
    row = settings(band, depth, supports, load_x, load_y, load_vectors)
    before = jnp.where(first, outer, inner)
    after = jnp.where(first, inner, outer)
    mine = jnp.concatenate([before, solid, after, row])
    mine = jnp.broadcast_to(mine[None], (groups, *mine.shape))
    bands = lax.all_to_all(mine, "case", split_axis=0, concat_axis=0, tiled=True)
    field, sensitivity = relaxed(bands)
    return (field[None], sensitivity)


def solution(mesh):
    return jax.shard_map(
        shards,
        mesh=mesh,
        in_specs=(
            P("space", "case", None),
            P("space", "case"),
            P("case", None),
            P("case"),
            P("case"),
            P("case", None, None),
        ),
        out_specs=(P("case", None, "space", None, None), P("space", "case", None)),
        check_vma=False,
    )
```

```python
import math

import jax
import jax.numpy as jnp
from jax import lax
from jax.experimental import pallas as pl
from jax.experimental.pallas import tpu as pltpu
from jax.sharding import PartitionSpec as P

SWEEPS = 3
LOADW = 8
EMIN = 0.001
LOWER = 0.06
UPPER = 3.0
PATCH = 4.0
SUB = 8
CORES = 2
ABREAST = 3
HALO = SWEEPS + 1
EDGE = HALO - 1
PAD = 8

AXIAL = 1.5
PAIR = 0.625
FLAT = 0.5
FULL = 0.25 * (1.0 + 0.5 / 3.0)
CROSS2 = 0.125
CROSS3 = 0.125 / 3.0


def relaxations(count):
    middle = 0.5 * (UPPER + LOWER)
    radius = 0.5 * (UPPER - LOWER)
    return [
        1.0 / (middle + radius * math.cos(math.pi * (2 * index + 1) / (2 * count)))
        for index in range(count)
    ]


def both(pair):
    return pair[0] + pair[1], pair[0] - pair[1]


def plus(pair):
    return pair[0] + pair[1]


def minus(pair):
    return pair[0] - pair[1]


def span_of(cells):
    return cells + 2 * EDGE


def solid_kernel(
    density_in, void_in, solid_ref, outer_ref, inner_ref, density_ref, void_ref, arrived
):
    fetches = [
        pltpu.make_async_copy(void_in, void_ref, arrived.at[0]),
        pltpu.make_async_copy(density_in, density_ref, arrived.at[1]),
    ]
    for fetch in fetches:
        fetch.start()
    cells, band, depth = solid_ref.shape
    first = lax.rem(lax.axis_index("space"), CORES) == 0
    level = lax.broadcasted_iota(jnp.int32, (band, depth), 1) - depth // 2
    eye = lax.broadcasted_iota(jnp.int32, (band, band), 0) == lax.broadcasted_iota(
        jnp.int32, (band, band), 1
    )
    for fetch in fetches:
        fetch.wait()
    for i in range(cells):
        line = jnp.broadcast_to(void_ref[i : i + 1, :], (band, band)).astype(jnp.float32)
        column = jnp.sum(jnp.where(eye, line, 0.0), axis=1, keepdims=True)
        top = jnp.broadcast_to(column, (band, depth)).astype(jnp.int32)
        hollow = (level >= 0) & (level < top)
        solid_ref[i] = jnp.where(hollow, 0.0, density_ref[i])
    for i in range(HALO):
        low = solid_ref[i]
        high = solid_ref[cells - HALO + i]
        outer_ref[i] = jnp.where(first, low, high)
        inner_ref[i] = jnp.where(first, high, low)


def settings_kernel(
    supports_in, vectors_in, load_x_ref, load_y_ref, row_ref, supports_ref, vectors_ref, arrived
):
    fetches = [
        pltpu.make_async_copy(supports_in, supports_ref, arrived.at[0]),
        pltpu.make_async_copy(vectors_in, vectors_ref, arrived.at[1]),
    ]
    for fetch in fetches:
        fetch.start()
    for fetch in fetches:
        fetch.wait()
    slabs = lax.axis_size("space")
    band, depth = row_ref.shape[1:]
    total_x = vectors_ref.shape[2]
    cells = total_x // slabs
    span = span_of(cells)
    first = lax.axis_index("space") * cells - EDGE
    lane = lax.broadcasted_iota(jnp.int32, (1, depth), 1)
    row = jnp.where(lane == 5 * span, load_y_ref[0].astype(jnp.float32), 0.0)
    for m in range(span):
        place = first + m
        inside = jnp.logical_and(place >= 0, place < total_x)
        where = jnp.clip(place, 0, total_x - 1)
        for k in range(3):
            value = jnp.where(inside, vectors_ref[k, 0, where], 0.0)
            row = jnp.where(lane == k * span + m, value, row)
    place = first + lane - 3 * span
    pinned = (place < supports_ref[0, 0]) | (place >= total_x - supports_ref[0, 1])
    row = jnp.where((lane >= 3 * span) & (lane < 4 * span) & pinned, 1.0, row)
    place = first + lane - 4 * span
    loaded = (place >= load_x_ref[0]) & (place < load_x_ref[0] + LOADW)
    row = jnp.where((lane >= 4 * span) & (lane < 5 * span) & loaded, 1.0, row)
    row_ref[0] = jnp.broadcast_to(row, (band, depth))


def relax_kernel(
    bands_ref,
    field_ref,
    sensitivity_ref,
    natural,
    third_n,
    result_n,
    root_a,
    drive_a,
    push_a,
    inverse_a,
    shear_a,
    first_a,
    root_b,
    drive_b,
    push_b,
    inverse_b,
    shear_b,
    first_b,
    main_b,
    factor_b,
    second_b,
    squares_b,
    work_b,
    field_v,
    gone,
):
    groups, planes, band, depth = bands_ref.shape
    wide = planes - 1
    cells = wide - 2 * HALO
    span = span_of(cells)
    rows = groups * band
    case = lax.axis_index("case")
    total_x = lax.axis_size("space") * cells
    first_plane = lax.axis_index("space") * cells
    omegas = relaxations(SWEEPS)
    scale = omegas[0] * omegas[1] * omegas[2]

    blank = jnp.zeros((PAD, depth), jnp.float32)
    for i in range(wide):
        natural[i, 0:PAD, :] = blank
        for at in range(PAD + rows, natural.shape[1], PAD):
            natural[i, at : at + PAD, :] = blank
    for k in range(3):
        for i in range(cells + 2):
            third_n[k, i, 0:PAD, :] = blank
            for at in range(PAD + rows, natural.shape[1], PAD):
                third_n[k, i, at : at + PAD, :] = blank
    for g in range(groups):
        natural[:, PAD + g * band : PAD + (g + 1) * band, :] = bands_ref[g, 0:wide]

    tile = (1, SUB, depth)
    lane = lax.broadcasted_iota(jnp.int32, tile, 2)
    line = lax.broadcasted_iota(jnp.int32, tile, 1)
    not_first_z = (lane > 0).astype(jnp.float32)
    not_last_z = (lane < depth - 1).astype(jnp.float32)
    not_first_s = (line > 0).astype(jnp.float32)
    not_last_s = (line < SUB - 1).astype(jnp.float32)
    at_bottom = (lane == 0).astype(jnp.float32)
    half_first_z = 0.5 * not_first_z
    half_last_z = 0.5 * not_last_z

    def along_z(a):
        after = pltpu.roll(a, depth - 1, 2) * not_last_z
        before = pltpu.roll(a, 1, 2) * not_first_z
        return after, before

    def along_y(a, closed):
        fold = a.shape[0]
        after = pltpu.roll(a[0:1], SUB - 1, 1)
        before = pltpu.roll(a[fold - 1 : fold], 1, 1)
        if closed:
            after = after * not_last_s
            before = before * not_first_s
        return (
            jnp.concatenate([a[1:], after], axis=0),
            jnp.concatenate([before, a[:-1]], axis=0),
        )

    def inside_of(plane, margin):
        place = first_plane - margin + plane
        return jnp.logical_and(place >= 0, place < total_x).astype(jnp.float32)

    def lines_of(fold):
        shape = (fold, SUB, depth)
        return fold * lax.broadcasted_iota(jnp.int32, shape, 1) + lax.broadcasted_iota(
            jnp.int32, shape, 0
        )

    def case_values(which):
        plain = jnp.broadcast_to(bands_ref[which, wide, 0:1, :], (SUB, depth))

        def value(kind, j):
            at = kind * span + j
            return jnp.broadcast_to(plain[:, at : at + 1], (SUB, depth))[None]

        corner = jnp.broadcast_to(plain[:, 5 * span : 5 * span + 1], (SUB, depth))[None]
        return value, corner

    def patch_of(y_of, corner):
        y = y_of.astype(jnp.float32)
        high = lax.broadcasted_iota(jnp.int32, y_of.shape, 2) == depth - 1
        return jnp.where(high & (y >= corner) & (y < corner + LOADW), PATCH, 0.0)

    def stiffness(fold, start, keep_rows, root_s, drive_s, inv_s, factor_s):
        for i in range(wide):
            solid = jnp.stack(
                [natural[i, pl.ds(start + t, SUB, stride=fold), :] for t in range(fold)]
            )
            stiff = EMIN + (1.0 - EMIN) * (solid * solid * solid)
            inv_root = lax.rsqrt(stiff)
            root = stiff * inv_root * inside_of(i, HALO)
            root_s[i] = root if keep_rows is None else root * keep_rows
            if 0 < i < wide - 1:
                drive_s[i - 1] = solid * inv_root
                inv_s[i - 1] = inv_root
            if factor_s is not None and HALO <= i < HALO + cells:
                ratio = solid * inv_root
                factor_s[i - HALO] = ((-1.5 * (1.0 - EMIN)) * scale * scale / groups) * (ratio * ratio)

    def tensor_parts(r, closed):
        zs, zd = both(along_z(r))
        ys, yd = both(along_y(r, closed))
        yszs, ydzs = both(along_y(zs, closed))
        yszd, ydzd = both(along_y(zd, closed))
        cross = ys + zs
        corner = PAIR * yszs
        here = [
            cross + FLAT * yszs,
            cross + 0.5 * ys + corner,
            cross + 0.5 * zs + corner,
            CROSS2 * ydzd,
        ]
        base = FULL * yszs + 0.5 * cross + r
        even = [
            base + 0.5 * r + 0.125 * cross,
            base + 0.125 * ys,
            base + 0.125 * zs,
            CROSS3 * ydzd,
        ]
        odd = [CROSS2 * yd + CROSS3 * ydzs, CROSS2 * zd + CROSS3 * yszd]
        return here, even, odd

    def tensor(closed, keep_rows, root_s, shear_s, inverse_s, main_s):
        older = None
        newer = None
        for i in range(wide):
            latest = tensor_parts(root_s[i], closed)
            if i >= 2:
                j = i - 2
                keep = inside_of(j, EDGE)
                if keep_rows is not None:
                    keep = keep * keep_rows
                total = [newer[0][k] + (latest[1][k] + older[1][k]) for k in range(4)]
                shear_s[0, j] = latest[2][0] - older[2][0]
                shear_s[1, j] = latest[2][1] - older[2][1]
                shear_s[2, j] = total[3]
                for k in range(3):
                    if main_s is not None and EDGE <= j < EDGE + cells:
                        main_s[k, j - EDGE] = total[k]
                    inverse_s[k, j] = keep / (total[k] + (1.0 - keep))
            older, newer = newer, latest

    def pushes(which, y_of, drive_s, inv_s, inverse_s, push_s):
        value, corner = case_values(which)
        patch = patch_of(y_of, corner)
        for j in range(wide - 2):
            free = 1.0 - value(3, j) * at_bottom
            push = (drive_s[j] + (value(4, j) * patch) * inv_s[j]) * free
            for k in range(3):
                push_s[k, j] = push * inverse_s[k, j] * value(k, j)
        return value

    def field_parts(w, closed):
        zs, zd = [], []
        for k in range(3):
            after = pltpu.roll(w[k], depth - 1, 2) * half_last_z
            before = pltpu.roll(w[k], 1, 2) * half_first_z
            zs.append(after + before)
            zd.append(after - before)
        mean = [w[k] + zs[k] for k in range(2)]
        mixed = [CROSS2 * w[k] + (2.0 * CROSS3) * zs[k] for k in range(2)]
        even_y = [plus(along_y(0.5 * mean[k] + mixed[k], closed)) for k in range(2)]
        odd_y = [minus(along_y(mixed[k], closed)) for k in range(2)]
        strong = [(2.0 * PAIR) * mean[k] + (AXIAL - 2.0 * PAIR) * w[k] for k in range(2)]
        upright = w[2] + (2.0 * PAIR) * zs[2]
        flat = FLAT * w[2] + (2.0 * FULL) * zs[2]
        twist_y = minus(along_y(zd[1], closed))
        spread_z, twist_z = both(along_y(zd[2], closed))
        slope_x = (2.0 * CROSS2) * zd[0] + (2.0 * CROSS3) * plus(along_y(zd[0], closed))
        slope_z = (2.0 * CROSS2) * zd[2] + (2.0 * CROSS3) * spread_z
        here = [
            plus(along_y(mean[0], closed)) + (zs[0] + zs[0]),
            plus(along_y(strong[1], closed)) + (zs[1] + zs[1]) + (2.0 * CROSS2) * twist_z,
            plus(along_y(upright, closed)) + (2.0 * AXIAL) * zs[2] + (2.0 * CROSS2) * twist_y,
        ]
        even = [
            strong[0] + even_y[0],
            mean[1] + even_y[1] + (2.0 * CROSS3) * twist_z,
            upright + plus(along_y(flat, closed)) + (2.0 * CROSS3) * twist_y,
        ]
        odd = [odd_y[1] + slope_z, odd_y[0], slope_x]
        ahead = [even[k] + odd[k] for k in range(3)]
        behind = [even[k] - odd[k] for k in range(3)]
        return here, ahead, behind

    def window_parts(w):
        zs, zd = [], []
        for k in range(3):
            after = pltpu.roll(w[k], depth - 1, 2) * half_last_z
            before = pltpu.roll(w[k], 1, 2) * half_first_z
            zs.append(after + before)
            zd.append(after - before)
        mean = [w[k] + zs[k] for k in range(2)]
        mixed = [CROSS2 * w[k] + (2.0 * CROSS3) * zs[k] for k in range(2)]
        lift = [0.5 * mean[k] + mixed[k] for k in range(2)]
        strong = [(2.0 * PAIR) * mean[k] + (AXIAL - 2.0 * PAIR) * w[k] for k in range(2)]
        upright = w[2] + (2.0 * PAIR) * zs[2]
        flat = FLAT * w[2] + (2.0 * FULL) * zs[2]
        edge = [(2.0 * CROSS2) * zd[k] for k in range(3)]
        tip = [(2.0 * CROSS3) * zd[k] for k in range(3)]
        here = [
            (zs[0] + zs[0], mean[0], None),
            (zs[1] + zs[1], strong[1], edge[2]),
            ((2.0 * AXIAL) * zs[2], upright, edge[1]),
        ]
        ahead = [
            (strong[0] + edge[2], lift[0] + tip[2], mixed[1]),
            (mean[1], lift[1], tip[2] + mixed[0]),
            (upright + edge[0], flat + tip[0], tip[1]),
        ]
        behind = [
            (strong[0] - edge[2], lift[0] - tip[2], -mixed[1]),
            (mean[1], lift[1], tip[2] - mixed[0]),
            (upright - edge[0], flat - tip[0], tip[1]),
        ]
        return tuple([term for row in part for term in row] for part in (here, ahead, behind))

    def window_sums(terms):
        sums = []
        for k in range(3):
            stays, even, odd = terms[3 * k : 3 * k + 3]
            after = along_y(even + odd, False)[0]
            before = along_y(even - odd, False)[1]
            sums.append(stays + after + before)
        return sums

    def slab_parts(w):
        return field_parts(w, True)

    def slab_sums(terms):
        return terms

    def joined(left, right):
        return [b if a is None else a + b for a, b in zip(left, right)]

    def sweep(
        parts, sums, count, load, keep, drive, value, store, root_s, push_s, inverse_s, shear_s
    ):
        offset = (wide - count) // 2
        partial = None
        trail = None
        free = None
        for i in range(count):
            held = free
            r = root_s[i + offset]
            if drive is not None:
                free = 1.0 - value(3, i + offset - 1) * at_bottom
                r = r * free
            here, ahead, behind = parts([r * load(k, i) for k in range(3)])
            if i >= 2:
                j = i - 1
                d = j + offset - 1
                old = [load(k, j) for k in range(3)]
                shear = [shear_s[k, d] for k in range(3)]
                rest = [
                    shear[0] * old[1] + shear[1] * old[2],
                    shear[0] * old[0] + shear[2] * old[2],
                    shear[1] * old[0] + shear[2] * old[1],
                ]
                total = sums(joined(partial, ahead))
                for k in range(3):
                    new = keep * old[k] + (total[k] - rest[k]) * inverse_s[k, d]
                    if drive is not None:
                        new = (new + drive * push_s[k, d]) * held
                    store(k, j - 1, new)
            if i >= 1:
                partial = joined(here, trail)
            trail = behind

    keep_second = (1.0 - omegas[1]) / omegas[1] + 1.0 / omegas[0]
    keep_third = (1.0 - omegas[2]) / omegas[2]
    drive_third = 1.0 / (omegas[0] * omegas[1])

    fold = rows // SUB
    inv_a = first_a.at[0]
    stiffness(fold, PAD, None, root_a, drive_a, inv_a, None)
    tensor(True, None, root_a, shear_a, inverse_a, None)
    value = pushes(case, lines_of(fold), drive_a, inv_a, inverse_a, push_a)

    def store_first_a(k, i, new):
        first_a[k, i] = new

    def store_third_a(k, i, new):
        for t in range(fold):
            third_n[k, i, pl.ds(PAD + t, SUB, stride=fold), :] = new[t]
            if 1 <= i <= cells:
                field_v[k, i - 1, pl.ds(t, SUB, stride=fold), :] = scale * new[t]

    arrays = (root_a, push_a, inverse_a, shear_a)
    whole = (slab_parts, slab_sums)
    sweep(
        *whole,
        wide - 2,
        lambda k, i: push_a[k, i],
        keep_second,
        None,
        value,
        store_first_a,
        *arrays,
    )
    sweep(
        *whole,
        wide - 4,
        lambda k, i: first_a[k, i],
        keep_third,
        drive_third,
        value,
        store_third_a,
        *arrays,
    )
    leaving = pltpu.make_async_copy(field_v, field_ref, gone.at[0])
    leaving.start()

    fold_b = result_n.shape[1] // SUB
    top = case * band - HALO
    y_of = top + lines_of(fold_b)
    keep_rows = ((y_of >= 0) & (y_of < rows)).astype(jnp.float32)
    inv_b = work_b.at[pl.ds(0, wide - 2)]
    stiffness(fold_b, PAD + top, keep_rows, root_b, drive_b, inv_b, factor_b)
    tensor(False, keep_rows, root_b, shear_b, inverse_b, main_b)
    gathered = work_b.at[pl.ds(wide - 2, cells)]
    window_only = (window_parts, window_sums)
    products = ((0, 0), (1, 1), (2, 2), (0, 1), (0, 2), (1, 2))

    def relax_other(which, slot):
        push_s = push_b.at[slot]
        first_s = first_b.at[slot]
        value = pushes(which, y_of, drive_b, inv_b, inverse_b, push_s)

        def store_first(k, i, new):
            first_s[k, i] = new

        def store_second(k, i, new):
            second_b[slot, k, i] = new

        arrays = (root_b, push_s, inverse_b, shear_b)
        sweep(
            *window_only,
            wide - 2,
            lambda k, i: push_s[k, i],
            keep_second,
            None,
            value,
            store_first,
            *arrays,
        )
        sweep(
            *window_only,
            wide - 4,
            lambda k, i: first_s[k, i],
            keep_third,
            drive_third,
            value,
            store_second,
            *arrays,
        )

    def add_energies(places, fresh):
        for i in range(cells + 2):
            sums = [None] * len(products)
            for slot in places:
                v = [second_b[slot, k, i] for k in range(3)]
                sums = joined(sums, [v[a] * v[b] for a, b in products])
            r = root_b[i + EDGE]
            for n, total in enumerate(sums):
                if fresh:
                    squares_b[n, i] = r * total
                else:
                    squares_b[n, i] += r * total
        for slot in places:
            partial = None
            trail = None
            for i in range(cells + 2):
                r = root_b[i + EDGE]
                here, ahead, behind = window_parts([r * second_b[slot, k, i] for k in range(3)])
                if i >= 2:
                    total = window_sums(joined(partial, ahead))
                    dot = [second_b[slot, k, i - 1] * total[k] for k in range(3)]
                    if fresh:
                        gathered[i - 2] = dot[0] + dot[1] + dot[2]
                    else:
                        gathered[i - 2] += dot[0] + dot[1] + dot[2]
                if i >= 1:
                    partial = joined(here, trail)
                trail = behind

    abreast = second_b.shape[0] - 1
    for k in range(3):
        for i in range(cells + 2):
            second_b[abreast, k, i] = jnp.stack(
                [third_n[k, i, pl.ds(PAD + top + t, SUB, stride=fold_b), :] for t in range(fold_b)]
            )
    add_energies([abreast], True)

    def add_others(start):
        for slot in range(abreast):
            relax_other(lax.rem(case + start + slot, groups), slot)
        add_energies(range(abreast), False)

    if groups - 1 == abreast:
        add_others(1)
    else:
        pl.loop(1, groups, step=abreast)(add_others)

    def square_parts(q):
        qxx, qyy, qzz, qxy, qxz, qyz = q
        s = qxx + qyy + qzz
        zs_s = plus(along_z(s))
        zs_x = plus(along_z(qxx))
        zs_z = plus(along_z(qzz))
        zs_xy = plus(along_z(qxy))
        zd_yz = minus(along_z(qyz))
        zd_xz = minus(along_z(qxz))
        twist = minus(along_y(zd_yz, False))
        half = 0.5 * zs_s + 0.125 * zs_z
        here = (
            zs_s
            + 0.5 * zs_z
            + plus(along_y(s + 0.5 * qyy + (PAIR * zs_s - 0.125 * zs_x), False))
            + 0.25 * twist
        )
        even = (
            s
            + 0.5 * qxx
            + half
            + 0.125 * zs_x
            + plus(along_y(0.5 * s + 0.125 * (qxx + qyy) + FULL * zs_s, False))
            + (1.0 / 12.0) * twist
        )
        odd = (
            minus(along_y(0.25 * qxy + (1.0 / 12.0) * zs_xy, False))
            + 0.25 * zd_xz
            + plus(along_y((1.0 / 12.0) * zd_xz, False))
        )
        return here, even + odd, even - odd

    partial = None
    trail = None
    for i in range(cells + 2):
        here, ahead, behind = square_parts([squares_b[n, i] for n in range(6)])
        if i >= 2:
            j = i - 2
            q = [squares_b[n, i - 1] for n in range(6)]
            d = j + EDGE
            held = main_b[0, j] * q[0] + main_b[1, j] * q[1] + main_b[2, j] * q[2]
            mixed = shear_b[0, d] * q[3] + shear_b[1, d] * q[4] + shear_b[2, d] * q[5]
            rest = partial + ahead - 2.0 * gathered[j]
            total = held + 2.0 * mixed + root_b[d + 1] * rest
            total = total * factor_b[j]
            for t in range(fold_b):
                result_n[j, pl.ds(t, SUB, stride=fold_b), :] = total[t]
        if i >= 1:
            partial = here + trail
        trail = behind
    sensitivity_ref[...] = result_n[:, HALO : HALO + band, :]
    leaving.wait()


def on_vmem():
    return pl.BlockSpec(memory_space=pltpu.VMEM)


def on_smem():
    return pl.BlockSpec(memory_space=pltpu.SMEM)


def solids(density, void_depth):
    cells, band, depth = density.shape
    return pl.pallas_call(
        solid_kernel,
        out_shape=[
            pltpu.VMEM((planes, band, depth), jnp.float32) for planes in (cells, HALO, HALO)
        ],
        in_specs=[pl.BlockSpec(memory_space=pltpu.HBM)] * 2,
        out_specs=[on_vmem()] * 3,
        scratch_shapes=[
            pltpu.VMEM(density.shape, jnp.float32),
            pltpu.VMEM(void_depth.shape, jnp.int32),
            pltpu.SemaphoreType.DMA((2,)),
        ],
    )(*(pltpu.with_memory_space_constraint(array, pltpu.HBM) for array in (density, void_depth)))


def settings(band, depth, supports, load_x, load_y, load_vectors):
    vectors = load_vectors.transpose(1, 0, 2)
    return pl.pallas_call(
        settings_kernel,
        out_shape=pltpu.VMEM((1, band, depth), jnp.float32),
        in_specs=[pl.BlockSpec(memory_space=pltpu.HBM)] * 2 + [on_smem()] * 2,
        out_specs=on_vmem(),
        scratch_shapes=[
            pltpu.SMEM(supports.shape, jnp.int32),
            pltpu.SMEM(vectors.shape, jnp.float32),
            pltpu.SemaphoreType.DMA((2,)),
        ],
    )(
        *(pltpu.with_memory_space_constraint(array, pltpu.HBM) for array in (supports, vectors)),
        load_x,
        load_y,
    )


def relaxed(bands):
    groups, planes, band, depth = bands.shape
    wide = planes - 1
    cells = wide - 2 * HALO
    rows = groups * band
    fold = rows // SUB
    fold_b = -(-(band + 2 * HALO) // SUB)
    tall = PAD + rows + fold_b * SUB
    abreast = ABREAST if (groups - 1) % ABREAST == 0 else 1

    def area(*lead):
        return pltpu.VMEM((*lead, fold, SUB, depth), jnp.float32)

    def window(*lead):
        return pltpu.VMEM((*lead, fold_b, SUB, depth), jnp.float32)

    return pl.pallas_call(
        relax_kernel,
        out_shape=(
            jax.ShapeDtypeStruct((3, cells, rows, depth), jnp.float32),
            jax.ShapeDtypeStruct((cells, band, depth), jnp.float32),
        ),
        in_specs=[on_vmem()],
        out_specs=(pl.BlockSpec(memory_space=pltpu.HBM), on_vmem()),
        scratch_shapes=[
            pltpu.VMEM((wide, tall, depth), jnp.float32),
            pltpu.VMEM((3, cells + 2, tall, depth), jnp.float32),
            pltpu.VMEM((cells, fold_b * SUB, depth), jnp.float32),
            area(wide),
            area(wide - 2),
            area(3, wide - 2),
            area(3, wide - 2),
            area(3, wide - 2),
            area(3, wide - 2),
            window(wide),
            window(wide - 2),
            window(abreast, 3, wide - 2),
            window(3, wide - 2),
            window(3, wide - 2),
            window(abreast, 3, wide - 4),
            window(3, cells),
            window(cells),
            window(abreast + 1, 3, cells + 2),
            window(6, cells + 2),
            window(wide - 2 + cells),
            pltpu.VMEM((3, cells, rows, depth), jnp.float32),
            pltpu.SemaphoreType.DMA((1,)),
        ],
        compiler_params=pltpu.CompilerParams(vmem_limit_bytes=32 * 1024 * 1024),
    )(bands)


def shards(density, void_depth, supports, load_x, load_y, load_vectors):
    cells, band, depth = density.shape
    groups = lax.axis_size("case")
    slabs = lax.axis_size("space")
    solid, far, near = solids(density, void_depth)
    across = [(i, i + 1) for i in range(1, slabs - 1, 2)]
    across += [(j, i) for i, j in across]
    inside = [(i, i + 1) for i in range(0, slabs, 2)]
    inside += [(j, i) for i, j in inside]
    first = lax.rem(lax.axis_index("space"), CORES) == 0
    outer = lax.ppermute(far, "space", across)
    inner = lax.ppermute(near, "space", inside)
    row = settings(band, depth, supports, load_x, load_y, load_vectors)
    before = jnp.where(first, outer, inner)
    after = jnp.where(first, inner, outer)
    mine = jnp.concatenate([before, solid, after, row])
    mine = jnp.broadcast_to(mine[None], (groups, *mine.shape))
    bands = lax.all_to_all(mine, "case", split_axis=0, concat_axis=0, tiled=True)
    field, sensitivity = relaxed(bands)
    return (field[None], sensitivity)


def solution(mesh):
    return jax.shard_map(
        shards,
        mesh=mesh,
        in_specs=(
            P("space", "case", None),
            P("space", "case"),
            P("case", None),
            P("case"),
            P("case"),
            P("case", None, None),
        ),
        out_specs=(P("case", None, "space", None, None), P("space", "case", None)),
        check_vma=False,
    )
```

```python
import math

import jax
import jax.numpy as jnp
from jax import lax
from jax.experimental import pallas as pl
from jax.experimental.pallas import tpu as pltpu
from jax.sharding import PartitionSpec as P

SWEEPS = 3
LOADW = 8
EMIN = 0.001
LOWER = 0.06
UPPER = 3.0
PATCH = 4.0
SUB = 8
CORES = 2
ABREAST = 3
HALO = SWEEPS + 1
EDGE = HALO - 1
PAD = 8

AXIAL = 1.5
PAIR = 0.625
FLAT = 0.5
FULL = 0.25 * (1.0 + 0.5 / 3.0)
CROSS2 = 0.125
CROSS3 = 0.125 / 3.0


def relaxations(count):
    middle = 0.5 * (UPPER + LOWER)
    radius = 0.5 * (UPPER - LOWER)
    return [
        1.0 / (middle + radius * math.cos(math.pi * (2 * index + 1) / (2 * count)))
        for index in range(count)
    ]


def both(pair):
    return pair[0] + pair[1], pair[0] - pair[1]


def plus(pair):
    return pair[0] + pair[1]


def minus(pair):
    return pair[0] - pair[1]


def span_of(cells):
    return cells + 2 * EDGE


def solid_kernel(
    density_in, void_in, solid_ref, inner_ref, outer_ref, density_ref, void_ref, arrived
):
    fetches = [
        pltpu.make_async_copy(void_in, void_ref, arrived.at[0]),
        pltpu.make_async_copy(density_in, density_ref, arrived.at[1]),
    ]
    for fetch in fetches:
        fetch.start()
    cells, band, depth = solid_ref.shape
    first = lax.rem(lax.axis_index("space"), CORES) == 0
    level = lax.broadcasted_iota(jnp.int32, (band, depth), 1) - depth // 2
    eye = lax.broadcasted_iota(jnp.int32, (band, band), 0) == lax.broadcasted_iota(
        jnp.int32, (band, band), 1
    )
    for fetch in fetches:
        fetch.wait()
    for i in range(cells):
        line = jnp.broadcast_to(void_ref[i : i + 1, :], (band, band)).astype(jnp.float32)
        column = jnp.sum(jnp.where(eye, line, 0.0), axis=1, keepdims=True)
        top = jnp.broadcast_to(column, (band, depth)).astype(jnp.int32)
        hollow = (level >= 0) & (level < top)
        solid_ref[i] = jnp.where(hollow, 0.0, density_ref[i])
    for i in range(HALO):
        low = solid_ref[i]
        high = solid_ref[cells - HALO + i]
        outer_ref[i] = jnp.where(first, low, high)
        inner_ref[i] = jnp.where(first, high, low)


def settings_kernel(
    supports_in, vectors_in, load_x_ref, load_y_ref, row_ref, supports_ref, vectors_ref, arrived
):
    fetches = [
        pltpu.make_async_copy(supports_in, supports_ref, arrived.at[0]),
        pltpu.make_async_copy(vectors_in, vectors_ref, arrived.at[1]),
    ]
    for fetch in fetches:
        fetch.start()
    for fetch in fetches:
        fetch.wait()
    slabs = lax.axis_size("space")
    band, depth = row_ref.shape[1:]
    total_x = vectors_ref.shape[2]
    cells = total_x // slabs
    span = span_of(cells)
    first = lax.axis_index("space") * cells - EDGE
    lane = lax.broadcasted_iota(jnp.int32, (1, depth), 1)
    row = jnp.where(lane == 5 * span, load_y_ref[0].astype(jnp.float32), 0.0)
    for m in range(span):
        place = first + m
        inside = jnp.logical_and(place >= 0, place < total_x)
        where = jnp.clip(place, 0, total_x - 1)
        for k in range(3):
            value = jnp.where(inside, vectors_ref[k, 0, where], 0.0)
            row = jnp.where(lane == k * span + m, value, row)
    place = first + lane - 3 * span
    pinned = (place < supports_ref[0, 0]) | (place >= total_x - supports_ref[0, 1])
    row = jnp.where((lane >= 3 * span) & (lane < 4 * span) & pinned, 1.0, row)
    place = first + lane - 4 * span
    loaded = (place >= load_x_ref[0]) & (place < load_x_ref[0] + LOADW)
    row = jnp.where((lane >= 4 * span) & (lane < 5 * span) & loaded, 1.0, row)
    row_ref[0] = jnp.broadcast_to(row, (band, depth))


def relax_kernel(
    bands_ref,
    field_ref,
    sensitivity_ref,
    natural,
    third_n,
    result_n,
    root_a,
    drive_a,
    push_a,
    inverse_a,
    shear_a,
    first_a,
    root_b,
    drive_b,
    push_b,
    inverse_b,
    shear_b,
    first_b,
    main_b,
    factor_b,
    second_b,
    squares_b,
    work_b,
    field_v,
    gone,
):
    groups, planes, band, depth = bands_ref.shape
    wide = planes - 1
    cells = wide - 2 * HALO
    span = span_of(cells)
    rows = groups * band
    case = lax.axis_index("case")
    total_x = lax.axis_size("space") * cells
    first_plane = lax.axis_index("space") * cells
    omegas = relaxations(SWEEPS)
    scale = omegas[0] * omegas[1] * omegas[2]

    blank = jnp.zeros((PAD, depth), jnp.float32)
    for i in range(wide):
        natural[i, 0:PAD, :] = blank
        for at in range(PAD + rows, natural.shape[1], PAD):
            natural[i, at : at + PAD, :] = blank
    for k in range(3):
        for i in range(cells + 2):
            third_n[k, i, 0:PAD, :] = blank
            for at in range(PAD + rows, natural.shape[1], PAD):
                third_n[k, i, at : at + PAD, :] = blank
    for g in range(groups):
        natural[:, PAD + g * band : PAD + (g + 1) * band, :] = bands_ref[g, 0:wide]

    tile = (1, SUB, depth)
    lane = lax.broadcasted_iota(jnp.int32, tile, 2)
    line = lax.broadcasted_iota(jnp.int32, tile, 1)
    not_first_z = (lane > 0).astype(jnp.float32)
    not_last_z = (lane < depth - 1).astype(jnp.float32)
    not_first_s = (line > 0).astype(jnp.float32)
    not_last_s = (line < SUB - 1).astype(jnp.float32)
    at_bottom = (lane == 0).astype(jnp.float32)
    half_first_z = 0.5 * not_first_z
    half_last_z = 0.5 * not_last_z

    def along_z(a):
        after = pltpu.roll(a, depth - 1, 2) * not_last_z
        before = pltpu.roll(a, 1, 2) * not_first_z
        return after, before

    def along_y(a, closed):
        fold = a.shape[0]
        after = pltpu.roll(a[0:1], SUB - 1, 1)
        before = pltpu.roll(a[fold - 1 : fold], 1, 1)
        if closed:
            after = after * not_last_s
            before = before * not_first_s
        return (
            jnp.concatenate([a[1:], after], axis=0),
            jnp.concatenate([before, a[:-1]], axis=0),
        )

    def inside_of(plane, margin):
        place = first_plane - margin + plane
        return jnp.logical_and(place >= 0, place < total_x).astype(jnp.float32)

    def lines_of(fold):
        shape = (fold, SUB, depth)
        return fold * lax.broadcasted_iota(jnp.int32, shape, 1) + lax.broadcasted_iota(
            jnp.int32, shape, 0
        )

    def case_values(which):
        plain = jnp.broadcast_to(bands_ref[which, wide, 0:1, :], (SUB, depth))

        def value(kind, j):
            at = kind * span + j
            return jnp.broadcast_to(plain[:, at : at + 1], (SUB, depth))[None]

        corner = jnp.broadcast_to(plain[:, 5 * span : 5 * span + 1], (SUB, depth))[None]
        return value, corner

    def patch_of(y_of, corner):
        y = y_of.astype(jnp.float32)
        high = lax.broadcasted_iota(jnp.int32, y_of.shape, 2) == depth - 1
        return jnp.where(high & (y >= corner) & (y < corner + LOADW), PATCH, 0.0)

    def stiffness(fold, start, keep_rows, root_s, drive_s, inv_s, factor_s):
        for i in range(wide):
            solid = jnp.stack(
                [natural[i, pl.ds(start + t, SUB, stride=fold), :] for t in range(fold)]
            )
            stiff = EMIN + (1.0 - EMIN) * (solid * solid * solid)
            inv_root = lax.rsqrt(stiff)
            root = stiff * inv_root * inside_of(i, HALO)
            root_s[i] = root if keep_rows is None else root * keep_rows
            if 0 < i < wide - 1:
                drive_s[i - 1] = solid * inv_root
                inv_s[i - 1] = inv_root
            if factor_s is not None and HALO <= i < HALO + cells:
                ratio = solid * inv_root
                factor_s[i - HALO] = ((-1.5 * (1.0 - EMIN)) * scale * scale / groups) * (ratio * ratio)

    def tensor_parts(r, closed):
        zs, zd = both(along_z(r))
        ys, yd = both(along_y(r, closed))
        yszs, ydzs = both(along_y(zs, closed))
        yszd, ydzd = both(along_y(zd, closed))
        cross = ys + zs
        corner = PAIR * yszs
        here = [
            cross + FLAT * yszs,
            cross + 0.5 * ys + corner,
            cross + 0.5 * zs + corner,
            CROSS2 * ydzd,
        ]
        base = FULL * yszs + 0.5 * cross + r
        even = [
            base + 0.5 * r + 0.125 * cross,
            base + 0.125 * ys,
            base + 0.125 * zs,
            CROSS3 * ydzd,
        ]
        odd = [CROSS2 * yd + CROSS3 * ydzs, CROSS2 * zd + CROSS3 * yszd]
        return here, even, odd

    def tensor(closed, keep_rows, root_s, shear_s, inverse_s, main_s):
        older = None
        newer = None
        for i in range(wide):
            latest = tensor_parts(root_s[i], closed)
            if i >= 2:
                j = i - 2
                keep = inside_of(j, EDGE)
                if keep_rows is not None:
                    keep = keep * keep_rows
                total = [newer[0][k] + (latest[1][k] + older[1][k]) for k in range(4)]
                shear_s[0, j] = latest[2][0] - older[2][0]
                shear_s[1, j] = latest[2][1] - older[2][1]
                shear_s[2, j] = total[3]
                for k in range(3):
                    if main_s is not None and EDGE <= j < EDGE + cells:
                        main_s[k, j - EDGE] = total[k]
                    inverse_s[k, j] = keep / (total[k] + (1.0 - keep))
            older, newer = newer, latest

    def pushes(which, y_of, drive_s, inv_s, inverse_s, push_s):
        value, corner = case_values(which)
        patch = patch_of(y_of, corner)
        for j in range(wide - 2):
            free = 1.0 - value(3, j) * at_bottom
            push = (drive_s[j] + (value(4, j) * patch) * inv_s[j]) * free
            for k in range(3):
                push_s[k, j] = push * inverse_s[k, j] * value(k, j)
        return value

    def field_parts(w, closed):
        zs, zd = [], []
        for k in range(3):
            after = pltpu.roll(w[k], depth - 1, 2) * half_last_z
            before = pltpu.roll(w[k], 1, 2) * half_first_z
            zs.append(after + before)
            zd.append(after - before)
        mean = [w[k] + zs[k] for k in range(2)]
        mixed = [CROSS2 * w[k] + (2.0 * CROSS3) * zs[k] for k in range(2)]
        even_y = [plus(along_y(0.5 * mean[k] + mixed[k], closed)) for k in range(2)]
        odd_y = [minus(along_y(mixed[k], closed)) for k in range(2)]
        strong = [(2.0 * PAIR) * mean[k] + (AXIAL - 2.0 * PAIR) * w[k] for k in range(2)]
        upright = w[2] + (2.0 * PAIR) * zs[2]
        flat = FLAT * w[2] + (2.0 * FULL) * zs[2]
        twist_y = minus(along_y(zd[1], closed))
        spread_z, twist_z = both(along_y(zd[2], closed))
        slope_x = (2.0 * CROSS2) * zd[0] + (2.0 * CROSS3) * plus(along_y(zd[0], closed))
        slope_z = (2.0 * CROSS2) * zd[2] + (2.0 * CROSS3) * spread_z
        here = [
            plus(along_y(mean[0], closed)) + (zs[0] + zs[0]),
            plus(along_y(strong[1], closed)) + (zs[1] + zs[1]) + (2.0 * CROSS2) * twist_z,
            plus(along_y(upright, closed)) + (2.0 * AXIAL) * zs[2] + (2.0 * CROSS2) * twist_y,
        ]
        even = [
            strong[0] + even_y[0],
            mean[1] + even_y[1] + (2.0 * CROSS3) * twist_z,
            upright + plus(along_y(flat, closed)) + (2.0 * CROSS3) * twist_y,
        ]
        odd = [odd_y[1] + slope_z, odd_y[0], slope_x]
        ahead = [even[k] + odd[k] for k in range(3)]
        behind = [even[k] - odd[k] for k in range(3)]
        return here, ahead, behind

    def window_parts(w):
        zs, zd = [], []
        for k in range(3):
            after = pltpu.roll(w[k], depth - 1, 2) * half_last_z
            before = pltpu.roll(w[k], 1, 2) * half_first_z
            zs.append(after + before)
            zd.append(after - before)
        mean = [w[k] + zs[k] for k in range(2)]
        mixed = [CROSS2 * w[k] + (2.0 * CROSS3) * zs[k] for k in range(2)]
        lift = [0.5 * mean[k] + mixed[k] for k in range(2)]
        strong = [(2.0 * PAIR) * mean[k] + (AXIAL - 2.0 * PAIR) * w[k] for k in range(2)]
        upright = w[2] + (2.0 * PAIR) * zs[2]
        flat = FLAT * w[2] + (2.0 * FULL) * zs[2]
        edge = [(2.0 * CROSS2) * zd[k] for k in range(3)]
        tip = [(2.0 * CROSS3) * zd[k] for k in range(3)]
        here = [
            (zs[0] + zs[0], mean[0], None),
            (zs[1] + zs[1], strong[1], edge[2]),
            ((2.0 * AXIAL) * zs[2], upright, edge[1]),
        ]
        ahead = [
            (strong[0] + edge[2], lift[0] + tip[2], mixed[1]),
            (mean[1], lift[1], tip[2] + mixed[0]),
            (upright + edge[0], flat + tip[0], tip[1]),
        ]
        behind = [
            (strong[0] - edge[2], lift[0] - tip[2], -mixed[1]),
            (mean[1], lift[1], tip[2] - mixed[0]),
            (upright - edge[0], flat - tip[0], tip[1]),
        ]
        return tuple([term for row in part for term in row] for part in (here, ahead, behind))

    def window_sums(terms):
        sums = []
        for k in range(3):
            stays, even, odd = terms[3 * k : 3 * k + 3]
            after = along_y(even + odd, False)[0]
            before = along_y(even - odd, False)[1]
            sums.append(stays + after + before)
        return sums

    def slab_parts(w):
        return field_parts(w, True)

    def slab_sums(terms):
        return terms

    def joined(left, right):
        return [b if a is None else a + b for a, b in zip(left, right)]

    def sweep(
        parts, sums, count, load, keep, drive, value, store, root_s, push_s, inverse_s, shear_s
    ):
        offset = (wide - count) // 2
        partial = None
        trail = None
        free = None
        for i in range(count):
            held = free
            r = root_s[i + offset]
            if drive is not None:
                free = 1.0 - value(3, i + offset - 1) * at_bottom
                r = r * free
            here, ahead, behind = parts([r * load(k, i) for k in range(3)])
            if i >= 2:
                j = i - 1
                d = j + offset - 1
                old = [load(k, j) for k in range(3)]
                shear = [shear_s[k, d] for k in range(3)]
                rest = [
                    shear[0] * old[1] + shear[1] * old[2],
                    shear[0] * old[0] + shear[2] * old[2],
                    shear[1] * old[0] + shear[2] * old[1],
                ]
                total = sums(joined(partial, ahead))
                for k in range(3):
                    new = keep * old[k] + (total[k] - rest[k]) * inverse_s[k, d]
                    if drive is not None:
                        new = (new + drive * push_s[k, d]) * held
                    store(k, j - 1, new)
            if i >= 1:
                partial = joined(here, trail)
            trail = behind

    keep_second = (1.0 - omegas[1]) / omegas[1] + 1.0 / omegas[0]
    keep_third = (1.0 - omegas[2]) / omegas[2]
    drive_third = 1.0 / (omegas[0] * omegas[1])

    fold = rows // SUB
    inv_a = first_a.at[0]
    stiffness(fold, PAD, None, root_a, drive_a, inv_a, None)
    tensor(True, None, root_a, shear_a, inverse_a, None)
    value = pushes(case, lines_of(fold), drive_a, inv_a, inverse_a, push_a)

    def store_first_a(k, i, new):
        first_a[k, i] = new

    def store_third_a(k, i, new):
        for t in range(fold):
            third_n[k, i, pl.ds(PAD + t, SUB, stride=fold), :] = new[t]
            if 1 <= i <= cells:
                field_v[k, i - 1, pl.ds(t, SUB, stride=fold), :] = scale * new[t]

    arrays = (root_a, push_a, inverse_a, shear_a)
    whole = (slab_parts, slab_sums)
    sweep(
        *whole,
        wide - 2,
        lambda k, i: push_a[k, i],
        keep_second,
        None,
        value,
        store_first_a,
        *arrays,
    )
    sweep(
        *whole,
        wide - 4,
        lambda k, i: first_a[k, i],
        keep_third,
        drive_third,
        value,
        store_third_a,
        *arrays,
    )
    leaving = pltpu.make_async_copy(field_v, field_ref, gone.at[0])
    leaving.start()

    fold_b = result_n.shape[1] // SUB
    top = case * band - HALO
    y_of = top + lines_of(fold_b)
    keep_rows = ((y_of >= 0) & (y_of < rows)).astype(jnp.float32)
    inv_b = work_b.at[pl.ds(0, wide - 2)]
    stiffness(fold_b, PAD + top, keep_rows, root_b, drive_b, inv_b, factor_b)
    tensor(False, keep_rows, root_b, shear_b, inverse_b, main_b)
    gathered = work_b.at[pl.ds(wide - 2, cells)]
    window_only = (window_parts, window_sums)
    products = ((0, 0), (1, 1), (2, 2), (0, 1), (0, 2), (1, 2))

    def relax_other(which, slot):
        push_s = push_b.at[slot]
        first_s = first_b.at[slot]
        value = pushes(which, y_of, drive_b, inv_b, inverse_b, push_s)

        def store_first(k, i, new):
            first_s[k, i] = new

        def store_second(k, i, new):
            second_b[slot, k, i] = new

        arrays = (root_b, push_s, inverse_b, shear_b)
        sweep(
            *window_only,
            wide - 2,
            lambda k, i: push_s[k, i],
            keep_second,
            None,
            value,
            store_first,
            *arrays,
        )
        sweep(
            *window_only,
            wide - 4,
            lambda k, i: first_s[k, i],
            keep_third,
            drive_third,
            value,
            store_second,
            *arrays,
        )

    def add_energies(places, fresh):
        for i in range(cells + 2):
            sums = [None] * len(products)
            for slot in places:
                v = [second_b[slot, k, i] for k in range(3)]
                sums = joined(sums, [v[a] * v[b] for a, b in products])
            r = root_b[i + EDGE]
            for n, total in enumerate(sums):
                if fresh:
                    squares_b[n, i] = r * total
                else:
                    squares_b[n, i] += r * total
        for slot in places:
            partial = None
            trail = None
            for i in range(cells + 2):
                r = root_b[i + EDGE]
                here, ahead, behind = window_parts([r * second_b[slot, k, i] for k in range(3)])
                if i >= 2:
                    total = window_sums(joined(partial, ahead))
                    dot = [second_b[slot, k, i - 1] * total[k] for k in range(3)]
                    if fresh:
                        gathered[i - 2] = dot[0] + dot[1] + dot[2]
                    else:
                        gathered[i - 2] += dot[0] + dot[1] + dot[2]
                if i >= 1:
                    partial = joined(here, trail)
                trail = behind

    abreast = second_b.shape[0] - 1
    for k in range(3):
        for i in range(cells + 2):
            second_b[abreast, k, i] = jnp.stack(
                [third_n[k, i, pl.ds(PAD + top + t, SUB, stride=fold_b), :] for t in range(fold_b)]
            )
    add_energies([abreast], True)

    def add_others(start):
        for slot in range(abreast):
            relax_other(lax.rem(case + start + slot, groups), slot)
        add_energies(range(abreast), False)

    if groups - 1 == abreast:
        add_others(1)
    else:
        pl.loop(1, groups, step=abreast)(add_others)

    def square_parts(q):
        qxx, qyy, qzz, qxy, qxz, qyz = q
        s = qxx + qyy + qzz
        zs_s = plus(along_z(s))
        zs_x = plus(along_z(qxx))
        zs_z = plus(along_z(qzz))
        zs_xy = plus(along_z(qxy))
        zd_yz = minus(along_z(qyz))
        zd_xz = minus(along_z(qxz))
        twist = minus(along_y(zd_yz, False))
        half = 0.5 * zs_s + 0.125 * zs_z
        here = (
            zs_s
            + 0.5 * zs_z
            + plus(along_y(s + 0.5 * qyy + (PAIR * zs_s - 0.125 * zs_x), False))
            + 0.25 * twist
        )
        even = (
            s
            + 0.5 * qxx
            + half
            + 0.125 * zs_x
            + plus(along_y(0.5 * s + 0.125 * (qxx + qyy) + FULL * zs_s, False))
            + (1.0 / 12.0) * twist
        )
        odd = (
            minus(along_y(0.25 * qxy + (1.0 / 12.0) * zs_xy, False))
            + 0.25 * zd_xz
            + plus(along_y((1.0 / 12.0) * zd_xz, False))
        )
        return here, even + odd, even - odd

    partial = None
    trail = None
    for i in range(cells + 2):
        here, ahead, behind = square_parts([squares_b[n, i] for n in range(6)])
        if i >= 2:
            j = i - 2
            q = [squares_b[n, i - 1] for n in range(6)]
            d = j + EDGE
            held = main_b[0, j] * q[0] + main_b[1, j] * q[1] + main_b[2, j] * q[2]
            mixed = shear_b[0, d] * q[3] + shear_b[1, d] * q[4] + shear_b[2, d] * q[5]
            rest = partial + ahead - 2.0 * gathered[j]
            total = held + 2.0 * mixed + root_b[d + 1] * rest
            total = total * factor_b[j]
            for t in range(fold_b):
                result_n[j, pl.ds(t, SUB, stride=fold_b), :] = total[t]
        if i >= 1:
            partial = here + trail
        trail = behind
    sensitivity_ref[...] = result_n[:, HALO : HALO + band, :]
    leaving.wait()


def on_vmem():
    return pl.BlockSpec(memory_space=pltpu.VMEM)


def on_smem():
    return pl.BlockSpec(memory_space=pltpu.SMEM)


def solids(density, void_depth):
    cells, band, depth = density.shape
    return pl.pallas_call(
        solid_kernel,
        out_shape=[
            pltpu.VMEM((planes, band, depth), jnp.float32) for planes in (cells, HALO, HALO)
        ],
        in_specs=[pl.BlockSpec(memory_space=pltpu.HBM)] * 2,
        out_specs=[on_vmem()] * 3,
        scratch_shapes=[
            pltpu.VMEM(density.shape, jnp.float32),
            pltpu.VMEM(void_depth.shape, jnp.int32),
            pltpu.SemaphoreType.DMA((2,)),
        ],
    )(*(pltpu.with_memory_space_constraint(array, pltpu.HBM) for array in (density, void_depth)))


def settings(band, depth, supports, load_x, load_y, load_vectors):
    vectors = load_vectors.transpose(1, 0, 2)
    return pl.pallas_call(
        settings_kernel,
        out_shape=pltpu.VMEM((1, band, depth), jnp.float32),
        in_specs=[pl.BlockSpec(memory_space=pltpu.HBM)] * 2 + [on_smem()] * 2,
        out_specs=on_vmem(),
        scratch_shapes=[
            pltpu.SMEM(supports.shape, jnp.int32),
            pltpu.SMEM(vectors.shape, jnp.float32),
            pltpu.SemaphoreType.DMA((2,)),
        ],
    )(
        *(pltpu.with_memory_space_constraint(array, pltpu.HBM) for array in (supports, vectors)),
        load_x,
        load_y,
    )


def relaxed(bands):
    groups, planes, band, depth = bands.shape
    wide = planes - 1
    cells = wide - 2 * HALO
    rows = groups * band
    fold = rows // SUB
    fold_b = -(-(band + 2 * HALO) // SUB)
    tall = PAD + rows + fold_b * SUB
    abreast = ABREAST if (groups - 1) % ABREAST == 0 else 1

    def area(*lead):
        return pltpu.VMEM((*lead, fold, SUB, depth), jnp.float32)

    def window(*lead):
        return pltpu.VMEM((*lead, fold_b, SUB, depth), jnp.float32)

    return pl.pallas_call(
        relax_kernel,
        out_shape=(
            jax.ShapeDtypeStruct((3, cells, rows, depth), jnp.float32),
            jax.ShapeDtypeStruct((cells, band, depth), jnp.float32),
        ),
        in_specs=[on_vmem()],
        out_specs=(pl.BlockSpec(memory_space=pltpu.HBM), on_vmem()),
        scratch_shapes=[
            pltpu.VMEM((wide, tall, depth), jnp.float32),
            pltpu.VMEM((3, cells + 2, tall, depth), jnp.float32),
            pltpu.VMEM((cells, fold_b * SUB, depth), jnp.float32),
            area(wide),
            area(wide - 2),
            area(3, wide - 2),
            area(3, wide - 2),
            area(3, wide - 2),
            area(3, wide - 2),
            window(wide),
            window(wide - 2),
            window(abreast, 3, wide - 2),
            window(3, wide - 2),
            window(3, wide - 2),
            window(abreast, 3, wide - 4),
            window(3, cells),
            window(cells),
            window(abreast + 1, 3, cells + 2),
            window(6, cells + 2),
            window(wide - 2 + cells),
            pltpu.VMEM((3, cells, rows, depth), jnp.float32),
            pltpu.SemaphoreType.DMA((1,)),
        ],
        compiler_params=pltpu.CompilerParams(vmem_limit_bytes=32 * 1024 * 1024),
    )(bands)


def shards(density, void_depth, supports, load_x, load_y, load_vectors):
    cells, band, depth = density.shape
    groups = lax.axis_size("case")
    slabs = lax.axis_size("space")
    solid, near, far = solids(density, void_depth)
    across = [(i, i + 1) for i in range(1, slabs - 1, 2)]
    across += [(j, i) for i, j in across]
    inside = [(i, i + 1) for i in range(0, slabs, 2)]
    inside += [(j, i) for i, j in inside]
    first = lax.rem(lax.axis_index("space"), CORES) == 0
    inner = lax.ppermute(near, "space", inside)
    outer = lax.ppermute(far, "space", across)
    row = settings(band, depth, supports, load_x, load_y, load_vectors)
    second = jnp.logical_not(first)
    before = jnp.where(second, inner, outer)
    after = jnp.where(second, outer, inner)
    mine = jnp.concatenate([before, solid, after, row])
    mine = jnp.broadcast_to(mine[None], (groups, *mine.shape))
    bands = lax.all_to_all(mine, "case", split_axis=0, concat_axis=0, tiled=True)
    field, sensitivity = relaxed(bands)
    return (field[None], sensitivity)


def solution(mesh):
    return jax.shard_map(
        shards,
        mesh=mesh,
        in_specs=(
            P("space", "case", None),
            P("space", "case"),
            P("case", None),
            P("case"),
            P("case"),
            P("case", None, None),
        ),
        out_specs=(P("case", None, "space", None, None), P("space", "case", None)),
        check_vma=False,
    )
```

```python
import math

import jax
import jax.numpy as jnp
from jax import lax
from jax.experimental import pallas as pl
from jax.experimental.pallas import tpu as pltpu
from jax.sharding import PartitionSpec as P

SWEEPS = 3
LOADW = 8
EMIN = 0.001
LOWER = 0.06
UPPER = 3.0
PATCH = 4.0
SUB = 8
CORES = 2
ABREAST = 3
HALO = SWEEPS + 1
EDGE = HALO - 1
PAD = 8

AXIAL = 1.5
PAIR = 0.625
FLAT = 0.5
FULL = 0.25 * (1.0 + 0.5 / 3.0)
CROSS2 = 0.125
CROSS3 = 0.125 / 3.0


def relaxations(count):
    middle = 0.5 * (UPPER + LOWER)
    radius = 0.5 * (UPPER - LOWER)
    return [
        1.0 / (middle + radius * math.cos(math.pi * (2 * index + 1) / (2 * count)))
        for index in range(count)
    ]


def both(pair):
    return pair[0] + pair[1], pair[0] - pair[1]


def plus(pair):
    return pair[0] + pair[1]


def minus(pair):
    return pair[0] - pair[1]


def span_of(cells):
    return cells + 2 * EDGE


def solid_kernel(
    density_in, void_in, solid_ref, inner_ref, outer_ref, density_ref, void_ref, arrived
):
    fetches = [
        pltpu.make_async_copy(void_in, void_ref, arrived.at[0]),
        pltpu.make_async_copy(density_in, density_ref, arrived.at[1]),
    ]
    for fetch in fetches:
        fetch.start()
    cells, band, depth = solid_ref.shape
    first = lax.rem(lax.axis_index("space"), CORES) == 0
    level = lax.broadcasted_iota(jnp.int32, (band, depth), 1) - depth // 2
    eye = lax.broadcasted_iota(jnp.int32, (band, band), 0) == lax.broadcasted_iota(
        jnp.int32, (band, band), 1
    )
    for fetch in fetches:
        fetch.wait()
    for i in range(cells):
        line = jnp.broadcast_to(void_ref[i : i + 1, :], (band, band)).astype(jnp.float32)
        column = jnp.sum(jnp.where(eye, line, 0.0), axis=1, keepdims=True)
        top = jnp.broadcast_to(column, (band, depth)).astype(jnp.int32)
        hollow = (level >= 0) & (level < top)
        solid_ref[i] = jnp.where(hollow, 0.0, density_ref[i])
    for i in range(HALO):
        low = solid_ref[i]
        high = solid_ref[cells - HALO + i]
        outer_ref[i] = jnp.where(first, low, high)
        inner_ref[i] = jnp.where(first, high, low)


def settings_kernel(
    supports_in, vectors_in, load_x_ref, load_y_ref, row_ref, supports_ref, vectors_ref, arrived
):
    fetches = [
        pltpu.make_async_copy(supports_in, supports_ref, arrived.at[0]),
        pltpu.make_async_copy(vectors_in, vectors_ref, arrived.at[1]),
    ]
    for fetch in fetches:
        fetch.start()
    for fetch in fetches:
        fetch.wait()
    slabs = lax.axis_size("space")
    band, depth = row_ref.shape[1:]
    total_x = vectors_ref.shape[2]
    cells = total_x // slabs
    span = span_of(cells)
    first = lax.axis_index("space") * cells - EDGE
    lane = lax.broadcasted_iota(jnp.int32, (1, depth), 1)
    row = jnp.where(lane == 5 * span, load_y_ref[0].astype(jnp.float32), 0.0)
    for m in range(span):
        place = first + m
        inside = jnp.logical_and(place >= 0, place < total_x)
        where = jnp.clip(place, 0, total_x - 1)
        for k in range(3):
            value = jnp.where(inside, vectors_ref[k, 0, where], 0.0)
            row = jnp.where(lane == k * span + m, value, row)
    place = first + lane - 3 * span
    pinned = (place < supports_ref[0, 0]) | (place >= total_x - supports_ref[0, 1])
    row = jnp.where((lane >= 3 * span) & (lane < 4 * span) & pinned, 1.0, row)
    place = first + lane - 4 * span
    loaded = (place >= load_x_ref[0]) & (place < load_x_ref[0] + LOADW)
    row = jnp.where((lane >= 4 * span) & (lane < 5 * span) & loaded, 1.0, row)
    row_ref[0] = jnp.broadcast_to(row, (band, depth))


def relax_kernel(
    bands_ref,
    field_ref,
    sensitivity_ref,
    natural,
    third_n,
    result_n,
    root_a,
    drive_a,
    push_a,
    inverse_a,
    shear_a,
    first_a,
    root_b,
    drive_b,
    push_b,
    inverse_b,
    shear_b,
    first_b,
    main_b,
    factor_b,
    second_b,
    squares_b,
    work_b,
    field_v,
    gone,
):
    groups, planes, band, depth = bands_ref.shape
    wide = planes - 1
    cells = wide - 2 * HALO
    span = span_of(cells)
    rows = groups * band
    case = lax.axis_index("case")
    total_x = lax.axis_size("space") * cells
    first_plane = lax.axis_index("space") * cells
    omegas = relaxations(SWEEPS)
    scale = omegas[0] * omegas[1] * omegas[2]

    blank = jnp.zeros((PAD, depth), jnp.float32)
    for i in range(wide):
        natural[i, 0:PAD, :] = blank
        for at in range(PAD + rows, natural.shape[1], PAD):
            natural[i, at : at + PAD, :] = blank
    for k in range(3):
        for i in range(cells + 2):
            third_n[k, i, 0:PAD, :] = blank
            for at in range(PAD + rows, natural.shape[1], PAD):
                third_n[k, i, at : at + PAD, :] = blank
    for g in range(groups):
        natural[:, PAD + g * band : PAD + (g + 1) * band, :] = bands_ref[g, 0:wide]

    tile = (1, SUB, depth)
    lane = lax.broadcasted_iota(jnp.int32, tile, 2)
    line = lax.broadcasted_iota(jnp.int32, tile, 1)
    not_first_z = (lane > 0).astype(jnp.float32)
    not_last_z = (lane < depth - 1).astype(jnp.float32)
    not_first_s = (line > 0).astype(jnp.float32)
    not_last_s = (line < SUB - 1).astype(jnp.float32)
    at_bottom = (lane == 0).astype(jnp.float32)
    half_first_z = 0.5 * not_first_z
    half_last_z = 0.5 * not_last_z

    def along_z(a):
        after = pltpu.roll(a, depth - 1, 2) * not_last_z
        before = pltpu.roll(a, 1, 2) * not_first_z
        return after, before

    def along_y(a, closed):
        fold = a.shape[0]
        after = pltpu.roll(a[0:1], SUB - 1, 1)
        before = pltpu.roll(a[fold - 1 : fold], 1, 1)
        if closed:
            after = after * not_last_s
            before = before * not_first_s
        return (
            jnp.concatenate([a[1:], after], axis=0),
            jnp.concatenate([before, a[:-1]], axis=0),
        )

    def inside_of(plane, margin):
        place = first_plane - margin + plane
        return jnp.logical_and(place >= 0, place < total_x).astype(jnp.float32)

    def lines_of(fold):
        shape = (fold, SUB, depth)
        return fold * lax.broadcasted_iota(jnp.int32, shape, 1) + lax.broadcasted_iota(
            jnp.int32, shape, 0
        )

    def case_values(which):
        plain = jnp.broadcast_to(bands_ref[which, wide, 0:1, :], (SUB, depth))

        def value(kind, j):
            at = kind * span + j
            return jnp.broadcast_to(plain[:, at : at + 1], (SUB, depth))[None]

        corner = jnp.broadcast_to(plain[:, 5 * span : 5 * span + 1], (SUB, depth))[None]
        return value, corner

    def patch_of(y_of, corner):
        y = y_of.astype(jnp.float32)
        high = lax.broadcasted_iota(jnp.int32, y_of.shape, 2) == depth - 1
        return jnp.where(high & (y >= corner) & (y < corner + LOADW), PATCH, 0.0)

    def stiffness(fold, start, keep_rows, root_s, drive_s, inv_s, factor_s):
        for i in range(wide):
            solid = jnp.stack(
                [natural[i, pl.ds(start + t, SUB, stride=fold), :] for t in range(fold)]
            )
            stiff = EMIN + (1.0 - EMIN) * (solid * solid * solid)
            inv_root = lax.rsqrt(stiff)
            root = stiff * inv_root * inside_of(i, HALO)
            root_s[i] = root if keep_rows is None else root * keep_rows
            if 0 < i < wide - 1:
                drive_s[i - 1] = solid * inv_root
                inv_s[i - 1] = inv_root
            if factor_s is not None and HALO <= i < HALO + cells:
                ratio = solid * inv_root
                factor_s[i - HALO] = ((-1.5 * (1.0 - EMIN)) * scale * scale / groups) * (ratio * ratio)

    def tensor_parts(r, closed):
        zs, zd = both(along_z(r))
        ys, yd = both(along_y(r, closed))
        yszs, ydzs = both(along_y(zs, closed))
        yszd, ydzd = both(along_y(zd, closed))
        cross = ys + zs
        corner = PAIR * yszs
        here = [
            cross + FLAT * yszs,
            cross + 0.5 * ys + corner,
            cross + 0.5 * zs + corner,
            CROSS2 * ydzd,
        ]
        base = FULL * yszs + 0.5 * cross + r
        even = [
            base + 0.5 * r + 0.125 * cross,
            base + 0.125 * ys,
            base + 0.125 * zs,
            CROSS3 * ydzd,
        ]
        odd = [CROSS2 * yd + CROSS3 * ydzs, CROSS2 * zd + CROSS3 * yszd]
        return here, even, odd

    def tensor(closed, keep_rows, root_s, shear_s, inverse_s, main_s):
        older = None
        newer = None
        for i in range(wide):
            latest = tensor_parts(root_s[i], closed)
            if i >= 2:
                j = i - 2
                keep = inside_of(j, EDGE)
                if keep_rows is not None:
                    keep = keep * keep_rows
                total = [newer[0][k] + (latest[1][k] + older[1][k]) for k in range(4)]
                shear_s[0, j] = latest[2][0] - older[2][0]
                shear_s[1, j] = latest[2][1] - older[2][1]
                shear_s[2, j] = total[3]
                for k in range(3):
                    if main_s is not None and EDGE <= j < EDGE + cells:
                        main_s[k, j - EDGE] = total[k]
                    inverse_s[k, j] = keep / (total[k] + (1.0 - keep))
            older, newer = newer, latest

    def pushes(which, y_of, drive_s, inv_s, inverse_s, push_s):
        value, corner = case_values(which)
        patch = patch_of(y_of, corner)
        for j in range(wide - 2):
            free = 1.0 - value(3, j) * at_bottom
            push = (drive_s[j] + (value(4, j) * patch) * inv_s[j]) * free
            for k in range(3):
                push_s[k, j] = push * inverse_s[k, j] * value(k, j)
        return value

    def field_parts(w):
        zs, zd = [], []
        for k in range(3):
            after = pltpu.roll(w[k], depth - 1, 2) * half_last_z
            before = pltpu.roll(w[k], 1, 2) * half_first_z
            zs.append(after + before)
            zd.append(after - before)
        mean = [w[k] + zs[k] for k in range(2)]
        mixed = [CROSS2 * w[k] + (2.0 * CROSS3) * zs[k] for k in range(2)]
        lift = [0.5 * mean[k] + mixed[k] for k in range(2)]
        strong = [(2.0 * PAIR) * mean[k] + (AXIAL - 2.0 * PAIR) * w[k] for k in range(2)]
        upright = w[2] + (2.0 * PAIR) * zs[2]
        flat = FLAT * w[2] + (2.0 * FULL) * zs[2]
        edge = [(2.0 * CROSS2) * zd[k] for k in range(3)]
        tip = [(2.0 * CROSS3) * zd[k] for k in range(3)]
        here = [
            (zs[0] + zs[0], mean[0], None),
            (zs[1] + zs[1], strong[1], edge[2]),
            ((2.0 * AXIAL) * zs[2], upright, edge[1]),
        ]
        ahead = [
            (strong[0] + edge[2], lift[0] + tip[2], mixed[1]),
            (mean[1], lift[1], tip[2] + mixed[0]),
            (upright + edge[0], flat + tip[0], tip[1]),
        ]
        behind = [
            (strong[0] - edge[2], lift[0] - tip[2], -mixed[1]),
            (mean[1], lift[1], tip[2] - mixed[0]),
            (upright - edge[0], flat - tip[0], tip[1]),
        ]
        return tuple([term for row in part for term in row] for part in (here, ahead, behind))

    def field_sums(terms, closed):
        sums = []
        for k in range(3):
            stays, even, odd = terms[3 * k : 3 * k + 3]
            after = along_y(even + odd, closed)[0]
            before = along_y(even - odd, closed)[1]
            sums.append(stays + after + before)
        return sums

    def joined(left, right):
        return [b if a is None else a + b for a, b in zip(left, right)]

    def sweep(
        closed, count, load, keep, drive, value, store, root_s, push_s, inverse_s, shear_s
    ):
        offset = (wide - count) // 2
        partial = None
        trail = None
        free = None
        for i in range(count):
            held = free
            r = root_s[i + offset]
            if drive is not None:
                free = 1.0 - value(3, i + offset - 1) * at_bottom
                r = r * free
            here, ahead, behind = field_parts([r * load(k, i) for k in range(3)])
            if i >= 2:
                j = i - 1
                d = j + offset - 1
                old = [load(k, j) for k in range(3)]
                shear = [shear_s[k, d] for k in range(3)]
                rest = [
                    shear[0] * old[1] + shear[1] * old[2],
                    shear[0] * old[0] + shear[2] * old[2],
                    shear[1] * old[0] + shear[2] * old[1],
                ]
                total = field_sums(joined(partial, ahead), closed)
                for k in range(3):
                    new = keep * old[k] + (total[k] - rest[k]) * inverse_s[k, d]
                    if drive is not None:
                        new = (new + drive * push_s[k, d]) * held
                    store(k, j - 1, new)
            if i >= 1:
                partial = joined(here, trail)
            trail = behind

    keep_second = (1.0 - omegas[1]) / omegas[1] + 1.0 / omegas[0]
    keep_third = (1.0 - omegas[2]) / omegas[2]
    drive_third = 1.0 / (omegas[0] * omegas[1])

    fold = rows // SUB
    inv_a = first_a.at[0]
    stiffness(fold, PAD, None, root_a, drive_a, inv_a, None)
    tensor(True, None, root_a, shear_a, inverse_a, None)
    value = pushes(case, lines_of(fold), drive_a, inv_a, inverse_a, push_a)

    def store_first_a(k, i, new):
        first_a[k, i] = new

    def store_third_a(k, i, new):
        for t in range(fold):
            third_n[k, i, pl.ds(PAD + t, SUB, stride=fold), :] = new[t]
            if 1 <= i <= cells:
                field_v[k, i - 1, pl.ds(t, SUB, stride=fold), :] = scale * new[t]

    arrays = (root_a, push_a, inverse_a, shear_a)
    sweep(
        True,
        wide - 2,
        lambda k, i: push_a[k, i],
        keep_second,
        None,
        value,
        store_first_a,
        *arrays,
    )
    sweep(
        True,
        wide - 4,
        lambda k, i: first_a[k, i],
        keep_third,
        drive_third,
        value,
        store_third_a,
        *arrays,
    )
    leaving = pltpu.make_async_copy(field_v, field_ref, gone.at[0])
    leaving.start()

    fold_b = result_n.shape[1] // SUB
    top = case * band - HALO
    y_of = top + lines_of(fold_b)
    keep_rows = ((y_of >= 0) & (y_of < rows)).astype(jnp.float32)
    inv_b = work_b.at[pl.ds(0, wide - 2)]
    stiffness(fold_b, PAD + top, keep_rows, root_b, drive_b, inv_b, factor_b)
    tensor(False, keep_rows, root_b, shear_b, inverse_b, main_b)
    gathered = work_b.at[pl.ds(wide - 2, cells)]
    products = ((0, 0), (1, 1), (2, 2), (0, 1), (0, 2), (1, 2))

    def relax_other(which, slot):
        push_s = push_b.at[slot]
        first_s = first_b.at[slot]
        value = pushes(which, y_of, drive_b, inv_b, inverse_b, push_s)

        def store_first(k, i, new):
            first_s[k, i] = new

        def store_second(k, i, new):
            second_b[slot, k, i] = new

        arrays = (root_b, push_s, inverse_b, shear_b)
        sweep(
            False,
            wide - 2,
            lambda k, i: push_s[k, i],
            keep_second,
            None,
            value,
            store_first,
            *arrays,
        )
        sweep(
            False,
            wide - 4,
            lambda k, i: first_s[k, i],
            keep_third,
            drive_third,
            value,
            store_second,
            *arrays,
        )

    def add_energies(places, fresh):
        for i in range(cells + 2):
            sums = [None] * len(products)
            for slot in places:
                v = [second_b[slot, k, i] for k in range(3)]
                sums = joined(sums, [v[a] * v[b] for a, b in products])
            r = root_b[i + EDGE]
            for n, total in enumerate(sums):
                if fresh:
                    squares_b[n, i] = r * total
                else:
                    squares_b[n, i] += r * total
        for slot in places:
            partial = None
            trail = None
            for i in range(cells + 2):
                r = root_b[i + EDGE]
                here, ahead, behind = field_parts([r * second_b[slot, k, i] for k in range(3)])
                if i >= 2:
                    total = field_sums(joined(partial, ahead), False)
                    dot = [second_b[slot, k, i - 1] * total[k] for k in range(3)]
                    if fresh:
                        gathered[i - 2] = dot[0] + dot[1] + dot[2]
                    else:
                        gathered[i - 2] += dot[0] + dot[1] + dot[2]
                if i >= 1:
                    partial = joined(here, trail)
                trail = behind

    abreast = second_b.shape[0] - 1
    for k in range(3):
        for i in range(cells + 2):
            second_b[abreast, k, i] = jnp.stack(
                [third_n[k, i, pl.ds(PAD + top + t, SUB, stride=fold_b), :] for t in range(fold_b)]
            )
    add_energies([abreast], True)

    def add_others(start):
        for slot in range(abreast):
            relax_other(lax.rem(case + start + slot, groups), slot)
        add_energies(range(abreast), False)

    if groups - 1 == abreast:
        add_others(1)
    else:
        pl.loop(1, groups, step=abreast)(add_others)

    def square_parts(q):
        qxx, qyy, qzz, qxy, qxz, qyz = q
        s = qxx + qyy + qzz
        zs_s = plus(along_z(s))
        zs_x = plus(along_z(qxx))
        zs_z = plus(along_z(qzz))
        zs_xy = plus(along_z(qxy))
        zd_yz = minus(along_z(qyz))
        zd_xz = minus(along_z(qxz))
        twist = minus(along_y(zd_yz, False))
        half = 0.5 * zs_s + 0.125 * zs_z
        here = (
            zs_s
            + 0.5 * zs_z
            + plus(along_y(s + 0.5 * qyy + (PAIR * zs_s - 0.125 * zs_x), False))
            + 0.25 * twist
        )
        even = (
            s
            + 0.5 * qxx
            + half
            + 0.125 * zs_x
            + plus(along_y(0.5 * s + 0.125 * (qxx + qyy) + FULL * zs_s, False))
            + (1.0 / 12.0) * twist
        )
        odd = (
            minus(along_y(0.25 * qxy + (1.0 / 12.0) * zs_xy, False))
            + 0.25 * zd_xz
            + plus(along_y((1.0 / 12.0) * zd_xz, False))
        )
        return here, even + odd, even - odd

    partial = None
    trail = None
    for i in range(cells + 2):
        here, ahead, behind = square_parts([squares_b[n, i] for n in range(6)])
        if i >= 2:
            j = i - 2
            q = [squares_b[n, i - 1] for n in range(6)]
            d = j + EDGE
            held = main_b[0, j] * q[0] + main_b[1, j] * q[1] + main_b[2, j] * q[2]
            mixed = shear_b[0, d] * q[3] + shear_b[1, d] * q[4] + shear_b[2, d] * q[5]
            rest = partial + ahead - 2.0 * gathered[j]
            total = held + 2.0 * mixed + root_b[d + 1] * rest
            total = total * factor_b[j]
            for t in range(fold_b):
                result_n[j, pl.ds(t, SUB, stride=fold_b), :] = total[t]
        if i >= 1:
            partial = here + trail
        trail = behind
    sensitivity_ref[...] = result_n[:, HALO : HALO + band, :]
    leaving.wait()


def on_vmem():
    return pl.BlockSpec(memory_space=pltpu.VMEM)


def on_smem():
    return pl.BlockSpec(memory_space=pltpu.SMEM)


def solids(density, void_depth):
    cells, band, depth = density.shape
    return pl.pallas_call(
        solid_kernel,
        out_shape=[
            pltpu.VMEM((planes, band, depth), jnp.float32) for planes in (cells, HALO, HALO)
        ],
        in_specs=[pl.BlockSpec(memory_space=pltpu.HBM)] * 2,
        out_specs=[on_vmem()] * 3,
        scratch_shapes=[
            pltpu.VMEM(density.shape, jnp.float32),
            pltpu.VMEM(void_depth.shape, jnp.int32),
            pltpu.SemaphoreType.DMA((2,)),
        ],
    )(*(pltpu.with_memory_space_constraint(array, pltpu.HBM) for array in (density, void_depth)))


def settings(band, depth, supports, load_x, load_y, load_vectors):
    vectors = load_vectors.transpose(1, 0, 2)
    return pl.pallas_call(
        settings_kernel,
        out_shape=pltpu.VMEM((1, band, depth), jnp.float32),
        in_specs=[pl.BlockSpec(memory_space=pltpu.HBM)] * 2 + [on_smem()] * 2,
        out_specs=on_vmem(),
        scratch_shapes=[
            pltpu.SMEM(supports.shape, jnp.int32),
            pltpu.SMEM(vectors.shape, jnp.float32),
            pltpu.SemaphoreType.DMA((2,)),
        ],
    )(
        *(pltpu.with_memory_space_constraint(array, pltpu.HBM) for array in (supports, vectors)),
        load_x,
        load_y,
    )


def relaxed(bands):
    groups, planes, band, depth = bands.shape
    wide = planes - 1
    cells = wide - 2 * HALO
    rows = groups * band
    fold = rows // SUB
    fold_b = -(-(band + 2 * HALO) // SUB)
    tall = PAD + rows + fold_b * SUB
    abreast = ABREAST if (groups - 1) % ABREAST == 0 else 1

    def area(*lead):
        return pltpu.VMEM((*lead, fold, SUB, depth), jnp.float32)

    def window(*lead):
        return pltpu.VMEM((*lead, fold_b, SUB, depth), jnp.float32)

    return pl.pallas_call(
        relax_kernel,
        out_shape=(
            jax.ShapeDtypeStruct((3, cells, rows, depth), jnp.float32),
            jax.ShapeDtypeStruct((cells, band, depth), jnp.float32),
        ),
        in_specs=[on_vmem()],
        out_specs=(pl.BlockSpec(memory_space=pltpu.HBM), on_vmem()),
        scratch_shapes=[
            pltpu.VMEM((wide, tall, depth), jnp.float32),
            pltpu.VMEM((3, cells + 2, tall, depth), jnp.float32),
            pltpu.VMEM((cells, fold_b * SUB, depth), jnp.float32),
            area(wide),
            area(wide - 2),
            area(3, wide - 2),
            area(3, wide - 2),
            area(3, wide - 2),
            area(3, wide - 2),
            window(wide),
            window(wide - 2),
            window(abreast, 3, wide - 2),
            window(3, wide - 2),
            window(3, wide - 2),
            window(abreast, 3, wide - 4),
            window(3, cells),
            window(cells),
            window(abreast + 1, 3, cells + 2),
            window(6, cells + 2),
            window(wide - 2 + cells),
            pltpu.VMEM((3, cells, rows, depth), jnp.float32),
            pltpu.SemaphoreType.DMA((1,)),
        ],
        compiler_params=pltpu.CompilerParams(vmem_limit_bytes=32 * 1024 * 1024),
    )(bands)


def shards(density, void_depth, supports, load_x, load_y, load_vectors):
    cells, band, depth = density.shape
    groups = lax.axis_size("case")
    slabs = lax.axis_size("space")
    solid, near, far = solids(density, void_depth)
    across = [(i, i + 1) for i in range(1, slabs - 1, 2)]
    across += [(j, i) for i, j in across]
    inside = [(i, i + 1) for i in range(0, slabs, 2)]
    inside += [(j, i) for i, j in inside]
    first = lax.rem(lax.axis_index("space"), CORES) == 0
    inner = lax.ppermute(near, "space", inside)
    outer = lax.ppermute(far, "space", across)
    row = settings(band, depth, supports, load_x, load_y, load_vectors)
    second = jnp.logical_not(first)
    before = jnp.where(second, inner, outer)
    after = jnp.where(second, outer, inner)
    mine = jnp.concatenate([before, solid, after, row])
    mine = jnp.broadcast_to(mine[None], (groups, *mine.shape))
    bands = lax.all_to_all(mine, "case", split_axis=0, concat_axis=0, tiled=True)
    field, sensitivity = relaxed(bands)
    return (field[None], sensitivity)


def solution(mesh):
    return jax.shard_map(
        shards,
        mesh=mesh,
        in_specs=(
            P("space", "case", None),
            P("space", "case"),
            P("case", None),
            P("case"),
            P("case"),
            P("case", None, None),
        ),
        out_specs=(P("case", None, "space", None, None), P("space", "case", None)),
        check_vma=False,
    )
```

```python
import math

import jax
import jax.numpy as jnp
from jax import lax
from jax.experimental import pallas as pl
from jax.experimental.pallas import tpu as pltpu
from jax.sharding import PartitionSpec as P

SWEEPS = 3
LOADW = 8
EMIN = 0.001
LOWER = 0.06
UPPER = 3.0
PATCH = 4.0
SUB = 8
CORES = 2
ABREAST = 3
HALO = SWEEPS + 1
EDGE = HALO - 1
PAD = 8

AXIAL = 1.5
PAIR = 0.625
FLAT = 0.5
FULL = 0.25 * (1.0 + 0.5 / 3.0)
CROSS2 = 0.125
CROSS3 = 0.125 / 3.0


def relaxations(count):
    middle = 0.5 * (UPPER + LOWER)
    radius = 0.5 * (UPPER - LOWER)
    return [
        1.0 / (middle + radius * math.cos(math.pi * (2 * index + 1) / (2 * count)))
        for index in range(count)
    ]


def both(pair):
    return pair[0] + pair[1], pair[0] - pair[1]


def plus(pair):
    return pair[0] + pair[1]


def minus(pair):
    return pair[0] - pair[1]


def span_of(cells):
    return cells + 2 * EDGE


def solid_kernel(
    density_in, void_in, solid_ref, inner_ref, outer_ref, density_ref, void_ref, arrived
):
    fetches = [
        pltpu.make_async_copy(void_in, void_ref, arrived.at[0]),
        pltpu.make_async_copy(density_in, density_ref, arrived.at[1]),
    ]
    for fetch in fetches:
        fetch.start()
    cells, band, depth = solid_ref.shape
    first = lax.rem(lax.axis_index("space"), CORES) == 0
    level = lax.broadcasted_iota(jnp.int32, (band, depth), 1) - depth // 2
    eye = lax.broadcasted_iota(jnp.int32, (band, band), 0) == lax.broadcasted_iota(
        jnp.int32, (band, band), 1
    )
    for fetch in fetches:
        fetch.wait()
    for i in range(cells):
        line = jnp.broadcast_to(void_ref[i : i + 1, :], (band, band)).astype(jnp.float32)
        column = jnp.sum(jnp.where(eye, line, 0.0), axis=1, keepdims=True)
        top = jnp.broadcast_to(column, (band, depth)).astype(jnp.int32)
        hollow = (level >= 0) & (level < top)
        solid_ref[i] = jnp.where(hollow, 0.0, density_ref[i])
    for i in range(HALO):
        low = solid_ref[i]
        high = solid_ref[cells - HALO + i]
        outer_ref[i] = jnp.where(first, low, high)
        inner_ref[i] = jnp.where(first, high, low)


def settings_kernel(
    supports_in, vectors_in, load_x_ref, load_y_ref, row_ref, supports_ref, vectors_ref, arrived
):
    fetches = [
        pltpu.make_async_copy(supports_in, supports_ref, arrived.at[0]),
        pltpu.make_async_copy(vectors_in, vectors_ref, arrived.at[1]),
    ]
    for fetch in fetches:
        fetch.start()
    for fetch in fetches:
        fetch.wait()
    slabs = lax.axis_size("space")
    band, depth = row_ref.shape[1:]
    total_x = vectors_ref.shape[2]
    cells = total_x // slabs
    span = span_of(cells)
    first = lax.axis_index("space") * cells - EDGE
    lane = lax.broadcasted_iota(jnp.int32, (1, depth), 1)
    row = jnp.where(lane == 5 * span, load_y_ref[0].astype(jnp.float32), 0.0)
    for m in range(span):
        place = first + m
        inside = jnp.logical_and(place >= 0, place < total_x)
        where = jnp.clip(place, 0, total_x - 1)
        for k in range(3):
            value = jnp.where(inside, vectors_ref[k, 0, where], 0.0)
            row = jnp.where(lane == k * span + m, value, row)
    place = first + lane - 3 * span
    pinned = (place < supports_ref[0, 0]) | (place >= total_x - supports_ref[0, 1])
    row = jnp.where((lane >= 3 * span) & (lane < 4 * span) & pinned, 1.0, row)
    place = first + lane - 4 * span
    loaded = (place >= load_x_ref[0]) & (place < load_x_ref[0] + LOADW)
    row = jnp.where((lane >= 4 * span) & (lane < 5 * span) & loaded, 1.0, row)
    row_ref[0] = jnp.broadcast_to(row, (band, depth))


def relax_kernel(
    bands_ref,
    field_ref,
    sensitivity_ref,
    natural,
    third_n,
    result_n,
    root_a,
    drive_a,
    push_a,
    inverse_a,
    shear_a,
    first_a,
    root_b,
    drive_b,
    push_b,
    inverse_b,
    shear_b,
    first_b,
    main_b,
    factor_b,
    second_b,
    squares_b,
    work_b,
    field_v,
    gone,
):
    groups, planes, band, depth = bands_ref.shape
    wide = planes - 1
    cells = wide - 2 * HALO
    span = span_of(cells)
    rows = groups * band
    case = lax.axis_index("case")
    total_x = lax.axis_size("space") * cells
    first_plane = lax.axis_index("space") * cells
    omegas = relaxations(SWEEPS)
    scale = omegas[0] * omegas[1] * omegas[2]

    blank = jnp.zeros((PAD, depth), jnp.float32)
    for i in range(wide):
        natural[i, 0:PAD, :] = blank
        for at in range(PAD + rows, natural.shape[1], PAD):
            natural[i, at : at + PAD, :] = blank
    for k in range(3):
        for i in range(cells + 2):
            third_n[k, i, 0:PAD, :] = blank
            for at in range(PAD + rows, natural.shape[1], PAD):
                third_n[k, i, at : at + PAD, :] = blank
    for g in range(groups):
        natural[:, PAD + g * band : PAD + (g + 1) * band, :] = bands_ref[g, 0:wide]

    tile = (1, SUB, depth)
    lane = lax.broadcasted_iota(jnp.int32, tile, 2)
    line = lax.broadcasted_iota(jnp.int32, tile, 1)
    not_first_z = (lane > 0).astype(jnp.float32)
    not_last_z = (lane < depth - 1).astype(jnp.float32)
    not_first_s = (line > 0).astype(jnp.float32)
    not_last_s = (line < SUB - 1).astype(jnp.float32)
    at_bottom = (lane == 0).astype(jnp.float32)
    half_first_z = 0.5 * not_first_z
    half_last_z = 0.5 * not_last_z

    def along_z(a):
        after = pltpu.roll(a, depth - 1, 2) * not_last_z
        before = pltpu.roll(a, 1, 2) * not_first_z
        return after, before

    def along_y(a, closed):
        fold = a.shape[0]
        after = pltpu.roll(a[0:1], SUB - 1, 1)
        before = pltpu.roll(a[fold - 1 : fold], 1, 1)
        if closed:
            after = after * not_last_s
            before = before * not_first_s
        return (
            jnp.concatenate([a[1:], after], axis=0),
            jnp.concatenate([before, a[:-1]], axis=0),
        )

    def inside_of(plane, margin):
        place = first_plane - margin + plane
        return jnp.logical_and(place >= 0, place < total_x).astype(jnp.float32)

    def lines_of(fold):
        shape = (fold, SUB, depth)
        return fold * lax.broadcasted_iota(jnp.int32, shape, 1) + lax.broadcasted_iota(
            jnp.int32, shape, 0
        )

    def case_values(which):
        plain = jnp.broadcast_to(bands_ref[which, wide, 0:1, :], (SUB, depth))

        def value(kind, j):
            at = kind * span + j
            return jnp.broadcast_to(plain[:, at : at + 1], (SUB, depth))[None]

        corner = jnp.broadcast_to(plain[:, 5 * span : 5 * span + 1], (SUB, depth))[None]
        return value, corner

    def patch_of(y_of, corner):
        y = y_of.astype(jnp.float32)
        high = lax.broadcasted_iota(jnp.int32, y_of.shape, 2) == depth - 1
        return jnp.where(high & (y >= corner) & (y < corner + LOADW), PATCH, 0.0)

    def stiffness(fold, start, keep_rows, root_s, drive_s, inv_s, factor_s):
        for i in range(wide):
            solid = jnp.stack(
                [natural[i, pl.ds(start + t, SUB, stride=fold), :] for t in range(fold)]
            )
            stiff = EMIN + (1.0 - EMIN) * (solid * solid * solid)
            inv_root = lax.rsqrt(stiff)
            root = stiff * inv_root * inside_of(i, HALO)
            root_s[i] = root if keep_rows is None else root * keep_rows
            if 0 < i < wide - 1:
                drive_s[i - 1] = solid * inv_root
                inv_s[i - 1] = inv_root
            if factor_s is not None and HALO <= i < HALO + cells:
                ratio = solid * inv_root
                factor_s[i - HALO] = ((-1.5 * (1.0 - EMIN)) * scale * scale / groups) * (ratio * ratio)

    def tensor_parts(r, closed):
        zs, zd = both(along_z(r))
        ys, yd = both(along_y(r, closed))
        yszs, ydzs = both(along_y(zs, closed))
        yszd, ydzd = both(along_y(zd, closed))
        cross = ys + zs
        corner = PAIR * yszs
        here = [
            cross + FLAT * yszs,
            cross + 0.5 * ys + corner,
            cross + 0.5 * zs + corner,
            CROSS2 * ydzd,
        ]
        base = FULL * yszs + 0.5 * cross + r
        even = [
            base + 0.5 * r + 0.125 * cross,
            base + 0.125 * ys,
            base + 0.125 * zs,
            CROSS3 * ydzd,
        ]
        odd = [CROSS2 * yd + CROSS3 * ydzs, CROSS2 * zd + CROSS3 * yszd]
        return here, even, odd

    def tensor(closed, keep_rows, root_s, shear_s, inverse_s, main_s):
        older = None
        newer = None
        for i in range(wide):
            latest = tensor_parts(root_s[i], closed)
            if i >= 2:
                j = i - 2
                keep = inside_of(j, EDGE)
                if keep_rows is not None:
                    keep = keep * keep_rows
                total = [newer[0][k] + (latest[1][k] + older[1][k]) for k in range(4)]
                shear_s[0, j] = latest[2][0] - older[2][0]
                shear_s[1, j] = latest[2][1] - older[2][1]
                shear_s[2, j] = total[3]
                for k in range(3):
                    if main_s is not None and EDGE <= j < EDGE + cells:
                        main_s[k, j - EDGE] = total[k]
                    inverse_s[k, j] = keep / (total[k] + (1.0 - keep))
            older, newer = newer, latest

    def pushes(which, y_of, drive_s, inv_s, inverse_s, push_s):
        value, corner = case_values(which)
        patch = patch_of(y_of, corner)
        for j in range(wide - 2):
            free = 1.0 - value(3, j) * at_bottom
            push = (drive_s[j] + (value(4, j) * patch) * inv_s[j]) * free
            for k in range(3):
                push_s[k, j] = push * inverse_s[k, j] * value(k, j)
        return value

    def field_parts(w):
        zs, zd = [], []
        for k in range(3):
            after = pltpu.roll(w[k], depth - 1, 2) * half_last_z
            before = pltpu.roll(w[k], 1, 2) * half_first_z
            zs.append(after + before)
            zd.append(after - before)
        mean = [w[k] + zs[k] for k in range(2)]
        mixed = [CROSS2 * w[k] + (2.0 * CROSS3) * zs[k] for k in range(2)]
        lift = [0.5 * mean[k] + mixed[k] for k in range(2)]
        strong = [(2.0 * PAIR) * mean[k] + (AXIAL - 2.0 * PAIR) * w[k] for k in range(2)]
        upright = w[2] + (2.0 * PAIR) * zs[2]
        flat = FLAT * w[2] + (2.0 * FULL) * zs[2]
        edge = [(2.0 * CROSS2) * zd[k] for k in range(3)]
        tip = [(2.0 * CROSS3) * zd[k] for k in range(3)]
        here = [
            (zs[0] + zs[0], mean[0], None),
            (zs[1] + zs[1], strong[1], edge[2]),
            ((2.0 * AXIAL) * zs[2], upright, edge[1]),
        ]
        ahead = [
            (strong[0] + edge[2], lift[0] + tip[2], mixed[1]),
            (mean[1], lift[1], tip[2] + mixed[0]),
            (upright + edge[0], flat + tip[0], tip[1]),
        ]
        behind = [
            (strong[0] - edge[2], lift[0] - tip[2], -mixed[1]),
            (mean[1], lift[1], tip[2] - mixed[0]),
            (upright - edge[0], flat - tip[0], tip[1]),
        ]
        return tuple([term for row in part for term in row] for part in (here, ahead, behind))

    def field_sums(terms, closed):
        sums = []
        for k in range(3):
            stays, even, odd = terms[3 * k : 3 * k + 3]
            after = along_y(even + odd, closed)[0]
            before = along_y(even - odd, closed)[1]
            sums.append(stays + after + before)
        return sums

    def joined(left, right):
        return [b if a is None else a + b for a, b in zip(left, right)]

    def sweep(
        closed, count, load, keep, drive, value, store, root_s, push_s, inverse_s, shear_s
    ):
        offset = (wide - count) // 2
        partial = None
        trail = None
        free = None
        for i in range(count):
            held = free
            r = root_s[i + offset]
            if drive is not None:
                free = 1.0 - value(3, i + offset - 1) * at_bottom
                r = r * free
            here, ahead, behind = field_parts([r * load(k, i) for k in range(3)])
            if i >= 2:
                j = i - 1
                d = j + offset - 1
                old = [load(k, j) for k in range(3)]
                shear = [shear_s[k, d] for k in range(3)]
                rest = [
                    shear[0] * old[1] + shear[1] * old[2],
                    shear[0] * old[0] + shear[2] * old[2],
                    shear[1] * old[0] + shear[2] * old[1],
                ]
                total = field_sums(joined(partial, ahead), closed)
                for k in range(3):
                    new = keep * old[k] + (total[k] - rest[k]) * inverse_s[k, d]
                    if drive is not None:
                        new = (new + drive * push_s[k, d]) * held
                    store(k, j - 1, new)
            if i >= 1:
                partial = joined(here, trail)
            trail = behind
            yield

    def together(sweeps):
        for _ in zip(*sweeps):
            pass

    keep_second = (1.0 - omegas[1]) / omegas[1] + 1.0 / omegas[0]
    keep_third = (1.0 - omegas[2]) / omegas[2]
    drive_third = 1.0 / (omegas[0] * omegas[1])

    fold = rows // SUB
    inv_a = first_a.at[0]
    stiffness(fold, PAD, None, root_a, drive_a, inv_a, None)
    tensor(True, None, root_a, shear_a, inverse_a, None)
    value = pushes(case, lines_of(fold), drive_a, inv_a, inverse_a, push_a)

    def store_first_a(k, i, new):
        first_a[k, i] = new

    def store_third_a(k, i, new):
        for t in range(fold):
            third_n[k, i, pl.ds(PAD + t, SUB, stride=fold), :] = new[t]
            if 1 <= i <= cells:
                field_v[k, i - 1, pl.ds(t, SUB, stride=fold), :] = scale * new[t]

    arrays = (root_a, push_a, inverse_a, shear_a)
    first_sweep = sweep(
        True,
        wide - 2,
        lambda k, i: push_a[k, i],
        keep_second,
        None,
        value,
        store_first_a,
        *arrays,
    )
    second_sweep = sweep(
        True,
        wide - 4,
        lambda k, i: first_a[k, i],
        keep_third,
        drive_third,
        value,
        store_third_a,
        *arrays,
    )
    together([first_sweep])
    together([second_sweep])
    leaving = pltpu.make_async_copy(field_v, field_ref, gone.at[0])
    leaving.start()

    fold_b = result_n.shape[1] // SUB
    top = case * band - HALO
    y_of = top + lines_of(fold_b)
    keep_rows = ((y_of >= 0) & (y_of < rows)).astype(jnp.float32)
    inv_b = work_b.at[pl.ds(0, wide - 2)]
    stiffness(fold_b, PAD + top, keep_rows, root_b, drive_b, inv_b, factor_b)
    tensor(False, keep_rows, root_b, shear_b, inverse_b, main_b)
    gathered = work_b.at[pl.ds(wide - 2, cells)]
    products = ((0, 0), (1, 1), (2, 2), (0, 1), (0, 2), (1, 2))

    def sweeps_other(which, slot):
        push_s = push_b.at[slot]
        first_s = first_b.at[slot]
        value = pushes(which, y_of, drive_b, inv_b, inverse_b, push_s)

        def store_first(k, i, new):
            first_s[k, i] = new

        def store_second(k, i, new):
            second_b[slot, k, i] = new

        arrays = (root_b, push_s, inverse_b, shear_b)
        first_sweep = sweep(
            False,
            wide - 2,
            lambda k, i: push_s[k, i],
            keep_second,
            None,
            value,
            store_first,
            *arrays,
        )
        second_sweep = sweep(
            False,
            wide - 4,
            lambda k, i: first_s[k, i],
            keep_third,
            drive_third,
            value,
            store_second,
            *arrays,
        )
        return first_sweep, second_sweep

    def add_energies(places, fresh):
        for i in range(cells + 2):
            sums = [None] * len(products)
            for slot in places:
                v = [second_b[slot, k, i] for k in range(3)]
                sums = joined(sums, [v[a] * v[b] for a, b in products])
            r = root_b[i + EDGE]
            for n, total in enumerate(sums):
                if fresh:
                    squares_b[n, i] = r * total
                else:
                    squares_b[n, i] += r * total
        for slot in places:
            partial = None
            trail = None
            for i in range(cells + 2):
                r = root_b[i + EDGE]
                here, ahead, behind = field_parts([r * second_b[slot, k, i] for k in range(3)])
                if i >= 2:
                    total = field_sums(joined(partial, ahead), False)
                    dot = [second_b[slot, k, i - 1] * total[k] for k in range(3)]
                    if fresh:
                        gathered[i - 2] = dot[0] + dot[1] + dot[2]
                    else:
                        gathered[i - 2] += dot[0] + dot[1] + dot[2]
                if i >= 1:
                    partial = joined(here, trail)
                trail = behind

    abreast = second_b.shape[0] - 1
    for k in range(3):
        for i in range(cells + 2):
            second_b[abreast, k, i] = jnp.stack(
                [third_n[k, i, pl.ds(PAD + top + t, SUB, stride=fold_b), :] for t in range(fold_b)]
            )
    add_energies([abreast], True)

    def add_others(start):
        pairs = [
            sweeps_other(lax.rem(case + start + slot, groups), slot) for slot in range(abreast)
        ]
        for sweeps in zip(*pairs):
            together(sweeps)
        add_energies(range(abreast), False)

    if groups - 1 == abreast:
        add_others(1)
    else:
        pl.loop(1, groups, step=abreast)(add_others)

    def square_parts(q):
        qxx, qyy, qzz, qxy, qxz, qyz = q
        s = qxx + qyy + qzz
        zs_s = plus(along_z(s))
        zs_x = plus(along_z(qxx))
        zs_z = plus(along_z(qzz))
        zs_xy = plus(along_z(qxy))
        zd_yz = minus(along_z(qyz))
        zd_xz = minus(along_z(qxz))
        twist = minus(along_y(zd_yz, False))
        half = 0.5 * zs_s + 0.125 * zs_z
        here = (
            zs_s
            + 0.5 * zs_z
            + plus(along_y(s + 0.5 * qyy + (PAIR * zs_s - 0.125 * zs_x), False))
            + 0.25 * twist
        )
        even = (
            s
            + 0.5 * qxx
            + half
            + 0.125 * zs_x
            + plus(along_y(0.5 * s + 0.125 * (qxx + qyy) + FULL * zs_s, False))
            + (1.0 / 12.0) * twist
        )
        odd = (
            minus(along_y(0.25 * qxy + (1.0 / 12.0) * zs_xy, False))
            + 0.25 * zd_xz
            + plus(along_y((1.0 / 12.0) * zd_xz, False))
        )
        return here, even + odd, even - odd

    partial = None
    trail = None
    for i in range(cells + 2):
        here, ahead, behind = square_parts([squares_b[n, i] for n in range(6)])
        if i >= 2:
            j = i - 2
            q = [squares_b[n, i - 1] for n in range(6)]
            d = j + EDGE
            held = main_b[0, j] * q[0] + main_b[1, j] * q[1] + main_b[2, j] * q[2]
            mixed = shear_b[0, d] * q[3] + shear_b[1, d] * q[4] + shear_b[2, d] * q[5]
            rest = partial + ahead - 2.0 * gathered[j]
            total = held + 2.0 * mixed + root_b[d + 1] * rest
            total = total * factor_b[j]
            for t in range(fold_b):
                result_n[j, pl.ds(t, SUB, stride=fold_b), :] = total[t]
        if i >= 1:
            partial = here + trail
        trail = behind
    sensitivity_ref[...] = result_n[:, HALO : HALO + band, :]
    leaving.wait()


def on_vmem():
    return pl.BlockSpec(memory_space=pltpu.VMEM)


def on_smem():
    return pl.BlockSpec(memory_space=pltpu.SMEM)


def solids(density, void_depth):
    cells, band, depth = density.shape
    return pl.pallas_call(
        solid_kernel,
        out_shape=[
            pltpu.VMEM((planes, band, depth), jnp.float32) for planes in (cells, HALO, HALO)
        ],
        in_specs=[pl.BlockSpec(memory_space=pltpu.HBM)] * 2,
        out_specs=[on_vmem()] * 3,
        scratch_shapes=[
            pltpu.VMEM(density.shape, jnp.float32),
            pltpu.VMEM(void_depth.shape, jnp.int32),
            pltpu.SemaphoreType.DMA((2,)),
        ],
    )(*(pltpu.with_memory_space_constraint(array, pltpu.HBM) for array in (density, void_depth)))


def settings(band, depth, supports, load_x, load_y, load_vectors):
    vectors = load_vectors.transpose(1, 0, 2)
    return pl.pallas_call(
        settings_kernel,
        out_shape=pltpu.VMEM((1, band, depth), jnp.float32),
        in_specs=[pl.BlockSpec(memory_space=pltpu.HBM)] * 2 + [on_smem()] * 2,
        out_specs=on_vmem(),
        scratch_shapes=[
            pltpu.SMEM(supports.shape, jnp.int32),
            pltpu.SMEM(vectors.shape, jnp.float32),
            pltpu.SemaphoreType.DMA((2,)),
        ],
    )(
        *(pltpu.with_memory_space_constraint(array, pltpu.HBM) for array in (supports, vectors)),
        load_x,
        load_y,
    )


def relaxed(bands):
    groups, planes, band, depth = bands.shape
    wide = planes - 1
    cells = wide - 2 * HALO
    rows = groups * band
    fold = rows // SUB
    fold_b = -(-(band + 2 * HALO) // SUB)
    tall = PAD + rows + fold_b * SUB
    abreast = ABREAST if (groups - 1) % ABREAST == 0 else 1

    def area(*lead):
        return pltpu.VMEM((*lead, fold, SUB, depth), jnp.float32)

    def window(*lead):
        return pltpu.VMEM((*lead, fold_b, SUB, depth), jnp.float32)

    return pl.pallas_call(
        relax_kernel,
        out_shape=(
            jax.ShapeDtypeStruct((3, cells, rows, depth), jnp.float32),
            jax.ShapeDtypeStruct((cells, band, depth), jnp.float32),
        ),
        in_specs=[on_vmem()],
        out_specs=(pl.BlockSpec(memory_space=pltpu.HBM), on_vmem()),
        scratch_shapes=[
            pltpu.VMEM((wide, tall, depth), jnp.float32),
            pltpu.VMEM((3, cells + 2, tall, depth), jnp.float32),
            pltpu.VMEM((cells, fold_b * SUB, depth), jnp.float32),
            area(wide),
            area(wide - 2),
            area(3, wide - 2),
            area(3, wide - 2),
            area(3, wide - 2),
            area(3, wide - 2),
            window(wide),
            window(wide - 2),
            window(abreast, 3, wide - 2),
            window(3, wide - 2),
            window(3, wide - 2),
            window(abreast, 3, wide - 4),
            window(3, cells),
            window(cells),
            window(abreast + 1, 3, cells + 2),
            window(6, cells + 2),
            window(wide - 2 + cells),
            pltpu.VMEM((3, cells, rows, depth), jnp.float32),
            pltpu.SemaphoreType.DMA((1,)),
        ],
        compiler_params=pltpu.CompilerParams(vmem_limit_bytes=32 * 1024 * 1024),
    )(bands)


def shards(density, void_depth, supports, load_x, load_y, load_vectors):
    cells, band, depth = density.shape
    groups = lax.axis_size("case")
    slabs = lax.axis_size("space")
    solid, near, far = solids(density, void_depth)
    across = [(i, i + 1) for i in range(1, slabs - 1, 2)]
    across += [(j, i) for i, j in across]
    inside = [(i, i + 1) for i in range(0, slabs, 2)]
    inside += [(j, i) for i, j in inside]
    first = lax.rem(lax.axis_index("space"), CORES) == 0
    inner = lax.ppermute(near, "space", inside)
    outer = lax.ppermute(far, "space", across)
    row = settings(band, depth, supports, load_x, load_y, load_vectors)
    second = jnp.logical_not(first)
    before = jnp.where(second, inner, outer)
    after = jnp.where(second, outer, inner)
    mine = jnp.concatenate([before, solid, after, row])
    mine = jnp.broadcast_to(mine[None], (groups, *mine.shape))
    bands = lax.all_to_all(mine, "case", split_axis=0, concat_axis=0, tiled=True)
    field, sensitivity = relaxed(bands)
    return (field[None], sensitivity)


def solution(mesh):
    return jax.shard_map(
        shards,
        mesh=mesh,
        in_specs=(
            P("space", "case", None),
            P("space", "case"),
            P("case", None),
            P("case"),
            P("case"),
            P("case", None, None),
        ),
        out_specs=(P("case", None, "space", None, None), P("space", "case", None)),
        check_vma=False,
    )
```

```python
import math

import jax
import jax.numpy as jnp
from jax import lax
from jax.experimental import pallas as pl
from jax.experimental.pallas import tpu as pltpu
from jax.sharding import PartitionSpec as P

SWEEPS = 3
LOADW = 8
EMIN = 0.001
LOWER = 0.06
UPPER = 3.0
PATCH = 4.0
SUB = 8
CORES = 2
ABREAST = 3
HALO = SWEEPS + 1
EDGE = HALO - 1
PAD = 8

AXIAL = 1.5
PAIR = 0.625
FLAT = 0.5
FULL = 0.25 * (1.0 + 0.5 / 3.0)
CROSS2 = 0.125
CROSS3 = 0.125 / 3.0


def relaxations(count):
    middle = 0.5 * (UPPER + LOWER)
    radius = 0.5 * (UPPER - LOWER)
    return [
        1.0 / (middle + radius * math.cos(math.pi * (2 * index + 1) / (2 * count)))
        for index in range(count)
    ]


def both(pair):
    return pair[0] + pair[1], pair[0] - pair[1]


def plus(pair):
    return pair[0] + pair[1]


def minus(pair):
    return pair[0] - pair[1]


def span_of(cells):
    return cells + 2 * EDGE


def solid_kernel(
    density_in, void_in, solid_ref, inner_ref, outer_ref, density_ref, void_ref, arrived
):
    fetches = [
        pltpu.make_async_copy(void_in, void_ref, arrived.at[0]),
        pltpu.make_async_copy(density_in, density_ref, arrived.at[1]),
    ]
    for fetch in fetches:
        fetch.start()
    cells, band, depth = solid_ref.shape
    first = lax.rem(lax.axis_index("space"), CORES) == 0
    level = lax.broadcasted_iota(jnp.int32, (band, depth), 1) - depth // 2
    eye = lax.broadcasted_iota(jnp.int32, (band, band), 0) == lax.broadcasted_iota(
        jnp.int32, (band, band), 1
    )
    for fetch in fetches:
        fetch.wait()
    for i in range(cells):
        line = jnp.broadcast_to(void_ref[i : i + 1, :], (band, band)).astype(jnp.float32)
        column = jnp.sum(jnp.where(eye, line, 0.0), axis=1, keepdims=True)
        top = jnp.broadcast_to(column, (band, depth)).astype(jnp.int32)
        hollow = (level >= 0) & (level < top)
        solid_ref[i] = jnp.where(hollow, 0.0, density_ref[i])
    for i in range(HALO):
        low = solid_ref[i]
        high = solid_ref[cells - HALO + i]
        outer_ref[i] = jnp.where(first, low, high)
        inner_ref[i] = jnp.where(first, high, low)


def settings_kernel(
    supports_in, vectors_in, load_x_ref, load_y_ref, row_ref, supports_ref, vectors_ref, arrived
):
    fetches = [
        pltpu.make_async_copy(supports_in, supports_ref, arrived.at[0]),
        pltpu.make_async_copy(vectors_in, vectors_ref, arrived.at[1]),
    ]
    for fetch in fetches:
        fetch.start()
    for fetch in fetches:
        fetch.wait()
    slabs = lax.axis_size("space")
    band, depth = row_ref.shape[1:]
    total_x = vectors_ref.shape[2]
    cells = total_x // slabs
    span = span_of(cells)
    first = lax.axis_index("space") * cells - EDGE
    lane = lax.broadcasted_iota(jnp.int32, (1, depth), 1)
    row = jnp.where(lane == 5 * span, load_y_ref[0].astype(jnp.float32), 0.0)
    for m in range(span):
        place = first + m
        inside = jnp.logical_and(place >= 0, place < total_x)
        where = jnp.clip(place, 0, total_x - 1)
        for k in range(3):
            value = jnp.where(inside, vectors_ref[k, 0, where], 0.0)
            row = jnp.where(lane == k * span + m, value, row)
    place = first + lane - 3 * span
    pinned = (place < supports_ref[0, 0]) | (place >= total_x - supports_ref[0, 1])
    row = jnp.where((lane >= 3 * span) & (lane < 4 * span) & pinned, 1.0, row)
    place = first + lane - 4 * span
    loaded = (place >= load_x_ref[0]) & (place < load_x_ref[0] + LOADW)
    row = jnp.where((lane >= 4 * span) & (lane < 5 * span) & loaded, 1.0, row)
    row_ref[0] = jnp.broadcast_to(row, (band, depth))


def relax_kernel(
    bands_ref,
    field_ref,
    sensitivity_ref,
    natural,
    third_n,
    result_n,
    root_a,
    drive_a,
    push_a,
    inverse_a,
    shear_a,
    first_a,
    root_b,
    drive_b,
    push_b,
    inverse_b,
    shear_b,
    first_b,
    main_b,
    factor_b,
    second_b,
    squares_b,
    work_b,
    field_v,
    gone,
):
    groups, planes, band, depth = bands_ref.shape
    wide = planes - 1
    cells = wide - 2 * HALO
    span = span_of(cells)
    rows = groups * band
    case = lax.axis_index("case")
    total_x = lax.axis_size("space") * cells
    first_plane = lax.axis_index("space") * cells
    omegas = relaxations(SWEEPS)
    scale = omegas[0] * omegas[1] * omegas[2]

    blank = jnp.zeros((PAD, depth), jnp.float32)
    for i in range(wide):
        natural[i, 0:PAD, :] = blank
        for at in range(PAD + rows, natural.shape[1], PAD):
            natural[i, at : at + PAD, :] = blank
    for k in range(3):
        for i in range(cells + 2):
            third_n[k, i, 0:PAD, :] = blank
            for at in range(PAD + rows, natural.shape[1], PAD):
                third_n[k, i, at : at + PAD, :] = blank
    for g in range(groups):
        natural[:, PAD + g * band : PAD + (g + 1) * band, :] = bands_ref[g, 0:wide]

    tile = (1, SUB, depth)
    lane = lax.broadcasted_iota(jnp.int32, tile, 2)
    line = lax.broadcasted_iota(jnp.int32, tile, 1)
    not_first_z = (lane > 0).astype(jnp.float32)
    not_last_z = (lane < depth - 1).astype(jnp.float32)
    not_first_s = (line > 0).astype(jnp.float32)
    not_last_s = (line < SUB - 1).astype(jnp.float32)
    at_bottom = (lane == 0).astype(jnp.float32)
    half_first_z = 0.5 * not_first_z
    half_last_z = 0.5 * not_last_z

    def along_z(a):
        after = pltpu.roll(a, depth - 1, 2) * not_last_z
        before = pltpu.roll(a, 1, 2) * not_first_z
        return after, before

    def along_y(a, closed):
        fold = a.shape[0]
        after = pltpu.roll(a[0:1], SUB - 1, 1)
        before = pltpu.roll(a[fold - 1 : fold], 1, 1)
        if closed:
            after = after * not_last_s
            before = before * not_first_s
        return (
            jnp.concatenate([a[1:], after], axis=0),
            jnp.concatenate([before, a[:-1]], axis=0),
        )

    def inside_of(plane, margin):
        place = first_plane - margin + plane
        return jnp.logical_and(place >= 0, place < total_x).astype(jnp.float32)

    def lines_of(fold):
        shape = (fold, SUB, depth)
        return fold * lax.broadcasted_iota(jnp.int32, shape, 1) + lax.broadcasted_iota(
            jnp.int32, shape, 0
        )

    def case_values(which):
        plain = jnp.broadcast_to(bands_ref[which, wide, 0:1, :], (SUB, depth))

        def value(kind, j):
            at = kind * span + j
            return jnp.broadcast_to(plain[:, at : at + 1], (SUB, depth))[None]

        corner = jnp.broadcast_to(plain[:, 5 * span : 5 * span + 1], (SUB, depth))[None]
        return value, corner

    def patch_of(y_of, corner):
        y = y_of.astype(jnp.float32)
        high = lax.broadcasted_iota(jnp.int32, y_of.shape, 2) == depth - 1
        return jnp.where(high & (y >= corner) & (y < corner + LOADW), PATCH, 0.0)

    def stiffness(fold, start, keep_rows, root_s, drive_s, inv_s, factor_s):
        for i in range(wide):
            solid = jnp.stack(
                [natural[i, pl.ds(start + t, SUB, stride=fold), :] for t in range(fold)]
            )
            stiff = EMIN + (1.0 - EMIN) * (solid * solid * solid)
            inv_root = lax.rsqrt(stiff)
            root = stiff * inv_root * inside_of(i, HALO)
            root_s[i] = root if keep_rows is None else root * keep_rows
            if 0 < i < wide - 1:
                drive_s[i - 1] = solid * inv_root
                inv_s[i - 1] = inv_root
            if factor_s is not None and HALO <= i < HALO + cells:
                ratio = solid * inv_root
                factor_s[i - HALO] = ((-1.5 * (1.0 - EMIN)) * scale * scale / groups) * (ratio * ratio)

    def tensor_parts(r, closed):
        zs, zd = both(along_z(r))
        ys, yd = both(along_y(r, closed))
        yszs, ydzs = both(along_y(zs, closed))
        yszd, ydzd = both(along_y(zd, closed))
        cross = ys + zs
        corner = PAIR * yszs
        here = [
            cross + FLAT * yszs,
            cross + 0.5 * ys + corner,
            cross + 0.5 * zs + corner,
            CROSS2 * ydzd,
        ]
        base = FULL * yszs + 0.5 * cross + r
        even = [
            base + 0.5 * r + 0.125 * cross,
            base + 0.125 * ys,
            base + 0.125 * zs,
            CROSS3 * ydzd,
        ]
        odd = [CROSS2 * yd + CROSS3 * ydzs, CROSS2 * zd + CROSS3 * yszd]
        return here, even, odd

    def tensor(closed, keep_rows, root_s, shear_s, inverse_s, main_s):
        older = None
        newer = None
        for i in range(wide):
            latest = tensor_parts(root_s[i], closed)
            if i >= 2:
                j = i - 2
                keep = inside_of(j, EDGE)
                if keep_rows is not None:
                    keep = keep * keep_rows
                total = [newer[0][k] + (latest[1][k] + older[1][k]) for k in range(4)]
                shear_s[0, j] = latest[2][0] - older[2][0]
                shear_s[1, j] = latest[2][1] - older[2][1]
                shear_s[2, j] = total[3]
                for k in range(3):
                    if main_s is not None and EDGE <= j < EDGE + cells:
                        main_s[k, j - EDGE] = total[k]
                    inverse_s[k, j] = keep / (total[k] + (1.0 - keep))
            older, newer = newer, latest

    def pushes(which, y_of, drive_s, inv_s, inverse_s, push_s):
        value, corner = case_values(which)
        patch = patch_of(y_of, corner)
        for j in range(wide - 2):
            free = 1.0 - value(3, j) * at_bottom
            push = (drive_s[j] + (value(4, j) * patch) * inv_s[j]) * free
            for k in range(3):
                push_s[k, j] = push * inverse_s[k, j] * value(k, j)
        return value

    def field_parts(w):
        zs, zd = [], []
        for k in range(3):
            after = pltpu.roll(w[k], depth - 1, 2) * half_last_z
            before = pltpu.roll(w[k], 1, 2) * half_first_z
            zs.append(after + before)
            zd.append(after - before)
        mean = [w[k] + zs[k] for k in range(2)]
        mixed = [CROSS2 * w[k] + (2.0 * CROSS3) * zs[k] for k in range(2)]
        lift = [0.5 * mean[k] + mixed[k] for k in range(2)]
        strong = [(2.0 * PAIR) * mean[k] + (AXIAL - 2.0 * PAIR) * w[k] for k in range(2)]
        upright = w[2] + (2.0 * PAIR) * zs[2]
        flat = FLAT * w[2] + (2.0 * FULL) * zs[2]
        edge = [(2.0 * CROSS2) * zd[k] for k in range(3)]
        tip = [(2.0 * CROSS3) * zd[k] for k in range(3)]
        here = [
            (zs[0] + zs[0], mean[0], None),
            (zs[1] + zs[1], strong[1], edge[2]),
            ((2.0 * AXIAL) * zs[2], upright, edge[1]),
        ]
        ahead = [
            (strong[0] + edge[2], lift[0] + tip[2], mixed[1]),
            (mean[1], lift[1], tip[2] + mixed[0]),
            (upright + edge[0], flat + tip[0], tip[1]),
        ]
        behind = [
            (strong[0] - edge[2], lift[0] - tip[2], -mixed[1]),
            (mean[1], lift[1], tip[2] - mixed[0]),
            (upright - edge[0], flat - tip[0], tip[1]),
        ]
        return tuple([term for row in part for term in row] for part in (here, ahead, behind))

    def field_sums(terms, closed):
        sums = []
        for k in range(3):
            stays, even, odd = terms[3 * k : 3 * k + 3]
            after = along_y(even + odd, closed)[0]
            before = along_y(even - odd, closed)[1]
            sums.append(stays + after + before)
        return sums

    def joined(left, right):
        return [b if a is None else a + b for a, b in zip(left, right)]

    def sweep(
        closed, count, load, keep, drive, value, store, root_s, push_s, inverse_s, shear_s
    ):
        offset = (wide - count) // 2
        partial = None
        trail = None
        free = None
        for i in range(count):
            held = free
            r = root_s[i + offset]
            if drive is not None:
                free = 1.0 - value(3, i + offset - 1) * at_bottom
                r = r * free
            here, ahead, behind = field_parts([r * load(k, i) for k in range(3)])
            if i >= 2:
                j = i - 1
                d = j + offset - 1
                old = [load(k, j) for k in range(3)]
                shear = [shear_s[k, d] for k in range(3)]
                rest = [
                    shear[0] * old[1] + shear[1] * old[2],
                    shear[0] * old[0] + shear[2] * old[2],
                    shear[1] * old[0] + shear[2] * old[1],
                ]
                total = field_sums(joined(partial, ahead), closed)
                for k in range(3):
                    new = keep * old[k] + (total[k] - rest[k]) * inverse_s[k, d]
                    if drive is not None:
                        new = (new + drive * push_s[k, d]) * held
                    store(k, j - 1, new)
            if i >= 1:
                partial = joined(here, trail)
            trail = behind
            yield

    def together(sweeps):
        for _ in zip(*sweeps):
            pass

    keep_second = (1.0 - omegas[1]) / omegas[1] + 1.0 / omegas[0]
    keep_third = (1.0 - omegas[2]) / omegas[2]
    drive_third = 1.0 / (omegas[0] * omegas[1])

    fold = rows // SUB
    inv_a = first_a.at[0]
    stiffness(fold, PAD, None, root_a, drive_a, inv_a, None)
    tensor(True, None, root_a, shear_a, inverse_a, None)
    value = pushes(case, lines_of(fold), drive_a, inv_a, inverse_a, push_a)

    def store_first_a(k, i, new):
        first_a[k, i] = new

    def store_third_a(k, i, new):
        for t in range(fold):
            third_n[k, i, pl.ds(PAD + t, SUB, stride=fold), :] = new[t]
            if 1 <= i <= cells:
                field_v[k, i - 1, pl.ds(t, SUB, stride=fold), :] = scale * new[t]

    arrays = (root_a, push_a, inverse_a, shear_a)
    first_sweep = sweep(
        True,
        wide - 2,
        lambda k, i: push_a[k, i],
        keep_second,
        None,
        value,
        store_first_a,
        *arrays,
    )
    second_sweep = sweep(
        True,
        wide - 4,
        lambda k, i: first_a[k, i],
        keep_third,
        drive_third,
        value,
        store_third_a,
        *arrays,
    )
    together([first_sweep])
    together([second_sweep])
    leaving = pltpu.make_async_copy(field_v, field_ref, gone.at[0])
    leaving.start()

    fold_b = result_n.shape[1] // SUB
    top = case * band - HALO
    y_of = top + lines_of(fold_b)
    keep_rows = ((y_of >= 0) & (y_of < rows)).astype(jnp.float32)
    inv_b = work_b.at[pl.ds(0, wide - 2)]
    stiffness(fold_b, PAD + top, keep_rows, root_b, drive_b, inv_b, factor_b)
    tensor(False, keep_rows, root_b, shear_b, inverse_b, main_b)
    gathered = work_b.at[pl.ds(wide - 2, cells)]
    products = ((0, 0), (1, 1), (2, 2), (0, 1), (0, 2), (1, 2))

    def sweeps_other(which, slot):
        push_s = push_b.at[slot]
        first_s = first_b.at[slot]
        value = pushes(which, y_of, drive_b, inv_b, inverse_b, push_s)

        def store_first(k, i, new):
            first_s[k, i] = new

        def store_second(k, i, new):
            second_b[slot, k, i] = new

        arrays = (root_b, push_s, inverse_b, shear_b)
        first_sweep = sweep(
            False,
            wide - 2,
            lambda k, i: push_s[k, i],
            keep_second,
            None,
            value,
            store_first,
            *arrays,
        )
        second_sweep = sweep(
            False,
            wide - 4,
            lambda k, i: first_s[k, i],
            keep_third,
            drive_third,
            value,
            store_second,
            *arrays,
        )
        return first_sweep, second_sweep

    def add_energies(places, fresh):
        for i in range(cells + 2):
            sums = [None] * len(products)
            for slot in places:
                v = [second_b[slot, k, i] for k in range(3)]
                sums = joined(sums, [v[a] * v[b] for a, b in products])
            r = root_b[i + EDGE]
            for n, total in enumerate(sums):
                if fresh:
                    squares_b[n, i] = r * total
                else:
                    squares_b[n, i] += r * total
        partial = [None] * len(places)
        trail = [None] * len(places)
        for i in range(cells + 2):
            r = root_b[i + EDGE]
            dots = [None]
            for n, slot in enumerate(places):
                here, ahead, behind = field_parts([r * second_b[slot, k, i] for k in range(3)])
                if i >= 2:
                    total = field_sums(joined(partial[n], ahead), False)
                    dot = [second_b[slot, k, i - 1] * total[k] for k in range(3)]
                    dots = joined(dots, [dot[0] + dot[1] + dot[2]])
                if i >= 1:
                    partial[n] = joined(here, trail[n])
                trail[n] = behind
            if i >= 2:
                if fresh:
                    gathered[i - 2] = dots[0]
                else:
                    gathered[i - 2] += dots[0]

    abreast = second_b.shape[0] - 1
    for k in range(3):
        for i in range(cells + 2):
            second_b[abreast, k, i] = jnp.stack(
                [third_n[k, i, pl.ds(PAD + top + t, SUB, stride=fold_b), :] for t in range(fold_b)]
            )
    def relax_others(start):
        pairs = [
            sweeps_other(lax.rem(case + start + slot, groups), slot) for slot in range(abreast)
        ]
        for sweeps in zip(*pairs):
            together(sweeps)

    if groups - 1 == abreast:
        relax_others(1)
        add_energies(range(groups), True)
    else:
        add_energies([abreast], True)

        @pl.loop(1, groups, step=abreast)
        def add_others(start):
            relax_others(start)
            add_energies(range(abreast), False)

    def square_parts(q):
        qxx, qyy, qzz, qxy, qxz, qyz = q
        s = qxx + qyy + qzz
        zs_s = plus(along_z(s))
        zs_x = plus(along_z(qxx))
        zs_z = plus(along_z(qzz))
        zs_xy = plus(along_z(qxy))
        zd_yz = minus(along_z(qyz))
        zd_xz = minus(along_z(qxz))
        twist = minus(along_y(zd_yz, False))
        half = 0.5 * zs_s + 0.125 * zs_z
        here = (
            zs_s
            + 0.5 * zs_z
            + plus(along_y(s + 0.5 * qyy + (PAIR * zs_s - 0.125 * zs_x), False))
            + 0.25 * twist
        )
        even = (
            s
            + 0.5 * qxx
            + half
            + 0.125 * zs_x
            + plus(along_y(0.5 * s + 0.125 * (qxx + qyy) + FULL * zs_s, False))
            + (1.0 / 12.0) * twist
        )
        odd = (
            minus(along_y(0.25 * qxy + (1.0 / 12.0) * zs_xy, False))
            + 0.25 * zd_xz
            + plus(along_y((1.0 / 12.0) * zd_xz, False))
        )
        return here, even + odd, even - odd

    partial = None
    trail = None
    for i in range(cells + 2):
        here, ahead, behind = square_parts([squares_b[n, i] for n in range(6)])
        if i >= 2:
            j = i - 2
            q = [squares_b[n, i - 1] for n in range(6)]
            d = j + EDGE
            held = main_b[0, j] * q[0] + main_b[1, j] * q[1] + main_b[2, j] * q[2]
            mixed = shear_b[0, d] * q[3] + shear_b[1, d] * q[4] + shear_b[2, d] * q[5]
            rest = partial + ahead - 2.0 * gathered[j]
            total = held + 2.0 * mixed + root_b[d + 1] * rest
            total = total * factor_b[j]
            for t in range(fold_b):
                result_n[j, pl.ds(t, SUB, stride=fold_b), :] = total[t]
        if i >= 1:
            partial = here + trail
        trail = behind
    sensitivity_ref[...] = result_n[:, HALO : HALO + band, :]
    leaving.wait()


def on_vmem():
    return pl.BlockSpec(memory_space=pltpu.VMEM)


def on_smem():
    return pl.BlockSpec(memory_space=pltpu.SMEM)


def solids(density, void_depth):
    cells, band, depth = density.shape
    return pl.pallas_call(
        solid_kernel,
        out_shape=[
            pltpu.VMEM((planes, band, depth), jnp.float32) for planes in (cells, HALO, HALO)
        ],
        in_specs=[pl.BlockSpec(memory_space=pltpu.HBM)] * 2,
        out_specs=[on_vmem()] * 3,
        scratch_shapes=[
            pltpu.VMEM(density.shape, jnp.float32),
            pltpu.VMEM(void_depth.shape, jnp.int32),
            pltpu.SemaphoreType.DMA((2,)),
        ],
    )(*(pltpu.with_memory_space_constraint(array, pltpu.HBM) for array in (density, void_depth)))


def settings(band, depth, supports, load_x, load_y, load_vectors):
    vectors = load_vectors.transpose(1, 0, 2)
    return pl.pallas_call(
        settings_kernel,
        out_shape=pltpu.VMEM((1, band, depth), jnp.float32),
        in_specs=[pl.BlockSpec(memory_space=pltpu.HBM)] * 2 + [on_smem()] * 2,
        out_specs=on_vmem(),
        scratch_shapes=[
            pltpu.SMEM(supports.shape, jnp.int32),
            pltpu.SMEM(vectors.shape, jnp.float32),
            pltpu.SemaphoreType.DMA((2,)),
        ],
    )(
        *(pltpu.with_memory_space_constraint(array, pltpu.HBM) for array in (supports, vectors)),
        load_x,
        load_y,
    )


def relaxed(bands):
    groups, planes, band, depth = bands.shape
    wide = planes - 1
    cells = wide - 2 * HALO
    rows = groups * band
    fold = rows // SUB
    fold_b = -(-(band + 2 * HALO) // SUB)
    tall = PAD + rows + fold_b * SUB
    abreast = ABREAST if (groups - 1) % ABREAST == 0 else 1

    def area(*lead):
        return pltpu.VMEM((*lead, fold, SUB, depth), jnp.float32)

    def window(*lead):
        return pltpu.VMEM((*lead, fold_b, SUB, depth), jnp.float32)

    return pl.pallas_call(
        relax_kernel,
        out_shape=(
            jax.ShapeDtypeStruct((3, cells, rows, depth), jnp.float32),
            jax.ShapeDtypeStruct((cells, band, depth), jnp.float32),
        ),
        in_specs=[on_vmem()],
        out_specs=(pl.BlockSpec(memory_space=pltpu.HBM), on_vmem()),
        scratch_shapes=[
            pltpu.VMEM((wide, tall, depth), jnp.float32),
            pltpu.VMEM((3, cells + 2, tall, depth), jnp.float32),
            pltpu.VMEM((cells, fold_b * SUB, depth), jnp.float32),
            area(wide),
            area(wide - 2),
            area(3, wide - 2),
            area(3, wide - 2),
            area(3, wide - 2),
            area(3, wide - 2),
            window(wide),
            window(wide - 2),
            window(abreast, 3, wide - 2),
            window(3, wide - 2),
            window(3, wide - 2),
            window(abreast, 3, wide - 4),
            window(3, cells),
            window(cells),
            window(abreast + 1, 3, cells + 2),
            window(6, cells + 2),
            window(wide - 2 + cells),
            pltpu.VMEM((3, cells, rows, depth), jnp.float32),
            pltpu.SemaphoreType.DMA((1,)),
        ],
        compiler_params=pltpu.CompilerParams(vmem_limit_bytes=32 * 1024 * 1024),
    )(bands)


def shards(density, void_depth, supports, load_x, load_y, load_vectors):
    cells, band, depth = density.shape
    groups = lax.axis_size("case")
    slabs = lax.axis_size("space")
    solid, near, far = solids(density, void_depth)
    across = [(i, i + 1) for i in range(1, slabs - 1, 2)]
    across += [(j, i) for i, j in across]
    inside = [(i, i + 1) for i in range(0, slabs, 2)]
    inside += [(j, i) for i, j in inside]
    first = lax.rem(lax.axis_index("space"), CORES) == 0
    inner = lax.ppermute(near, "space", inside)
    outer = lax.ppermute(far, "space", across)
    row = settings(band, depth, supports, load_x, load_y, load_vectors)
    second = jnp.logical_not(first)
    before = jnp.where(second, inner, outer)
    after = jnp.where(second, outer, inner)
    mine = jnp.concatenate([before, solid, after, row])
    mine = jnp.broadcast_to(mine[None], (groups, *mine.shape))
    bands = lax.all_to_all(mine, "case", split_axis=0, concat_axis=0, tiled=True)
    field, sensitivity = relaxed(bands)
    return (field[None], sensitivity)


def solution(mesh):
    return jax.shard_map(
        shards,
        mesh=mesh,
        in_specs=(
            P("space", "case", None),
            P("space", "case"),
            P("case", None),
            P("case"),
            P("case"),
            P("case", None, None),
        ),
        out_specs=(P("case", None, "space", None, None), P("space", "case", None)),
        check_vma=False,
    )
```
